32 devices in a mesh: dp: 4 (over y, core), fsdp: 8 (over z, x).
Axes of the slice: x: 2, y: 2, z: 4, core: 2. Of those that a mesh axis runs over, the one named last changes fastest.
Arguments:
- tokens: bfloat16 [16384, 1024], P(('dp', 'fsdp')), may hold values from -6 to 6
- cotangent: bfloat16 [16384, 1024], P(('dp', 'fsdp'))
- page_lengths: int32 [2, 32], P(None, ('dp', 'fsdp')), may hold values from 0 to 512, as said below
- layout_pos: int32 [2, 16384], P(None, ('dp', 'fsdp')), may hold values from 0 to 63
- attn_master: float32 [4, 1024, 1024], P(None, ('dp', 'fsdp'))
- attn_first: float32 [4, 1024, 1024], P(None, ('dp', 'fsdp'))
- attn_second: float32 [4, 1024, 1024], P(None, ('dp', 'fsdp')), as said below
- ffin_master: float32 [2, 1024, 2816], P(None, ('dp', 'fsdp')), may hold values from -0.1875 to 0.1875
- ffin_first: float32 [2, 1024, 2816], P(None, ('dp', 'fsdp'))
- ffin_second: float32 [2, 1024, 2816], P(None, ('dp', 'fsdp')), as said below
- down_master: float32 [1024, 2816], P(('dp', 'fsdp')), may hold values from -0.109375 to 0.109375
- down_first: float32 [1024, 2816], P(('dp', 'fsdp'))
- down_second: float32 [1024, 2816], P(('dp', 'fsdp')), as said below
- small_master: float32 [3584], P(('dp', 'fsdp'))
- small_first: float32 [3584], P(('dp', 'fsdp'))
- small_second: float32 [3584], P(('dp', 'fsdp')), as said below
Outputs:
- block_out: bfloat16 [16384, 1024], P(('dp', 'fsdp'))
- grad_tokens: float32 [16384, 1024], P(('dp', 'fsdp'))
- grad_norm: float32 [], replicated
- attn_master_new: float32 [4, 1024, 1024], P(None, ('dp', 'fsdp'))
- attn_first_new: float32 [4, 1024, 1024], P(None, ('dp', 'fsdp'))
- attn_second_new: float32 [3, 1024, 1024], P(None, ('dp', 'fsdp'))
- query_second_new: float32 [1024, 1024], P(('dp', 'fsdp'))
- ffin_master_new: float32 [2, 1024, 2816], P(None, ('dp', 'fsdp'))
- ffin_first_new: float32 [2, 1024, 2816], P(None, ('dp', 'fsdp'))
- ffin_second_new: float32 [2, 1024, 2816], P(None, ('dp', 'fsdp'))
- down_master_new: float32 [1024, 2816], P(('dp', 'fsdp'))
- down_first_new: float32 [1024, 2816], P(('dp', 'fsdp'))
- down_second_new: float32 [1024, 2816], P(('dp', 'fsdp'))
- small_master_new: float32 [3584], P(('dp', 'fsdp'))
- small_first_new: float32 [3584], P(('dp', 'fsdp'))
- small_second_new: float32 [3584], P(('dp', 'fsdp'))
The draws below stay inside these ranges and needn't reach their ends.
Inputs may be any that keep to these rules, and one draw needn't show every extreme that they name: `page_lengths`: row 0 holds the length of a device's first page, 246 to 512 tokens; row 1 that of a second page packed right after it, or 0; a device's pages together hold at most 512 tokens, and some device holds a single page of 512 tokens. `attn_second`: Positive. `ffin_second`: Positive. `down_second`: Positive. `small_second`: Positive.
All inputs are finite; a program needn't handle non-finite values.
Results may differ from the reference program's by a relative error of at most 0.012.
The reference program's roundings to bfloat16 on the way count: a program that leaves them out, or rounds other values in their place, can miss the bound.
Values may be sent and summed in bfloat16 or wider, within the bound.
A program may use at most 256 MiB of HBM per device.

```python
import math
from functools import partial
import jax
import jax.numpy as jnp
import numpy as np
from jax import lax

D = 1024
HEADS = 16
HEAD_DIM = 64
FF = 2816
BUCKETS = 32
LAYOUT_POS = 64
TOK_DEV = 512
STEP = 10
TOKENS = 16384
PAGE_MIN = 246
PAGE_MAX = 512
SMALL = 3584
DP_SPAN = 256


def rising_profile(steep):
    index_all = jnp.arange(D)
    coarse_pos = index_all // DP_SPAN / max(D // DP_SPAN - 1, 1)
    fine_pos = index_all % DP_SPAN / max(DP_SPAN - 1, 1)
    return jnp.sqrt((1.0 + steep * coarse_pos) * (1.0 + steep * fine_pos)) / (1.0 + 0.5 * steep)


def moment_scale(weight):
    total_sq = 94.6 * D * D + 1.14 * D * FF + 3.7 * D + 4.3 * BUCKETS * HEADS
    return weight / total_sq ** 0.5


def signed_moment_draw(key, shape, scale):
    return scale * jax.random.normal(key, shape, jnp.float32)


def positive_moment_draw(key, shape, scale):
    factor = jnp.exp(jax.random.uniform(key, shape, jnp.float32, minval=math.log(0.5), maxval=math.log(8.0)))
    return scale * scale * factor


def small_scales():
    pieces = [jnp.full((D,), 1.6), jnp.full((D,), 1.05), jnp.full((3 * BUCKETS * HEADS,), 1.2)]
    return moment_scale(jnp.concatenate(pieces))


def attn_scales():
    return moment_scale(jnp.array([9.6, 1.2, 0.85, 0.65]))[:, None, None]


def draw_cotangent(key, part):
    key = jax.random.fold_in(key, 11)
    profile = rising_profile(2.0)
    noise = jax.random.normal(key, (TOKENS, D), jnp.float32)
    return (noise * profile[None, :]).astype(jnp.bfloat16)


def draw_page_lengths(key, part):
    key = jax.random.fold_in(key, 12)
    devices = TOKENS // TOK_DEV
    subkeys = jax.random.split(key, 5)
    pair_fits = TOK_DEV >= 2 * PAGE_MIN
    paired = (jax.random.randint(subkeys[0], (devices,), 0, 2) == 1) & pair_fits
    single_len = jax.random.randint(subkeys[1], (devices,), PAGE_MIN, PAGE_MAX + 1)
    first_high = max(min(PAGE_MAX, TOK_DEV - PAGE_MIN), PAGE_MIN)
    first_pair = jax.random.randint(subkeys[2], (devices,), PAGE_MIN, first_high + 1)
    second_high = jnp.maximum(jnp.minimum(PAGE_MAX, TOK_DEV - first_pair), PAGE_MIN)
    second_pair = jax.random.randint(subkeys[3], (devices,), PAGE_MIN, second_high + 1)
    forced = jax.random.randint(subkeys[4], (), 0, devices)
    is_forced = jnp.arange(devices) == forced
    first_len = jnp.where(paired, first_pair, single_len)
    second_len = jnp.where(paired, second_pair, 0)
    first_len = jnp.where(is_forced, PAGE_MAX, first_len)
    second_len = jnp.where(is_forced, 0, second_len)
    return jnp.stack([first_len, second_len]).astype(jnp.int32)


def draw_attn_master(key, part):
    key = jax.random.fold_in(key, 13)
    scales = jnp.array([(64.0 * D) ** (-0.5), D ** (-0.5), D ** (-0.5), (D / 4.0) ** (-0.5)])
    return jax.random.normal(key, (4, D, D), jnp.float32) * scales[:, None, None]


def draw_attn_first(key, part):
    key = jax.random.fold_in(key, 14)
    return signed_moment_draw(key, (4, D, D), attn_scales())


def draw_attn_second(key, part):
    key = jax.random.fold_in(key, 15)
    return positive_moment_draw(key, (4, D, D), attn_scales())


def draw_ffin_first(key, part):
    key = jax.random.fold_in(key, 16)
    return signed_moment_draw(key, (2, D, FF), moment_scale(0.5))


def draw_ffin_second(key, part):
    key = jax.random.fold_in(key, 17)
    return positive_moment_draw(key, (2, D, FF), moment_scale(0.5))


def draw_down_first(key, part):
    key = jax.random.fold_in(key, 18)
    return signed_moment_draw(key, (D, FF), moment_scale(0.8))


def draw_down_second(key, part):
    key = jax.random.fold_in(key, 19)
    return positive_moment_draw(key, (D, FF), moment_scale(0.8))


def draw_small_master(key, part):
    key = jax.random.fold_in(key, 20)
    subkeys = jax.random.split(key, 2)
    steep = 2.0
    jitter = 1.0 + 0.1 * jax.random.uniform(subkeys[0], (2, D), jnp.float32, minval=-1.0, maxval=1.0)
    gains = 1.2 * rising_profile(steep)[None, :] * jitter
    tables = 0.5 * jax.random.normal(subkeys[1], (3 * BUCKETS * HEADS,), jnp.float32)
    return jnp.concatenate([gains.reshape(-1), tables])


def draw_small_first(key, part):
    key = jax.random.fold_in(key, 21)
    return signed_moment_draw(key, (SMALL,), small_scales())


def draw_small_second(key, part):
    key = jax.random.fold_in(key, 22)
    return positive_moment_draw(key, (SMALL,), small_scales())


def touch_ends(result, rng, least, top_value):
    longest = result.shape.index(max(result.shape))
    spots = []
    for shift in (0, 1):
        where = [jax.random.randint(jax.random.fold_in(rng, axis), (), 0, length) for axis, length in enumerate(result.shape)]
        where[longest] = (where[longest] + shift) % result.shape[longest]
        spots.append(tuple(where))
    return result.at[spots[0]].set(least).at[spots[1]].set(top_value)


def shard_levels(own_key, shape, shards, smallest, largest):
    def one(dim, parts):
        steps = jax.random.uniform(jax.random.fold_in(jax.random.fold_in(own_key, 6), dim), (parts,), jnp.float32, smallest / len(shards), largest / len(shards))
        return jnp.repeat(jnp.exp(steps), shape[dim] // parts).reshape((-1,) + (1,) * (len(shape) - dim - 1))

    factor_of = one(*shards[0])
    for cut in shards[1:]:
        factor_of = factor_of * one(*cut)
    return factor_of


def gaussian(key, shape, width, limit, cuts=(), held_as=jnp.bfloat16):
    values = width * jax.random.normal(key, shape, jnp.float32)
    if cuts:
        values = values * shard_levels(key, shape, cuts, -0.22, 0.18)
    return jnp.clip(values, -limit, limit).astype(held_as)


def setup_inputs(seed: int = 0) -> dict:
    seeds = jax.random.split(jax.random.key(seed), 17)
    tokens = gaussian(seeds[0], (TOKENS, D), 1.0, 6.0, ((0, 32),))
    cotangent = draw_cotangent(jax.random.fold_in(seeds[16], 71), 0)
    page_lengths = draw_page_lengths(jax.random.fold_in(seeds[16], 71), 0)
    layout_pos = touch_ends(jax.random.randint(seeds[3], (2, TOKENS), 0, LAYOUT_POS), jax.random.fold_in(seeds[3], 1), 0, LAYOUT_POS - 1).astype(jnp.int32)
    attn_master = draw_attn_master(jax.random.fold_in(seeds[16], 71), 0)
    attn_first = draw_attn_first(jax.random.fold_in(seeds[16], 71), 0)
    attn_second = draw_attn_second(jax.random.fold_in(seeds[16], 71), 0)
    ffin_master = gaussian(seeds[7], (2, D, FF), D ** -0.5, 0.1875, ((1, 32),), jnp.float32)
    ffin_first = draw_ffin_first(jax.random.fold_in(seeds[16], 71), 0)
    ffin_second = draw_ffin_second(jax.random.fold_in(seeds[16], 71), 0)
    down_master = gaussian(seeds[10], (D, FF), FF ** -0.5, 0.109375, ((0, 32),), jnp.float32)
    down_first = draw_down_first(jax.random.fold_in(seeds[16], 71), 0)
    down_second = draw_down_second(jax.random.fold_in(seeds[16], 71), 0)
    small_master = draw_small_master(jax.random.fold_in(seeds[16], 71), 0)
    small_first = draw_small_first(jax.random.fold_in(seeds[16], 71), 0)
    small_second = draw_small_second(jax.random.fold_in(seeds[16], 71), 0)
    return dict(tokens=tokens, cotangent=cotangent, page_lengths=page_lengths, layout_pos=layout_pos, attn_master=attn_master, attn_first=attn_first, attn_second=attn_second, ffin_master=ffin_master, ffin_first=ffin_first, ffin_second=ffin_second, down_master=down_master, down_first=down_first, down_second=down_second, small_master=small_master, small_first=small_first, small_second=small_second)


@jax.custom_vjp
def low(v):
    return lax.optimization_barrier(v.astype(jnp.bfloat16)).astype(jnp.float32)

@jax.custom_vjp
def low_back(v):
    return v

def low_keep(v):
    return (low(v), None)

def low_pass(kept, grad):
    return (grad,)

def back_keep(v):
    return (v, None)

def back_low(kept, grad):
    return (low(grad),)
low.defvjp(low_keep, low_pass)
low_back.defvjp(back_keep, back_low)
norm_eps = 1e-06
adam_eps = 1e-08
beta_one = 0.5
beta_two = 0.5
clip_max = 1.0
matrix_rate = 0.02
small_rate = 0.4
decay_rate = 0.01
far_negative = -1e+30
max_distance = 128

def relative_buckets(tok_count, buckets):
    offsets = np.arange(tok_count)[None, :] - np.arange(tok_count)[:, None]
    half_count = buckets // 2
    exact_count = half_count // 2
    distance = np.abs(offsets)
    far_bucket = exact_count + (np.log(np.maximum(distance, 1) / exact_count) / np.log(max_distance / exact_count) * (half_count - exact_count)).astype(np.int64)
    far_bucket = np.minimum(far_bucket, half_count - 1)
    bucket_ids = (offsets > 0).astype(np.int64) * half_count + np.where(distance < exact_count, distance, far_bucket)
    return bucket_ids.astype(np.int32)

def scaled_norm(values, gain):
    return values * lax.rsqrt(lax.optimization_barrier(jnp.mean(values * values, axis=-1, keepdims=True)) + norm_eps) * gain

def gated_gelu(gate_pre, up_pre):
    return jax.nn.gelu(gate_pre, approximate=True) * up_pre

def adamw_update(master, first_state, second_state, gradient, step_rate, weight_decay):
    first_new = beta_one * first_state + (1.0 - beta_one) * gradient
    second_new = beta_two * second_state + (1.0 - beta_two) * gradient * gradient
    first_hat = first_new / (1.0 - beta_one ** STEP)
    second_hat = second_new / (1.0 - beta_two ** STEP)
    master_new = master - step_rate * (first_hat / (jnp.sqrt(second_hat) + adam_eps) + weight_decay * master)
    return (master_new, first_new, second_new)

def attend_block(tables, block):
    query_rows, key_rows, value_rows, page_sizes, pos_horiz, pos_vert = block
    tok_count = query_rows.shape[0]
    tok_index = jnp.arange(tok_count)
    page_ids = jnp.where(tok_index < page_sizes[0], 0, jnp.where(tok_index < page_sizes[0] + page_sizes[1], 1, 2))
    valid_mask = tok_index < page_sizes[0] + page_sizes[1]
    allowed = (page_ids[:, None] == page_ids[None, :]) & valid_mask[None, :]
    half_count = BUCKETS // 2
    rel_idx = jnp.asarray(relative_buckets(tok_count, BUCKETS))
    horiz_idx = jnp.clip(pos_horiz[None, :] - pos_horiz[:, None], -half_count, half_count - 1) + half_count
    vert_idx = jnp.clip(pos_vert[None, :] - pos_vert[:, None], -half_count, half_count - 1) + half_count
    bias_all = tables[0][rel_idx] + tables[1][horiz_idx] + tables[2][vert_idx]
    scores = jnp.einsum('ihe,jhe->hij', query_rows, key_rows, precision=lax.Precision.HIGHEST) + jnp.transpose(bias_all, (2, 0, 1))
    scores = low_back(scores)
    masked = jnp.where(allowed[None], scores, far_negative)
    softmaxed = jax.nn.softmax(masked, axis=-1)
    return jnp.einsum('hij,jhe->ihe', low(softmaxed), value_rows, precision=lax.Precision.HIGHEST)

def forward(stream, w_attn, w_in, w_down, small_all, page_lengths, layout_pos):
    highest = lax.Precision.HIGHEST
    gain_one = small_all[:D]
    gain_two = small_all[D:2 * D]
    tables = small_all[2 * D:].reshape(3, BUCKETS, HEADS)
    normed_one = low(scaled_norm(stream, gain_one))
    queries = low(low_back(jnp.dot(normed_one, w_attn[0], precision=highest)))
    key_rows = low(low_back(jnp.dot(normed_one, w_attn[1], precision=highest)))
    values = low(low_back(jnp.dot(normed_one, w_attn[2], precision=highest)))
    block_count = TOKENS // TOK_DEV
    shape_four = (block_count, TOK_DEV, HEADS, HEAD_DIM)
    blocks = (queries.reshape(shape_four), key_rows.reshape(shape_four), values.reshape(shape_four), page_lengths.T, layout_pos[0].reshape(block_count, TOK_DEV), layout_pos[1].reshape(block_count, TOK_DEV))
    context = lax.map(jax.checkpoint(partial(attend_block, tables)), blocks)
    context = low(low_back(context.reshape(TOKENS, D)))
    attended = low_back(jnp.dot(context, w_attn[3], precision=highest))
    residual = stream + attended
    normed_two = low(scaled_norm(residual, gain_two))
    gate_pre = low_back(jnp.dot(normed_two, w_in[0], precision=highest))
    up_pre = low_back(jnp.dot(normed_two, w_in[1], precision=highest))
    hidden = low(gated_gelu(gate_pre, up_pre))
    mixed = jnp.dot(hidden, w_down.T, precision=highest)
    tok_index = jnp.arange(TOKENS)
    sizes_each = page_lengths[:, tok_index // TOK_DEV]
    valid_rows = (tok_index % TOK_DEV < sizes_each[0] + sizes_each[1]).astype(jnp.float32)
    return valid_rows[:, None] * (residual + mixed)

def reference(tokens, cotangent, page_lengths, layout_pos, attn_master, attn_first, attn_second, ffin_master, ffin_first, ffin_second, down_master, down_first, down_second, small_master, small_first, small_second):
    stream = tokens.astype(jnp.float32)
    attn_round = low(attn_master)
    ffin_round = low(ffin_master)
    down_round = low(down_master)
    small_round = low(small_master)
    layer = partial(forward, page_lengths=page_lengths, layout_pos=layout_pos)
    block_out, pull = jax.vjp(layer, stream, attn_round, ffin_round, down_round, small_round)
    grad_tokens, grad_attn, grad_in, grad_down, grad_small = pull(cotangent.astype(jnp.float32))
    squares = jnp.sum(grad_attn * grad_attn) + jnp.sum(grad_in * grad_in) + jnp.sum(grad_down * grad_down) + jnp.sum(grad_small * grad_small)
    grad_norm = jnp.sqrt(squares)
    clip_scale = clip_max / jnp.maximum(grad_norm, clip_max)
    attn_new = adamw_update(attn_master, attn_first, attn_second, grad_attn * clip_scale, matrix_rate, decay_rate)
    ffin_new = adamw_update(ffin_master, ffin_first, ffin_second, grad_in * clip_scale, matrix_rate, decay_rate)
    down_new = adamw_update(down_master, down_first, down_second, grad_down * clip_scale, matrix_rate, decay_rate)
    small_new = adamw_update(small_master, small_first, small_second, grad_small * clip_scale, small_rate, 0.0)
    return (block_out.astype(jnp.bfloat16), grad_tokens, grad_norm, attn_new[0], attn_new[1], attn_new[2][1:], attn_new[2][0], ffin_new[0], ffin_new[1], ffin_new[2], down_new[0], down_new[1], down_new[2], small_new[0], small_new[1], small_new[2])
```

```python
import functools

import jax
import jax.numpy as jnp
import numpy as np
from jax import lax
from jax.experimental import pallas as pl
from jax.experimental.pallas import tpu as pltpu
from jax.sharding import PartitionSpec as P

HEADS = 16
HEAD_DIM = 64
BUCKETS = 32
LAYOUT_POS = 64
STEP = 10


norm_eps = 1e-06
adam_eps = 1e-08
beta_one = 0.5
beta_two = 0.5
clip_max = 1.0
matrix_rate = 0.02
small_rate = 0.4
decay_rate = 0.01
far_negative = -1e30
max_distance = 128
block_rows = 512


def relative_buckets(tok_count, buckets):
    offsets = np.arange(tok_count)[None, :] - np.arange(tok_count)[:, None]
    half_count = buckets // 2
    exact_count = half_count // 2
    distance = np.abs(offsets)
    far_bucket = exact_count + (
        np.log(np.maximum(distance, 1) / exact_count)
        / np.log(max_distance / exact_count)
        * (half_count - exact_count)
    ).astype(np.int64)
    far_bucket = np.minimum(far_bucket, half_count - 1)
    bucket_ids = (offsets > 0).astype(np.int64) * half_count + np.where(
        distance < exact_count, distance, far_bucket
    )
    return bucket_ids.astype(np.int32)


def layout_table(positions, buckets):
    offsets = np.arange(positions)[None, :] - np.arange(positions)[:, None]
    half_count = buckets // 2
    bucket_ids = np.clip(offsets, -half_count, half_count - 1) + half_count
    return (np.arange(buckets)[:, None] == bucket_ids.reshape(1, -1)).astype(np.float32)


def scaled_norm(values, gain):
    return values * lax.rsqrt(jnp.mean(values * values, axis=-1, keepdims=True) + norm_eps) * gain


def gated_gelu(gate_pre, up_pre):
    return jax.nn.gelu(gate_pre, approximate=True) * up_pre


def adamw_update(master, first_state, second_state, gradient, step_rate, weight_decay):
    first_new = beta_one * first_state + (1.0 - beta_one) * gradient
    second_new = beta_two * second_state + (1.0 - beta_two) * gradient * gradient
    first_hat = first_new / (1.0 - beta_one**STEP)
    second_hat = second_new / (1.0 - beta_two**STEP)
    master_new = master - step_rate * (
        first_hat / (jnp.sqrt(second_hat) + adam_eps) + weight_decay * master
    )
    return (master_new, first_new, second_new)


def on_device(
    tokens,
    cotangent,
    page_lengths,
    layout_pos,
    attn_master,
    attn_first,
    attn_second,
    ffin_master,
    ffin_first,
    ffin_second,
    down_master,
    down_first,
    down_second,
    small_master,
    small_first,
    small_second,
):
    f32 = jnp.float32
    bf16 = jnp.bfloat16
    highest = lax.Precision.HIGHEST
    tok_count, model_width = tokens.shape
    attn_low = attn_master.astype(bf16)
    ffin_low = ffin_master.astype(bf16)
    down_low = down_master.astype(bf16)
    small_low = small_master.astype(bf16)
    w_attn, w_in, w_down, small_all = (
        lax.all_gather(attn_low, ("dp", "fsdp"), axis=1, tiled=True),
        lax.all_gather(ffin_low, ("dp", "fsdp"), axis=1, tiled=True),
        lax.all_gather(down_low, ("dp", "fsdp"), axis=0, tiled=True),
        lax.all_gather(small_low, ("dp", "fsdp"), axis=0, tiled=True),
    )
    gain_one = small_all[:model_width].astype(f32)
    gain_two = small_all[model_width : 2 * model_width].astype(f32)
    tables_t = jnp.transpose(small_all[2 * model_width :].reshape(3, BUCKETS, HEADS), (0, 2, 1))
    layout_hot = jnp.asarray(layout_table(LAYOUT_POS, BUCKETS))
    kernels = jnp.einsum(
        "khn,nm->khm", tables_t[1:], layout_hot.astype(bf16), preferred_element_type=f32
    )
    kernels = kernels.reshape(2, HEADS, LAYOUT_POS, LAYOUT_POS).astype(bf16)
    first_len = page_lengths[0, 0]
    both_len = page_lengths[0, 0] + page_lengths[1, 0]
    tok_index = jnp.arange(tok_count)
    page_ids = jnp.where(tok_index < first_len, 0, jnp.where(tok_index < both_len, 1, 2))
    valid_mask = tok_index < both_len
    valid_rows = valid_mask.astype(f32)[:, None]
    pos_grid = jnp.arange(LAYOUT_POS)
    pos_hot = (layout_pos[:, :, None] == pos_grid[None, None, :]).astype(bf16)
    pos_hot_f32 = pos_hot.astype(f32)
    rel_rows = jnp.asarray(relative_buckets(tok_count, BUCKETS))
    bucket_grid = jnp.arange(BUCKETS)
    rows_per_block = min(tok_count, block_rows)
    block_count = tok_count // rows_per_block
    block_starts = jnp.arange(block_count) * rows_per_block
    stream = tokens.astype(f32)
    normed_one = scaled_norm(stream, gain_one).astype(bf16)
    projected = jnp.einsum(
        "td,kde->kte", normed_one, w_attn[:3], preferred_element_type=f32
    ).astype(bf16)
    shaped = projected.reshape(3, tok_count, HEADS, HEAD_DIM)
    queries = shaped[0]
    key_rows = shaped[1]
    values = shaped[2]

    def block_scores(block_start, query_rows):
        rel_idx = lax.dynamic_slice_in_dim(rel_rows, block_start, rows_per_block, 0)
        rel_hot = (bucket_grid[:, None] == rel_idx.reshape(1, -1)).astype(bf16)
        bias_all = jnp.dot(tables_t[0], rel_hot, preferred_element_type=f32).reshape(
            HEADS, rows_per_block, tok_count
        )
        layout_rows = jnp.einsum(
            "kia,khab->khib", pos_hot, kernels, preferred_element_type=f32
        ).astype(bf16)
        bias_all = bias_all + jnp.einsum(
            "khib,kjb->hij", layout_rows, pos_hot, preferred_element_type=f32
        )
        scores = (
            jnp.einsum("ihe,jhe->hij", query_rows, key_rows, preferred_element_type=f32) + bias_all
        )
        allowed = (page_ids[:, None] == page_ids[None, :]) & valid_mask[None, :]
        masked = jnp.where(allowed[None], scores, far_negative)
        return (masked, allowed, rel_hot, pos_hot)

    def forward_block(running, block_start):
        masked, allowed, rel_hot, query_hot = block_scores(block_start, queries)
        row_max = jnp.max(masked, axis=-1, keepdims=True)
        exponent = jnp.exp(masked - row_max)
        row_total = jnp.sum(exponent, axis=-1, keepdims=True)
        weights_low = (exponent / row_total).astype(bf16)
        block_context = jnp.einsum("hij,jhe->ihe", weights_low, values, preferred_element_type=f32)
        return (running, (block_context, row_max + jnp.log(row_total)))

    unused_carry, (context_blocks, lse_blocks) = lax.scan(
        forward_block, jnp.zeros((), f32), block_starts
    )
    context = context_blocks.reshape(tok_count, model_width).astype(bf16)
    attended = jnp.dot(context, w_attn[3], preferred_element_type=f32)
    residual = stream + attended
    normed_two = scaled_norm(residual, gain_two).astype(bf16)
    gate_up = jnp.einsum("td,kdf->ktf", normed_two, w_in, preferred_element_type=f32)
    hidden = gated_gelu(gate_up[0], gate_up[1]).astype(bf16)
    mixed = jnp.einsum("tf,df->td", hidden, w_down, preferred_element_type=f32)
    block_out = (valid_rows * (residual + mixed)).astype(bf16)
    w_attn, w_in, w_down = (
        lax.all_gather(attn_low, ("dp", "fsdp"), axis=1, tiled=True),
        lax.all_gather(ffin_low, ("dp", "fsdp"), axis=1, tiled=True),
        lax.all_gather(down_low, ("dp", "fsdp"), axis=0, tiled=True),
    )
    grad_out = valid_rows * cotangent.astype(f32)
    grad_out_low = grad_out.astype(bf16)
    grad_down = jnp.einsum("td,tf->df", grad_out_low, hidden, preferred_element_type=f32)
    grad_hidden = jnp.einsum("td,df->tf", grad_out_low, w_down, preferred_element_type=f32)
    unused_gated, gated_pull = jax.vjp(gated_gelu, gate_up[0], gate_up[1])
    grad_gate, grad_up = gated_pull(grad_hidden)
    grad_gate_up = jnp.stack([grad_gate, grad_up]).astype(bf16)
    grad_in = jnp.einsum("td,ktf->kdf", normed_two, grad_gate_up, preferred_element_type=f32)
    grad_normed_two = jnp.einsum("ktf,kdf->td", grad_gate_up, w_in, preferred_element_type=f32)
    unused_second, norm_pull_two = jax.vjp(scaled_norm, residual, gain_two)
    grad_residual_norm, grad_gain_two = norm_pull_two(grad_normed_two)
    grad_residual = grad_out + grad_residual_norm
    grad_attended = grad_residual.astype(bf16)
    grad_out_proj = jnp.einsum("td,te->de", context, grad_attended, preferred_element_type=f32)
    grad_context = jnp.einsum(
        "te,de->td", grad_attended, w_attn[3], preferred_element_type=f32
    ).astype(bf16)
    grad_context = grad_context.reshape(tok_count, HEADS, HEAD_DIM)

    def backward_block(running, block_item):
        grad_key_rows, grad_value_rows, grad_rel, grad_layout = running
        block_start, lse_rows = block_item
        masked, allowed, rel_hot, query_hot = block_scores(block_start, queries)
        probs_f32 = jnp.exp(masked - lse_rows)
        grad_probs = jnp.einsum("ihe,jhe->hij", grad_context, values, preferred_element_type=f32)
        row_dot = jnp.sum(grad_probs * probs_f32, axis=-1, keepdims=True)
        grad_scores = jnp.where(allowed[None], probs_f32 * (grad_probs - row_dot), 0.0).astype(bf16)
        grad_query_rows = jnp.einsum(
            "hij,jhe->ihe", grad_scores, key_rows, preferred_element_type=f32
        )
        grad_key_rows = grad_key_rows + jnp.einsum(
            "hij,ihe->jhe", grad_scores, queries, preferred_element_type=f32
        )
        grad_value_rows = grad_value_rows + jnp.einsum(
            "hij,ihe->jhe", probs_f32.astype(bf16), grad_context, preferred_element_type=f32
        )
        grad_rel = grad_rel + lax.dot_general(
            grad_scores.reshape(HEADS, -1),
            rel_hot,
            (((1,), (1,)), ((), ())),
            preferred_element_type=f32,
        )
        query_sums = jnp.einsum("kia,hij->khaj", query_hot, grad_scores, preferred_element_type=f32)
        grad_layout = grad_layout + jnp.einsum(
            "khaj,kjb->khab", query_sums, pos_hot_f32, precision=highest
        )
        return ((grad_key_rows, grad_value_rows, grad_rel, grad_layout), grad_query_rows)

    start_state = (
        jnp.zeros((tok_count, HEADS, HEAD_DIM), f32),
        jnp.zeros((tok_count, HEADS, HEAD_DIM), f32),
        jnp.zeros((HEADS, BUCKETS), f32),
        jnp.zeros((2, HEADS, LAYOUT_POS, LAYOUT_POS), f32),
    )
    (grad_key_rows, grad_value_rows, grad_rel, grad_layout), grad_query_blocks = lax.scan(
        backward_block, start_state, (block_starts, lse_blocks)
    )
    grad_projected = jnp.stack(
        [
            grad_query_blocks.reshape(tok_count, model_width),
            grad_key_rows.reshape(tok_count, model_width),
            grad_value_rows.reshape(tok_count, model_width),
        ]
    ).astype(bf16)
    grad_qkv = jnp.einsum("td,kte->kde", normed_one, grad_projected, preferred_element_type=f32)
    grad_normed_one = jnp.einsum(
        "kte,kde->td", grad_projected, w_attn[:3], preferred_element_type=f32
    )
    unused_first, norm_pull_one = jax.vjp(scaled_norm, stream, gain_one)
    grad_stream, grad_gain_one = norm_pull_one(grad_normed_one)
    grad_tokens = grad_residual + grad_stream
    grad_layout_tables = jnp.dot(
        grad_layout.reshape(2 * HEADS, LAYOUT_POS * LAYOUT_POS), layout_hot.T, precision=highest
    ).reshape(2, HEADS, BUCKETS)
    grad_tables = jnp.concatenate([grad_rel[None], grad_layout_tables], 0)
    grad_small = jnp.concatenate(
        [grad_gain_one, grad_gain_two, jnp.transpose(grad_tables, (0, 2, 1)).reshape(-1)]
    )
    grad_attn = jnp.concatenate([grad_qkv, grad_out_proj[None]], 0)
    owned_attn, owned_in, owned_down, owned_small = (
        lax.psum_scatter(grad_attn, ("dp", "fsdp"), scatter_dimension=1, tiled=True),
        lax.psum_scatter(grad_in, ("dp", "fsdp"), scatter_dimension=1, tiled=True),
        lax.psum_scatter(grad_down, ("dp", "fsdp"), scatter_dimension=0, tiled=True),
        lax.psum_scatter(grad_small, ("dp", "fsdp"), scatter_dimension=0, tiled=True),
    )
    local_squares = (
        jnp.sum(owned_attn * owned_attn)
        + jnp.sum(owned_in * owned_in)
        + jnp.sum(owned_down * owned_down)
        + jnp.sum(owned_small * owned_small)
    )
    grad_norm = jnp.sqrt(lax.psum(local_squares, ("dp", "fsdp")))
    clip_scale = clip_max / jnp.maximum(grad_norm, clip_max)
    attn_new = adamw_update(
        attn_master, attn_first, attn_second, owned_attn * clip_scale, matrix_rate, decay_rate
    )
    ffin_new = adamw_update(
        ffin_master, ffin_first, ffin_second, owned_in * clip_scale, matrix_rate, decay_rate
    )
    down_new = adamw_update(
        down_master, down_first, down_second, owned_down * clip_scale, matrix_rate, decay_rate
    )
    small_new = adamw_update(
        small_master, small_first, small_second, owned_small * clip_scale, small_rate, 0.0
    )
    return (
        block_out,
        grad_tokens,
        grad_norm,
        attn_new[0],
        attn_new[1],
        attn_new[2][1:],
        attn_new[2][0],
        ffin_new[0],
        ffin_new[1],
        ffin_new[2],
        down_new[0],
        down_new[1],
        down_new[2],
        small_new[0],
        small_new[1],
        small_new[2],
    )


MESH = pl.DeviceIdType.MESH
TILE = 256
HALF = 16
SLOTS = 4
VMEM_BYTES = 63 * 2**20
QKV_GROUPS = 4
OUT_GROUPS = 2
OUT_START = 12
FF_START = 16


def bucket_limits(tok_count):
    buckets = relative_buckets(tok_count, BUCKETS)[:, 0]
    return [int(np.argmax(buckets >= k)) for k in range(1, BUCKETS // 2)]


def dot(a, b):
    return lax.dot_general(a, b, (((1,), (0,)), ((), ())), preferred_element_type=jnp.float32)


def dot_nt(a, b):
    return lax.dot_general(a, b, (((1,), (1,)), ((), ())), preferred_element_type=jnp.float32)


def split_dot(a, b):
    high = a.astype(jnp.bfloat16)
    rest = (a - high.astype(jnp.float32)).astype(jnp.bfloat16)
    return dot(high, b) + dot(rest, b)


def iota(shape, dim):
    return lax.broadcasted_iota(jnp.int32, shape, dim)


def layer_kernel(
    sizes,
    page_ref,
    pos_ref,
    small_ref,
    tok_hbm,
    cot_hbm,
    attn_hbm,
    ffin_hbm,
    down_hbm,
    out_ref,
    gtok_ref,
    oattn_ref,
    oin_ref,
    odown_ref,
    osmall_ref,
    norm_ref,
    w,
    rh,
    rd,
    re,
    rf,
    own,
    smb,
    sga,
    sgr,
    sgz,
    nbr,
    nbz,
    tok,
    n1,
    n1t,
    qp,
    kp,
    vp,
    ctx,
    ctxt,
    res,
    n2,
    n2t,
    gout,
    goutt,
    gn,
    gctx,
    kxs,
    km,
    gv,
    lse,
    ggv,
    ggx,
    ggy,
    acc,
    hx,
    hxx,
    hq2,
    k2,
    hxt,
    hyt,
    dq,
    dk,
    dv,
    gains,
    gsum,
    load_sem,
    in_sem,
    ag_send,
    ag_recv,
    rs_send,
    rs_recv,
    sm_send,
    sm_recv,
):
    ny, nz, nx, per, ff_groups = sizes
    f32, bf16 = jnp.float32, jnp.bfloat16
    groups = QKV_GROUPS + OUT_GROUPS + ff_groups
    tok_count, width = tok.shape
    rows = w.shape[5]
    dp, fs = lax.axis_index("dp"), lax.axis_index("fsdp")
    y, c, z, x = dp // 2, dp % 2, fs // nx, fs % nx

    def device(yy, cc, zz, xx):
        return (yy * 2 + cc, zz * nx + xx)

    sib, xnb, ynb = device(y, 1 - c, z, x), device(y, c, z, 1 - x), device(1 - y, c, z, x)

    def zdev(k):
        return device(y, c, lax.rem(z + k, nz), x)

    def remote(src, dst, send, recv, dev):
        return pltpu.make_async_remote_copy(
            src_ref=src, dst_ref=dst, send_sem=send, recv_sem=recv, device_id=dev, device_id_type=MESH
        )

    barrier = pltpu.get_barrier_semaphore()
    for dev in [sib, xnb, ynb] + [zdev(k) for k in range(1, nz)]:
        pl.semaphore_signal(barrier, inc=1, device_id=dev, device_id_type=MESH)

    def on_group(g, fn):
        if isinstance(g, int):
            if 0 <= g < groups:
                if g < QKV_GROUPS:
                    fn(3 * g, 3, g)
                elif g < QKV_GROUPS + OUT_GROUPS:
                    fn(OUT_START + 2 * (g - QKV_GROUPS), 2, g)
                else:
                    fn(FF_START + 3 * (g - QKV_GROUPS - OUT_GROUPS), 3, g)
            return
        is_out = jnp.logical_and(g >= QKV_GROUPS, g < QKV_GROUPS + OUT_GROUPS)
        inside = jnp.logical_and(g >= 0, g < groups)

        @pl.when(is_out)
        def _():
            fn(OUT_START + 2 * (g - QKV_GROUPS), 2, g)

        @pl.when(jnp.logical_and(inside, jnp.logical_not(is_out)))
        def _():
            fn(jnp.where(g < QKV_GROUPS, 3 * g, FF_START + 3 * (g - QKV_GROUPS - OUT_GROUPS)), 3, g)

    def load(g):
        def go(t0, count, g):
            if count == 2:
                for i in range(2):
                    cols = pl.ds(pl.multiple_of((t0 - OUT_START + i) * TILE, TILE), TILE)
                    pltpu.make_async_copy(attn_hbm.at[3, :, cols], own.at[t0 + i], load_sem.at[g]).start()
            elif isinstance(g, int) and g < QKV_GROUPS:
                cols = pl.ds(g * TILE, TILE)
                pltpu.make_async_copy(
                    attn_hbm.at[pl.ds(0, 3), :, cols], own.at[pl.ds(t0, 3)], load_sem.at[g]
                ).start()
            else:
                cols = pl.ds((g - QKV_GROUPS - OUT_GROUPS) * TILE, TILE)
                pltpu.make_async_copy(
                    ffin_hbm.at[:, :, cols], own.at[pl.ds(t0, 2)], load_sem.at[g]
                ).start()
                pltpu.make_async_copy(down_hbm.at[:, cols], own.at[t0 + 2], load_sem.at[g]).start()

        on_group(g, go)

    def load_wait(g):
        def go(t0, count, g):
            tiles = own.at[pl.ds(t0, count)]
            pltpu.make_async_copy(tiles, tiles, load_sem.at[g]).wait()
            for i in range(count):
                w[t0 + i, y, c, z, x] = own[t0 + i].astype(bf16)

        on_group(g, go)

    for g in range(groups):
        load(g)
    tok_copy = pltpu.make_async_copy(tok_hbm, tok, in_sem.at[0])
    cot_copy = pltpu.make_async_copy(cot_hbm, gout, in_sem.at[1])
    tok_copy.start()
    cot_copy.start()

    def ag_parts(t0, count, g):
        t = pl.ds(t0, count)
        return t, (lambda i: ag_send.at[i, g]), (lambda i: ag_recv.at[i, g])

    def ag1(g):
        def go(t0, count, g):
            t, s, r = ag_parts(t0, count, g)
            mine = w.at[t, y, c, z, x]
            for k in range(1, nz):
                remote(mine, mine, s(0), r(0), zdev(k)).start()

        on_group(g, go)

    def ag2(g):
        def go(t0, count, g):
            t, s, r = ag_parts(t0, count, g)
            three = w.at[t, y, c, pl.ds(0, nz - 1), x]
            remote(three, three, s(0), r(0), zdev(1)).wait_recv()
            column = w.at[t, y, c, :, x]
            remote(column, column, s(1), r(1), xnb).start()
            remote(column, column, s(2), r(2), ynb).start()
            remote(column, column, s(5), r(5), sib).start()

        on_group(g, go)

    def ag3(g):
        def go(t0, count, g):
            t, s, r = ag_parts(t0, count, g)
            xcol = w.at[t, y, c, :, 1 - x]
            ycol = w.at[t, 1 - y, c, :, x]
            remote(xcol, xcol, s(1), r(1), xnb).wait_recv()
            xhalf = w.at[t, y, c, :, 1 - x, pl.ds(0, HALF)]
            remote(xhalf, xhalf, s(4), r(4), ynb).start()
            remote(xcol, xcol, s(5), r(5), sib).start()
            remote(ycol, ycol, s(2), r(2), ynb).wait_recv()
            yhalf = w.at[t, 1 - y, c, :, x, pl.ds(HALF, HALF)]
            remote(yhalf, yhalf, s(3), r(3), xnb).start()
            remote(ycol, ycol, s(5), r(5), sib).start()

        on_group(g, go)

    def ag4(g):
        def go(t0, count, g):
            t, s, r = ag_parts(t0, count, g)
            low = w.at[t, 1 - y, c, :, 1 - x, pl.ds(0, HALF)]
            high = w.at[t, 1 - y, c, :, 1 - x, pl.ds(HALF, HALF)]
            remote(low, low, s(4), r(4), ynb).wait_recv()
            remote(high, high, s(3), r(3), xnb).wait_recv()
            diag = w.at[t, 1 - y, c, :, 1 - x]
            remote(diag, diag, s(5), r(5), sib).start()

        on_group(g, go)

    def ag5(g):
        def go(t0, count, g):
            t, s, r = ag_parts(t0, count, g)
            plane = w.at[t, :, 1 - c]
            remote(plane, plane, s(5), r(5), sib).wait_recv()

        on_group(g, go)

    def ag_sent(g):
        def go(t0, count, g):
            t, s, r = ag_parts(t0, count, g)
            three = w.at[t, y, c, pl.ds(0, nz - 1), x]
            column = w.at[t, y, c, :, x]
            half = w.at[t, y, c, :, x, pl.ds(0, HALF)]
            plane = w.at[t, :, c]
            remote(three, three, s(0), r(0), zdev(1)).wait_send()
            remote(column, column, s(1), r(1), xnb).wait_send()
            remote(column, column, s(2), r(2), ynb).wait_send()
            remote(half, half, s(3), r(3), xnb).wait_send()
            remote(half, half, s(4), r(4), ynb).wait_send()
            remote(plane, plane, s(5), r(5), sib).wait_send()

        on_group(g, go)

    def ag_tick(t):
        ag2(t)
        ag3(t - 1)
        ag4(t - 2)
        ag5(t - 3)

    def rs_group(n):
        if isinstance(n, int):
            if n < 0 or n >= groups:
                return -1
            tail = n - ff_groups
            if tail < 0:
                return QKV_GROUPS + OUT_GROUPS + n
            return QKV_GROUPS + tail if tail < OUT_GROUPS else tail - OUT_GROUPS
        tail = n - ff_groups
        g = jnp.where(
            tail < 0,
            QKV_GROUPS + OUT_GROUPS + n,
            jnp.where(tail < OUT_GROUPS, QKV_GROUPS + tail, tail - OUT_GROUPS),
        )
        return jnp.where(jnp.logical_or(n < 0, n >= groups), -1, g)

    def on_sum(n, fn):
        slot = n % SLOTS if isinstance(n, int) else lax.rem(n + SLOTS, SLOTS)

        def go(t0, count, g):
            fn(t0, count, slot, (lambda i: rs_send.at[i, g]), (lambda i: rs_recv.at[i, g]))

        on_group(rs_group(n), go)

    def rs0(n):
        def go(t0, count, slot, s, r):
            remote(
                w.at[pl.ds(t0, count), :, 1 - c], rh.at[slot, pl.ds(0, count)], s(0), r(0), sib
            ).start()

        on_sum(n, go)

    def rs1(n):
        def go(t0, count, slot, s, r):
            t = pl.ds(t0, count)
            landed = rh.at[slot, pl.ds(0, count)]
            remote(w.at[t, :, 1 - c], landed, s(0), r(0), sib).wait_recv()

            def add(i, carry):
                for yy in range(ny):
                    w[t0 + i, yy, c] = w[t0 + i, yy, c] + rh[slot, i, yy]
                return carry

            lax.fori_loop(0, count, add, 0)
            for k, dev in ((0, xnb), (1, ynb)):
                remote(
                    w.at[t, 1 - y, c, :, 1 - x, pl.ds(k * HALF, HALF)],
                    rd.at[slot, k, pl.ds(0, count)],
                    s(1 + k),
                    r(1 + k),
                    dev,
                ).start()

        on_sum(n, go)

    def rs2(n):
        def go(t0, count, slot, s, r):
            t = pl.ds(t0, count)
            for k, dev, yy, xx in ((0, xnb, 1 - y, x), (1, ynb, y, 1 - x)):
                landed = rd.at[slot, k, pl.ds(0, count)]
                rows_k = pl.ds(k * HALF, HALF)
                remote(w.at[t, 1 - y, c, :, 1 - x, rows_k], landed, s(1 + k), r(1 + k), dev).wait_recv()
                for i in range(count):
                    w[t0 + i, yy, c, :, xx, rows_k] = w[t0 + i, yy, c, :, xx, rows_k] + rd[slot, k, i]
            for k, dev, yy, xx in ((0, xnb, y, 1 - x), (1, ynb, 1 - y, x)):
                remote(
                    w.at[t, yy, c, :, xx], re.at[slot, k, pl.ds(0, count)], s(3 + k), r(3 + k), dev
                ).start()

        on_sum(n, go)

    def rs3(n):
        def go(t0, count, slot, s, r):
            t = pl.ds(t0, count)
            for k, dev in ((0, xnb), (1, ynb)):
                landed = re.at[slot, k, pl.ds(0, count)]
                remote(w.at[t, y, c, :, x], landed, s(3 + k), r(3 + k), dev).wait_recv()
            for i in range(count):
                total = (
                    w[t0 + i, y, c, z, x].astype(f32)
                    + re[slot, 0, i, z].astype(f32)
                    + re[slot, 1, i, z].astype(f32)
                )
                own[t0 + i] = total
                for zz in range(nz):
                    w[t0 + i, y, c, zz, x] = (
                        w[t0 + i, y, c, zz, x].astype(f32)
                        + re[slot, 0, i, zz].astype(f32)
                        + re[slot, 1, i, zz].astype(f32)
                    ).astype(bf16)
            for k in range(1, nz):
                remote(
                    w.at[t, y, c, lax.rem(z + k, nz), x],
                    rf.at[slot, k - 1, pl.ds(0, count)],
                    s(5),
                    r(5),
                    zdev(k),
                ).start()

        on_sum(n, go)

    def rs4(n):
        def go(t0, count, slot, s, r):
            landed = rf.at[slot, :, pl.ds(0, count)]
            remote(landed, landed, s(5), r(5), zdev(1)).wait_recv()
            for i in range(count):
                total = own[t0 + i]
                for k in range(nz - 1):
                    total = total + rf[slot, k, i].astype(f32)
                own[t0 + i] = total

        on_sum(n, go)

    def rs_sent(g):
        def go(t0, count, g):
            t = pl.ds(t0, count)
            s, r = (lambda i: rs_send.at[i, g]), (lambda i: rs_recv.at[i, g])
            plane = w.at[t, :, c]
            half = w.at[t, y, c, :, x, pl.ds(0, HALF)]
            column = w.at[t, y, c, :, x]
            three = w.at[t, y, c, pl.ds(0, nz - 1), x]
            for i, part in enumerate((plane, half, half, column, column, three)):
                remote(part, part, s(i), r(i), sib).wait_send()

        on_group(g, go)

    def rs_tick(n):
        rs0(n)
        rs1(n - 1)
        rs2(n - 2)
        rs3(n - 3)
        rs4(n - 4)

    sm_steps = (
        (smb.at[y, c, z, x], None),
        (smb.at[y, c, :, x], xnb),
        (smb.at[y, c], ynb),
        (smb.at[:, c], sib),
    )

    def sm_start(i):
        part, dev = sm_steps[i]
        if i == 0:
            for k in range(1, nz):
                remote(part, part, sm_send.at[0], sm_recv.at[0], zdev(k)).start()
        else:
            remote(part, part, sm_send.at[i], sm_recv.at[i], dev).start()

    def sm_wait(i):
        part = (
            smb.at[y, c, pl.ds(0, nz - 1), x],
            smb.at[y, c, :, 1 - x],
            smb.at[1 - y, c],
            smb.at[:, 1 - c],
        )[i]
        dev = zdev(1) if i == 0 else sm_steps[i][1]
        copy = remote(part, part, sm_send.at[i], sm_recv.at[i], dev)
        copy.wait_recv()
        copy.wait_send()

    smb[y, c, z, x] = jnp.zeros(smb.shape[4:], f32)
    smb[y, c, z, x, 0:1, 0:per] = small_ref[...].astype(bf16).astype(f32)
    load_wait(0)
    pl.semaphore_wait(barrier, 3 + nz - 1)
    sm_start(0)
    ag1(0)
    for g in range(1, groups):
        load_wait(g)
        ag1(g)

    lane = iota((tok_count, 128), 1)
    row = iota((tok_count, 128), 0)
    first_len = page_ref[0, 0]
    both_len = page_ref[0, 0] + page_ref[1, 0]

    def pos_rows(k):
        line = pos_ref[k : k + 1, :].astype(f32)
        return jnp.broadcast_to(line, (128, tok_count)).T.astype(jnp.int32)

    pos_x, pos_y = pos_rows(0), pos_rows(1)
    hot_x = (pos_x == lane).astype(f32)
    hot_y = (pos_y == lane).astype(f32)
    page = jnp.where(row < first_len, 0, jnp.where(row < both_len, 1, 2))
    hx[...] = hot_x.astype(bf16)
    hxx[...] = (pos_x == lax.rem(lane, 64)).astype(f32).astype(bf16)
    hq2[...] = jnp.where(lane < 64, hot_y, (page == lane - 64).astype(f32)).astype(bf16)
    barred = jnp.where(jnp.logical_and(page == lane - 64, page < 2), 0.0, far_negative)
    k2[...] = jnp.where(lane < 64, hot_y, jnp.where(lane < 67, barred, 0.0)).astype(bf16)
    hxt[...] = hot_x.T[0:64].astype(bf16)
    hyt[...] = hot_y.T[0:64].astype(bf16)
    sm_wait(0)
    sm_start(1)
    ag_tick(0)
    cot_copy.wait()

    def mask_out(i, carry):
        at = pl.ds(pl.multiple_of(i * 128, 128), 128)
        valid = (iota((128, width), 0) + i * 128 < both_len).astype(f32)
        masked = valid * gout[at, :].astype(f32)
        gout[at, :] = masked.astype(bf16)
        goutt[:, at] = masked.T.astype(bf16)
        return carry

    lax.fori_loop(0, tok_count // 128, mask_out, 0)
    sm_wait(1)
    sm_start(2)
    ag_tick(1)
    sm_wait(2)
    sm_start(3)
    sm_wait(3)

    devs = [(a, b, d, e) for a in range(ny) for b in range(2) for d in range(nz) for e in range(nx)]
    lane1 = iota((1, 128), 1)

    def flat_tile(n):
        tile = jnp.zeros((1, 128), f32)
        for d in range(128 * n // per, (128 * n + 127) // per + 1):
            shift = d * per - 128 * n
            line = smb[devs[d] + (slice(0, 1), slice(None))]
            line = pltpu.roll(line, shift % 128, 1)
            inside = jnp.logical_and(lane1 >= shift, lane1 < shift + per)
            tile = jnp.where(inside, line, tile)
        return tile

    for n in range(2 * width // 128):
        gains[n // (width // 128), :, pl.ds(128 * (n % (width // 128)), 128)] = flat_tile(n)
    first_table = 2 * width // 128

    def table(k):
        flat = jnp.concatenate([flat_tile(first_table + 4 * k + i) for i in range(4)], axis=1)
        keep = lax.rem(iota((HEADS, 512), 1), HEADS) == iota((HEADS, 512), 0)
        return jnp.where(keep, jnp.broadcast_to(flat, (HEADS, 512)), 0.0).astype(bf16)

    def hot(bucket_line, count):
        return (iota((512, count), 0) // HEADS == bucket_line).astype(f32).astype(bf16)

    limits = bucket_limits(tok_count)
    span = 2 * tok_count

    def rel_bucket(offset):
        distance = jnp.abs(offset)
        bucket = jnp.where(offset > 0, BUCKETS // 2, 0)
        for limit in limits:
            bucket = bucket + (distance >= limit).astype(jnp.int32)
        return bucket

    def layout_bucket(offset):
        return jnp.clip(offset, -(BUCKETS // 2), BUCKETS // 2 - 1) + BUCKETS // 2

    rel_values = dot(table(0), hot(rel_bucket(tok_count - iota((1, span), 1)), span))
    for h in range(HEADS):
        gv[h, 0:1, :] = rel_values[h : h + 1]
    turned = jnp.where(lane1 < 64, lane1, lane1 - 128)
    x_even = dot(table(1), hot(layout_bucket(lane1 - 64), 128))
    x_odd = dot(table(1), hot(layout_bucket(turned), 128))
    y_any = dot(table(2), hot(layout_bucket(turned), 128))
    sq_lane, sq_row = iota((128, 128), 1), iota((128, 128), 0)

    def slope(line):
        return pltpu.roll(jnp.broadcast_to(line, (128, line.shape[1])), 0, 1, stride=1, stride_axis=0)

    for p in range(HEADS // 2):
        a, b = 2 * p, 2 * p + 1
        both = jnp.where(sq_lane < 64, slope(x_odd[b : b + 1]), slope(x_even[a : a + 1]))
        kxs[p] = jnp.where(sq_row < 64, both, 0.0).astype(bf16)
        for h in (a, b):
            part = jnp.where(sq_lane < 64, slope(y_any[h : h + 1]), 0.0)
            km[h] = jnp.where(sq_row < 64, part, (sq_lane == sq_row).astype(f32)).astype(bf16)

    tok_copy.wait()

    def norm_one(i, carry):
        at = pl.ds(pl.multiple_of(i * 128, 128), 128)
        stream = tok[at, :].astype(f32)
        scale = lax.rsqrt(jnp.mean(stream * stream, axis=-1, keepdims=True) + norm_eps)
        low = (stream * scale * gains[0]).astype(bf16)
        n1[at, :] = low
        n1t[:, at] = low.astype(f32).T.astype(bf16)
        return carry

    lax.fori_loop(0, tok_count // 128, norm_one, 0)
    ag_tick(2)

    def tile_of(t):
        return w[t].reshape(width, TILE)

    half_lane = iota((tok_count, 128), 1) < 64

    def pick(low, high):
        return jnp.where(half_lane, low.astype(f32), high.astype(f32)).astype(bf16)

    def augmented(p, e):
        shift = dot(hx[...], kxs[p])
        q_own, k_own = qp[p], kp[p]
        q_first = pick(q_own, shift) if e == 0 else pick(shift, q_own)
        k_first = pick(k_own, hxx[...]) if e == 0 else pick(hxx[...], k_own)
        q_second = dot(hq2[...], km[2 * p + e]).astype(bf16)
        return (
            jnp.concatenate([q_first, q_second], axis=1),
            jnp.concatenate([k_first, k2[...]], axis=1),
        )

    blocks = tok_count // 128
    half_rows = tok_count // 2

    def rel_bias(steep, part):
        return jnp.concatenate(
            [
                steep[:, tok_count - 128 * jb + half_rows * part : tok_count - 128 * jb + half_rows * (part + 1)]
                for jb in range(blocks)
            ],
            axis=0,
        )

    def forward_pair(p):
        v_turned = vp[p].astype(f32).T.astype(bf16)
        pieces = []
        for e in range(2):
            q_all, k_all = augmented(p, e)
            steep = slope(gv[2 * p + e, 0:1, :])
            parts = []
            for part in range(2):
                cols = slice(half_rows * part, half_rows * (part + 1))
                scores = dot_nt(k_all, q_all[cols]) + rel_bias(steep, part)
                top = jnp.max(scores, axis=0, keepdims=True)
                exponent = jnp.exp(scores - top)
                total = jnp.sum(exponent, axis=0, keepdims=True)
                probs = (exponent * (1.0 / total)).astype(bf16)
                lse[2 * p + e, 0:1, cols] = top + jnp.log(total)
                parts.append(dot(v_turned[64 * e : 64 * (e + 1)], probs))
            pieces.append(jnp.concatenate(parts, axis=1))
        turned = jnp.concatenate(pieces, axis=0)
        at = pl.ds(pl.multiple_of(p * 128, 128), 128)
        ctxt[at, :] = turned.astype(bf16)
        ctx[:, at] = turned.T.astype(bf16)

    def project(j):
        for i, dest in enumerate((qp, kp, vp)):
            result = dot(n1[...], tile_of(3 * j + i)).astype(bf16)
            dest[2 * j] = result[:, 0:128]
            dest[2 * j + 1] = result[:, 128:256]

    def forward_heads(j, carry):
        ag_tick(j + 3)
        project(j)

        def one(i, inner):
            forward_pair(2 * j + i)
            return inner

        lax.fori_loop(0, 2, one, 0)
        return carry

    lax.fori_loop(0, QKV_GROUPS, forward_heads, 0)
    ag_tick(7)
    ag_tick(8)

    for e in range(4):
        cols = pl.ds(e * TILE, TILE)
        res[:, cols] = tok[:, cols].astype(f32) + dot(ctx[...], tile_of(OUT_START + e))

    mix = gtok_ref

    def norm_two(i, carry):
        at = pl.ds(pl.multiple_of(i * 128, 128), 128)
        stream = res[at, :]
        scale = lax.rsqrt(jnp.mean(stream * stream, axis=-1, keepdims=True) + norm_eps)
        low = (stream * scale * gains[1]).astype(bf16)
        n2[at, :] = low
        n2t[:, at] = low.astype(f32).T.astype(bf16)
        mix[at, :] = stream
        gn[at, :] = jnp.zeros((128, width), f32)
        return carry

    lax.fori_loop(0, tok_count // 128, norm_two, 0)

    root = float(np.sqrt(2.0 / np.pi))

    def feed(f, carry):
        ag_tick(f + 9)
        t0 = FF_START + 3 * f
        gate_w, up_w, down_w = tile_of(t0), tile_of(t0 + 1), tile_of(t0 + 2)
        gate = dot(n2[...], gate_w)
        up = dot(n2[...], up_w)
        grad_hidden = dot(gout[...], down_w)
        square = gate * gate
        turn = jnp.tanh(root * gate * (1.0 + 0.044715 * square))
        half = 0.5 * (1.0 + turn)
        active = gate * half
        slope_of = half + 0.5 * gate * (1.0 - turn * turn) * (root * (1.0 + 3 * 0.044715 * square))
        hidden = (active * up).astype(bf16)
        grad_gate = (grad_hidden * up * slope_of).astype(bf16)
        grad_up = (grad_hidden * active).astype(bf16)
        mix[...] += dot_nt(hidden, down_w)
        gn[...] += dot_nt(grad_gate, gate_w) + dot_nt(grad_up, up_w)
        ag_sent(f + QKV_GROUPS + OUT_GROUPS)
        shape = w.shape[1:]
        w[t0] = dot(n2t[...], grad_gate).astype(bf16).reshape(shape)
        w[t0 + 1] = dot(n2t[...], grad_up).astype(bf16).reshape(shape)
        w[t0 + 2] = dot(goutt[...], hidden).astype(bf16).reshape(shape)
        rs_tick(f)
        return carry

    lax.fori_loop(0, ff_groups, feed, 0)

    gsum[...] = jnp.zeros_like(gsum)
    grad_res = mix

    def norm_two_back(i, carry):
        at = pl.ds(pl.multiple_of(i * 128, 128), 128)
        valid = (iota((128, width), 0) + i * 128 < both_len).astype(f32)
        out_ref[at, :] = (valid * mix[at, :]).astype(bf16)
        stream = res[at, :]
        scale = lax.rsqrt(jnp.mean(stream * stream, axis=-1, keepdims=True) + norm_eps)
        got = gn[at, :]
        gsum[1] += jnp.sum((got * stream * scale).reshape(16, 8, width), axis=0)
        scaled = gains[1] * got
        inner = jnp.mean(scaled * stream, axis=-1, keepdims=True)
        total = gout[at, :].astype(f32) + scale * scaled - stream * (scale * scale * scale * inner)
        grad_res[at, :] = total
        n2[at, :] = total.astype(bf16)
        gn[at, :] = jnp.zeros((128, width), f32)
        return carry

    lax.fori_loop(0, tok_count // 128, norm_two_back, 0)
    attended = n2
    shape = w.shape[1:]
    for yy in range(ny):
        for cc in range(2):
            part = jnp.zeros((tok_count, TILE), f32)
            for e in range(4):
                block = w[OUT_START + e, yy, cc].reshape(TILE, TILE)
                part = part + dot_nt(attended[:, pl.ds(e * TILE, TILE)], block)
            gctx[:, pl.ds((yy * 2 + cc) * TILE, TILE)] = part.astype(bf16)
    for i in range(OUT_GROUPS):
        ag_sent(QKV_GROUPS + i)
        for e in (2 * i, 2 * i + 1):
            w[OUT_START + e] = (
                dot(ctxt[...], attended[:, pl.ds(e * TILE, TILE)]).astype(bf16).reshape(shape)
            )
        rs_tick(ff_groups + i)

    flip = (sq_row + sq_lane == 127).astype(f32).astype(bf16)
    flip_halves = jnp.where(
        (sq_row < 64) == (sq_lane < 64), (lax.rem(sq_row, 64) + lax.rem(sq_lane, 64) == 63).astype(f32), 0.0
    ).astype(bf16)

    def split_left(matrix, value):
        high = value.astype(bf16)
        rest = (value - high.astype(f32)).astype(bf16)
        return dot(matrix, high) + dot(matrix, rest)

    def backward_pair(p, local):
        at = pl.ds(pl.multiple_of(p * 128, 128), 128)
        k_turned = kp[p].astype(f32).T.astype(bf16)
        grad_rows = gctx[:, at]
        dv_parts, dk_parts, dq_parts, x_parts, y_parts = [], [], [], [], []
        for e in range(2):
            h = 2 * p + e
            q_all, k_all = augmented(p, e)
            steep = slope(gv[h, 0:1, :])
            zero = jnp.zeros((tok_count, 128), f32)
            one_head = pick(grad_rows, zero) if e == 0 else pick(zero, grad_rows)
            left = jnp.concatenate([k_turned[64 * e : 64 * (e + 1)], hxt[...], hyt[...]], axis=0)
            acc[...] = jnp.zeros_like(acc)
            dv_e = jnp.zeros((tok_count, 128), f32)
            dk_e = jnp.zeros((tok_count, 128), f32)
            turned = []
            for part in range(2):
                cols = slice(half_rows * part, half_rows * (part + 1))
                scores = dot_nt(k_all, q_all[cols]) + rel_bias(steep, part)
                probs = jnp.exp(scores - lse[h, 0:1, cols])
                grad_probs = dot_nt(vp[p], one_head[cols])
                inner = jnp.sum(grad_probs * probs, axis=0, keepdims=True)
                grad_scores = (probs * (grad_probs - inner)).astype(bf16)
                dv_e = dv_e + dot(probs.astype(bf16), grad_rows[cols])
                dk_e = dk_e + dot(grad_scores, qp[p, cols])
                turned.append(dot(left, grad_scores))
                for jb in range(blocks):
                    start = tok_count - 128 * jb + half_rows * part
                    acc[:, start : start + half_rows] += grad_scores[128 * jb : 128 * (jb + 1)].astype(f32)
            all_turned = jnp.concatenate(turned, axis=1)
            dq_parts.append(all_turned[0:64])
            x_parts.append(all_turned[64:128])
            y_parts.append(all_turned[128:192])
            dv_parts.append(dv_e)
            dk_parts.append(dk_e)
            rolled = pltpu.roll(split_left(flip, acc[...]), 0, 1, stride=1, stride_axis=0)
            ggv[h, 0:1, :] = jnp.sum(rolled, axis=0, keepdims=True)
        low = half_lane
        cols = pl.ds(local * 128, 128)
        dq[:, cols] = jnp.concatenate(dq_parts, axis=0).T.astype(bf16)
        dk[:, cols] = jnp.where(low, dk_parts[0], dk_parts[1]).astype(bf16)
        dv[:, cols] = jnp.where(low, dv_parts[0], dv_parts[1]).astype(bf16)
        for parts, hots, dest in ((x_parts, hx, ggx), (y_parts, hq2, ggy)):
            table_grad = dot(jnp.concatenate(parts, axis=0).astype(bf16), hots[...])
            table_grad = jnp.where(sq_lane < 64, table_grad, 0.0)
            rolled = pltpu.roll(split_left(flip_halves, table_grad), 0, 1, stride=1, stride_axis=0)
            dest[2 * p, 0:1, :] = jnp.sum(rolled[0:64], axis=0, keepdims=True)
            dest[2 * p + 1, 0:1, :] = jnp.sum(rolled[64:128], axis=0, keepdims=True)

    def backward_heads(j, carry):
        for i in range(2):
            backward_pair(2 * j + i, i)
        gn[...] += (
            dot_nt(dq[...], tile_of(3 * j))
            + dot_nt(dk[...], tile_of(3 * j + 1))
            + dot_nt(dv[...], tile_of(3 * j + 2))
        )
        ag_sent(j)
        for i, part in enumerate((dq, dk, dv)):
            w[3 * j + i] = dot(n1t[...], part[...]).astype(bf16).reshape(shape)
        rs_tick(ff_groups + OUT_GROUPS + j)
        return carry

    lax.fori_loop(0, QKV_GROUPS, backward_heads, 0)
    rs_tick(groups)

    def norm_one_back(i, carry):
        at = pl.ds(pl.multiple_of(i * 128, 128), 128)
        stream = tok[at, :].astype(f32)
        scale = lax.rsqrt(jnp.mean(stream * stream, axis=-1, keepdims=True) + norm_eps)
        got = gn[at, :]
        gsum[0] += jnp.sum((got * stream * scale).reshape(16, 8, width), axis=0)
        scaled = gains[0] * got
        inner = jnp.mean(scaled * stream, axis=-1, keepdims=True)
        gtok_ref[at, :] = (
            grad_res[at, :] + scale * scaled - stream * (scale * scale * scale * inner)
        )
        return carry

    lax.fori_loop(0, tok_count // 128, norm_one_back, 0)

    def unhot(bucket_col, count):
        return (bucket_col == iota((count, 128), 1)).astype(f32).astype(bf16)

    def head_rows(ref, start=0):
        return jnp.concatenate([ref[h, 0:1, :] for h in range(start, HEADS, 1)], axis=0)

    col_span = iota((span, 128), 0)
    rel_source = lax.rem(col_span - 127 + span, span)
    rel_sum = split_dot(head_rows(ggv), unhot(rel_bucket(tok_count - rel_source), span))
    col_square = iota((128, 128), 0)
    low_source = lax.rem(col_square - 63 + 128, 128)
    high_source = lax.rem(col_square - 127 + 128, 128)

    def signed(source):
        return jnp.where(source < 64, source, source - 128)

    low_hot = unhot(layout_bucket(-signed(low_source)), 128)
    high_hot = unhot(layout_bucket(-signed(high_source)), 128)
    odd = lax.rem(iota((HEADS, 128), 0), 2) == 1

    def layout_sum(ref):
        lines = head_rows(ref)
        return jnp.where(odd, split_dot(lines, high_hot), split_dot(lines, low_hot))

    spread = (iota((128, 512), 0) == iota((128, 512), 1) // HEADS).astype(f32).astype(bf16)
    keep = lax.rem(iota((HEADS, 512), 1), HEADS) == iota((HEADS, 512), 0)

    def flat_table(value):
        high = value.astype(bf16)
        rest = (value - high.astype(f32)).astype(bf16)
        rest_two = (value - high.astype(f32) - rest.astype(f32)).astype(bf16)
        wide = dot(high, spread) + dot(rest, spread) + dot(rest_two, spread)
        return jnp.sum(jnp.where(keep, wide, 0.0), axis=0, keepdims=True)

    tiles = []
    for k in range(2):
        line = jnp.sum(gsum[k], axis=0, keepdims=True)
        tiles += [line[:, 128 * n : 128 * (n + 1)] for n in range(width // 128)]
    for value in (rel_sum, layout_sum(ggx), layout_sum(ggy)):
        line = flat_table(value)
        tiles += [line[:, 128 * n : 128 * (n + 1)] for n in range(4)]
    for d in range(len(devs)):
        line = jnp.zeros((1, 128), f32)
        for n in range(d * per // 128, (d * per + per - 1) // 128 + 1):
            shift = 128 * n - d * per
            moved = pltpu.roll(tiles[n], shift % 128, 1)
            inside = jnp.logical_and(lane1 >= shift, lane1 < min(shift + 128, per))
            line = jnp.where(inside, moved, line)
        sga[d : d + 1, :] = line

    def exchange(k, mine, landed, dev):
        copy = remote(mine, landed, sm_send.at[4 + k], sm_recv.at[4 + k], dev)
        copy.start()
        copy.wait_send()
        copy.wait_recv()

    def sum_all(k, mine, landed, lined):
        for i, dev in enumerate((sib, xnb, ynb)):
            exchange(k + i, mine, landed.at[i], dev)
            mine[...] = mine[...] + landed[i]
        lined[z] = mine[...]
        for i in range(1, nz):
            remote(lined.at[z], lined.at[z], sm_send.at[k + 7], sm_recv.at[k + 7], zdev(i)).start()
        three = lined.at[pl.ds(0, nz - 1)]
        copy = remote(three, three, sm_send.at[k + 7], sm_recv.at[k + 7], zdev(1))
        copy.wait_send()
        copy.wait_recv()
        total = lined[0]
        for i in range(1, nz):
            total = total + lined[i]
        return total

    small_total = sum_all(0, sga, sgr, sgz)
    me = ((y * 2 + c) * nz + z) * nx + x
    mine = iota(small_total.shape, 0) == me
    osmall_ref[...] = jnp.sum(jnp.where(mine, small_total, 0.0), axis=0, keepdims=True)
    for n in range(groups + 1, groups + 4):
        rs_tick(n)

    squares = jnp.zeros((8, TILE), f32)
    for t in range(own.shape[0]):
        value = own[t]
        squares = squares + jnp.sum((value * value).reshape(rows // 8, 8, TILE), axis=0)
    nbr[3] = squares[:, 0:128] + squares[:, 128:256]
    all_squares = sum_all(4, nbr.at[3], nbr, nbz)
    total = jnp.sum(all_squares) + jnp.sum(small_total * small_total)
    norm_ref[...] = jnp.full((8, 128), 1.0, f32) * total
    for j in range(QKV_GROUPS):
        cols = pl.ds(j * TILE, TILE)
        for i in range(3):
            oattn_ref[i, :, cols] = own[3 * j + i]
        oattn_ref[3, :, cols] = own[OUT_START + j]
    for f in range(ff_groups):
        cols = pl.ds(f * TILE, TILE)
        for i in range(2):
            oin_ref[i, :, cols] = own[FF_START + 3 * f + i]
        odown_ref[:, cols] = own[FF_START + 3 * f + 2]
    for g in range(groups):
        rs_sent(g)


def fused_on_device(
    tokens,
    cotangent,
    page_lengths,
    layout_pos,
    attn_master,
    attn_first,
    attn_second,
    ffin_master,
    ffin_first,
    ffin_second,
    down_master,
    down_first,
    down_second,
    small_master,
    small_first,
    small_second,
    *,
    ny,
    nz,
    nx,
):
    f32, bf16 = jnp.float32, jnp.bfloat16
    tok_count, width = tokens.shape
    rows, ff = down_master.shape
    per = small_master.shape[0]
    ff_groups = ff // TILE
    tiles = FF_START + 3 * ff_groups
    groups = QKV_GROUPS + OUT_GROUPS + ff_groups
    pairs = HEADS // 2
    vmem, dma = pltpu.VMEM, pltpu.SemaphoreType.DMA
    square = (tok_count, width)
    scratch = [
        vmem((tiles, ny, 2, nz, nx, rows, TILE), bf16),
        vmem((SLOTS, 3, ny, nz, nx, rows, TILE), bf16),
        vmem((SLOTS, 2, 3, nz, HALF, TILE), bf16),
        vmem((SLOTS, 2, 3, nz, rows, TILE), bf16),
        vmem((SLOTS, nz - 1, 3, rows, TILE), bf16),
        vmem((tiles, rows, TILE), f32),
        vmem((ny, 2, nz, nx, 8, 128), f32),
        vmem((ny * 2 * nz * nx, 128), f32),
        vmem((3, ny * 2 * nz * nx, 128), f32),
        vmem((nz, ny * 2 * nz * nx, 128), f32),
        vmem((4, 8, 128), f32),
        vmem((nz, 8, 128), f32),
        vmem(square, bf16),
        vmem(square, bf16),
        vmem((width, tok_count), bf16),
        vmem((pairs, tok_count, 128), bf16),
        vmem((pairs, tok_count, 128), bf16),
        vmem((pairs, tok_count, 128), bf16),
        vmem(square, bf16),
        vmem((width, tok_count), bf16),
        vmem(square, f32),
        vmem(square, bf16),
        vmem((width, tok_count), bf16),
        vmem(square, bf16),
        vmem((width, tok_count), bf16),
        vmem(square, f32),
        vmem(square, bf16),
        vmem((pairs, 128, 128), bf16),
        vmem((HEADS, 128, 128), bf16),
        vmem((HEADS, 8, 2 * tok_count), f32),
        vmem((HEADS, 8, tok_count), f32),
        vmem((HEADS, 8, 2 * tok_count), f32),
        vmem((HEADS, 8, 128), f32),
        vmem((HEADS, 8, 128), f32),
        vmem((128, 2 * tok_count), f32),
        vmem((tok_count, 128), bf16),
        vmem((tok_count, 128), bf16),
        vmem((tok_count, 128), bf16),
        vmem((tok_count, 128), bf16),
        vmem((64, tok_count), bf16),
        vmem((64, tok_count), bf16),
        vmem((tok_count, TILE), bf16),
        vmem((tok_count, TILE), bf16),
        vmem((tok_count, TILE), bf16),
        vmem((2, 1, width), f32),
        vmem((2, 8, width), f32),
        dma((groups,)),
        dma((2,)),
        dma((6, groups)),
        dma((6, groups)),
        dma((6, groups)),
        dma((6, groups)),
        dma((12,)),
        dma((12,)),
    ]
    in_vmem = pl.BlockSpec(memory_space=pltpu.VMEM)
    in_hbm = pl.BlockSpec(memory_space=pl.ANY)
    weights = attn_master.size + ffin_master.size + down_master.size
    block_out, grad_tokens, owned_attn, owned_in, owned_down, owned_small, squares = pl.pallas_call(
        functools.partial(layer_kernel, (ny, nz, nx, per, ff_groups)),
        out_shape=[
            jax.ShapeDtypeStruct(square, bf16),
            jax.ShapeDtypeStruct(square, f32),
            jax.ShapeDtypeStruct(attn_master.shape, f32),
            jax.ShapeDtypeStruct(ffin_master.shape, f32),
            jax.ShapeDtypeStruct(down_master.shape, f32),
            jax.ShapeDtypeStruct((1, 128), f32),
            jax.ShapeDtypeStruct((8, 128), f32),
        ],
        in_specs=[pl.BlockSpec(memory_space=pltpu.SMEM), in_vmem, in_vmem] + [in_hbm] * 5,
        out_specs=[in_vmem] * 7,
        scratch_shapes=scratch,
        compiler_params=pltpu.CompilerParams(
            collective_id=0, has_side_effects=True, vmem_limit_bytes=VMEM_BYTES
        ),
        cost_estimate=pl.CostEstimate(
            flops=6 * tok_count * weights * ny * 2 * nz * nx,
            bytes_accessed=24 * weights,
            transcendentals=3 * tok_count * tok_count * HEADS,
        ),
    )(
        page_lengths,
        layout_pos,
        small_master.reshape(1, per),
        tokens,
        cotangent,
        attn_master,
        ffin_master,
        down_master,
    )
    grad_norm = jnp.sqrt(squares[0, 0])
    clip_scale = clip_max / jnp.maximum(grad_norm, clip_max)
    attn_new = adamw_update(
        attn_master, attn_first, attn_second, owned_attn * clip_scale, matrix_rate, decay_rate
    )
    ffin_new = adamw_update(
        ffin_master, ffin_first, ffin_second, owned_in * clip_scale, matrix_rate, decay_rate
    )
    down_new = adamw_update(
        down_master, down_first, down_second, owned_down * clip_scale, matrix_rate, decay_rate
    )
    small_new = adamw_update(
        small_master, small_first, small_second, owned_small[0, :per] * clip_scale, small_rate, 0.0
    )
    return (
        block_out,
        grad_tokens,
        grad_norm,
        attn_new[0],
        attn_new[1],
        attn_new[2][1:],
        attn_new[2][0],
        ffin_new[0],
        ffin_new[1],
        ffin_new[2],
        down_new[0],
        down_new[1],
        down_new[2],
        small_new[0],
        small_new[1],
        small_new[2],
    )


def choose(mesh, width):
    n_dp, n_fsdp = mesh.shape["dp"], mesh.shape["fsdp"]
    rows = width // (n_dp * n_fsdp)
    if n_dp == 4 and n_fsdp % 2 == 0 and rows % (2 * HALF) == 0:
        return functools.partial(fused_on_device, ny=n_dp // 2, nz=n_fsdp // 2, nx=2)
    return on_device


def sharded(mesh, program):
    return jax.shard_map(
        program,
        mesh=mesh,
        in_specs=(
            P(("dp", "fsdp"), None),
            P(("dp", "fsdp"), None),
            P(None, ("dp", "fsdp")),
            P(None, ("dp", "fsdp")),
            P(None, ("dp", "fsdp"), None),
            P(None, ("dp", "fsdp"), None),
            P(None, ("dp", "fsdp"), None),
            P(None, ("dp", "fsdp"), None),
            P(None, ("dp", "fsdp"), None),
            P(None, ("dp", "fsdp"), None),
            P(("dp", "fsdp"), None),
            P(("dp", "fsdp"), None),
            P(("dp", "fsdp"), None),
            P(("dp", "fsdp")),
            P(("dp", "fsdp")),
            P(("dp", "fsdp")),
        ),
        out_specs=(
            P(("dp", "fsdp"), None),
            P(("dp", "fsdp"), None),
            P(),
            P(None, ("dp", "fsdp"), None),
            P(None, ("dp", "fsdp"), None),
            P(None, ("dp", "fsdp"), None),
            P(("dp", "fsdp"), None),
            P(None, ("dp", "fsdp"), None),
            P(None, ("dp", "fsdp"), None),
            P(None, ("dp", "fsdp"), None),
            P(("dp", "fsdp"), None),
            P(("dp", "fsdp"), None),
            P(("dp", "fsdp"), None),
            P(("dp", "fsdp")),
            P(("dp", "fsdp")),
            P(("dp", "fsdp")),
        ),
        check_vma=False,
    )


def solution(mesh):
    def step(*args):
        return sharded(mesh, choose(mesh, args[0].shape[1]))(*args)

    return step
```

```python
import functools

import jax
import jax.numpy as jnp
import numpy as np
from jax import lax
from jax.experimental import pallas as pl
from jax.experimental.pallas import tpu as pltpu
from jax.sharding import PartitionSpec as P

HEADS = 16
HEAD_DIM = 64
BUCKETS = 32
LAYOUT_POS = 64
STEP = 10


norm_eps = 1e-06
adam_eps = 1e-08
beta_one = 0.5
beta_two = 0.5
clip_max = 1.0
matrix_rate = 0.02
small_rate = 0.4
decay_rate = 0.01
far_negative = -1e30
max_distance = 128
block_rows = 512


def relative_buckets(tok_count, buckets):
    offsets = np.arange(tok_count)[None, :] - np.arange(tok_count)[:, None]
    half_count = buckets // 2
    exact_count = half_count // 2
    distance = np.abs(offsets)
    far_bucket = exact_count + (
        np.log(np.maximum(distance, 1) / exact_count)
        / np.log(max_distance / exact_count)
        * (half_count - exact_count)
    ).astype(np.int64)
    far_bucket = np.minimum(far_bucket, half_count - 1)
    bucket_ids = (offsets > 0).astype(np.int64) * half_count + np.where(
        distance < exact_count, distance, far_bucket
    )
    return bucket_ids.astype(np.int32)


def layout_table(positions, buckets):
    offsets = np.arange(positions)[None, :] - np.arange(positions)[:, None]
    half_count = buckets // 2
    bucket_ids = np.clip(offsets, -half_count, half_count - 1) + half_count
    return (np.arange(buckets)[:, None] == bucket_ids.reshape(1, -1)).astype(np.float32)


def scaled_norm(values, gain):
    return values * lax.rsqrt(jnp.mean(values * values, axis=-1, keepdims=True) + norm_eps) * gain


def gated_gelu(gate_pre, up_pre):
    return jax.nn.gelu(gate_pre, approximate=True) * up_pre


def adamw_update(master, first_state, second_state, gradient, step_rate, weight_decay):
    first_new = beta_one * first_state + (1.0 - beta_one) * gradient
    second_new = beta_two * second_state + (1.0 - beta_two) * gradient * gradient
    first_hat = first_new / (1.0 - beta_one**STEP)
    second_hat = second_new / (1.0 - beta_two**STEP)
    master_new = master - step_rate * (
        first_hat / (jnp.sqrt(second_hat) + adam_eps) + weight_decay * master
    )
    return (master_new, first_new, second_new)


def on_device(
    tokens,
    cotangent,
    page_lengths,
    layout_pos,
    attn_master,
    attn_first,
    attn_second,
    ffin_master,
    ffin_first,
    ffin_second,
    down_master,
    down_first,
    down_second,
    small_master,
    small_first,
    small_second,
):
    f32 = jnp.float32
    bf16 = jnp.bfloat16
    highest = lax.Precision.HIGHEST
    tok_count, model_width = tokens.shape
    attn_low = attn_master.astype(bf16)
    ffin_low = ffin_master.astype(bf16)
    down_low = down_master.astype(bf16)
    small_low = small_master.astype(bf16)
    w_attn, w_in, w_down, small_all = (
        lax.all_gather(attn_low, ("dp", "fsdp"), axis=1, tiled=True),
        lax.all_gather(ffin_low, ("dp", "fsdp"), axis=1, tiled=True),
        lax.all_gather(down_low, ("dp", "fsdp"), axis=0, tiled=True),
        lax.all_gather(small_low, ("dp", "fsdp"), axis=0, tiled=True),
    )
    gain_one = small_all[:model_width].astype(f32)
    gain_two = small_all[model_width : 2 * model_width].astype(f32)
    tables_t = jnp.transpose(small_all[2 * model_width :].reshape(3, BUCKETS, HEADS), (0, 2, 1))
    layout_hot = jnp.asarray(layout_table(LAYOUT_POS, BUCKETS))
    kernels = jnp.einsum(
        "khn,nm->khm", tables_t[1:], layout_hot.astype(bf16), preferred_element_type=f32
    )
    kernels = kernels.reshape(2, HEADS, LAYOUT_POS, LAYOUT_POS).astype(bf16)
    first_len = page_lengths[0, 0]
    both_len = page_lengths[0, 0] + page_lengths[1, 0]
    tok_index = jnp.arange(tok_count)
    page_ids = jnp.where(tok_index < first_len, 0, jnp.where(tok_index < both_len, 1, 2))
    valid_mask = tok_index < both_len
    valid_rows = valid_mask.astype(f32)[:, None]
    pos_grid = jnp.arange(LAYOUT_POS)
    pos_hot = (layout_pos[:, :, None] == pos_grid[None, None, :]).astype(bf16)
    pos_hot_f32 = pos_hot.astype(f32)
    rel_rows = jnp.asarray(relative_buckets(tok_count, BUCKETS))
    bucket_grid = jnp.arange(BUCKETS)
    rows_per_block = min(tok_count, block_rows)
    block_count = tok_count // rows_per_block
    block_starts = jnp.arange(block_count) * rows_per_block
    stream = tokens.astype(f32)
    normed_one = scaled_norm(stream, gain_one).astype(bf16)
    projected = jnp.einsum(
        "td,kde->kte", normed_one, w_attn[:3], preferred_element_type=f32
    ).astype(bf16)
    shaped = projected.reshape(3, tok_count, HEADS, HEAD_DIM)
    queries = shaped[0]
    key_rows = shaped[1]
    values = shaped[2]

    def block_scores(block_start, query_rows):
        rel_idx = lax.dynamic_slice_in_dim(rel_rows, block_start, rows_per_block, 0)
        rel_hot = (bucket_grid[:, None] == rel_idx.reshape(1, -1)).astype(bf16)
        bias_all = jnp.dot(tables_t[0], rel_hot, preferred_element_type=f32).reshape(
            HEADS, rows_per_block, tok_count
        )
        layout_rows = jnp.einsum(
            "kia,khab->khib", pos_hot, kernels, preferred_element_type=f32
        ).astype(bf16)
        bias_all = bias_all + jnp.einsum(
            "khib,kjb->hij", layout_rows, pos_hot, preferred_element_type=f32
        )
        scores = (
            jnp.einsum("ihe,jhe->hij", query_rows, key_rows, preferred_element_type=f32) + bias_all
        )
        allowed = (page_ids[:, None] == page_ids[None, :]) & valid_mask[None, :]
        masked = jnp.where(allowed[None], scores, far_negative)
        return (masked, allowed, rel_hot, pos_hot)

    def forward_block(running, block_start):
        masked, allowed, rel_hot, query_hot = block_scores(block_start, queries)
        row_max = jnp.max(masked, axis=-1, keepdims=True)
        exponent = jnp.exp(masked - row_max)
        row_total = jnp.sum(exponent, axis=-1, keepdims=True)
        weights_low = (exponent / row_total).astype(bf16)
        block_context = jnp.einsum("hij,jhe->ihe", weights_low, values, preferred_element_type=f32)
        return (running, (block_context, row_max + jnp.log(row_total)))

    unused_carry, (context_blocks, lse_blocks) = lax.scan(
        forward_block, jnp.zeros((), f32), block_starts
    )
    context = context_blocks.reshape(tok_count, model_width).astype(bf16)
    attended = jnp.dot(context, w_attn[3], preferred_element_type=f32)
    residual = stream + attended
    normed_two = scaled_norm(residual, gain_two).astype(bf16)
    gate_up = jnp.einsum("td,kdf->ktf", normed_two, w_in, preferred_element_type=f32)
    hidden = gated_gelu(gate_up[0], gate_up[1]).astype(bf16)
    mixed = jnp.einsum("tf,df->td", hidden, w_down, preferred_element_type=f32)
    block_out = (valid_rows * (residual + mixed)).astype(bf16)
    w_attn, w_in, w_down = (
        lax.all_gather(attn_low, ("dp", "fsdp"), axis=1, tiled=True),
        lax.all_gather(ffin_low, ("dp", "fsdp"), axis=1, tiled=True),
        lax.all_gather(down_low, ("dp", "fsdp"), axis=0, tiled=True),
    )
    grad_out = valid_rows * cotangent.astype(f32)
    grad_out_low = grad_out.astype(bf16)
    grad_down = jnp.einsum("td,tf->df", grad_out_low, hidden, preferred_element_type=f32)
    grad_hidden = jnp.einsum("td,df->tf", grad_out_low, w_down, preferred_element_type=f32)
    unused_gated, gated_pull = jax.vjp(gated_gelu, gate_up[0], gate_up[1])
    grad_gate, grad_up = gated_pull(grad_hidden)
    grad_gate_up = jnp.stack([grad_gate, grad_up]).astype(bf16)
    grad_in = jnp.einsum("td,ktf->kdf", normed_two, grad_gate_up, preferred_element_type=f32)
    grad_normed_two = jnp.einsum("ktf,kdf->td", grad_gate_up, w_in, preferred_element_type=f32)
    unused_second, norm_pull_two = jax.vjp(scaled_norm, residual, gain_two)
    grad_residual_norm, grad_gain_two = norm_pull_two(grad_normed_two)
    grad_residual = grad_out + grad_residual_norm
    grad_attended = grad_residual.astype(bf16)
    grad_out_proj = jnp.einsum("td,te->de", context, grad_attended, preferred_element_type=f32)
    grad_context = jnp.einsum(
        "te,de->td", grad_attended, w_attn[3], preferred_element_type=f32
    ).astype(bf16)
    grad_context = grad_context.reshape(tok_count, HEADS, HEAD_DIM)

    def backward_block(running, block_item):
        grad_key_rows, grad_value_rows, grad_rel, grad_layout = running
        block_start, lse_rows = block_item
        masked, allowed, rel_hot, query_hot = block_scores(block_start, queries)
        probs_f32 = jnp.exp(masked - lse_rows)
        grad_probs = jnp.einsum("ihe,jhe->hij", grad_context, values, preferred_element_type=f32)
        row_dot = jnp.sum(grad_probs * probs_f32, axis=-1, keepdims=True)
        grad_scores = jnp.where(allowed[None], probs_f32 * (grad_probs - row_dot), 0.0).astype(bf16)
        grad_query_rows = jnp.einsum(
            "hij,jhe->ihe", grad_scores, key_rows, preferred_element_type=f32
        )
        grad_key_rows = grad_key_rows + jnp.einsum(
            "hij,ihe->jhe", grad_scores, queries, preferred_element_type=f32
        )
        grad_value_rows = grad_value_rows + jnp.einsum(
            "hij,ihe->jhe", probs_f32.astype(bf16), grad_context, preferred_element_type=f32
        )
        grad_rel = grad_rel + lax.dot_general(
            grad_scores.reshape(HEADS, -1),
            rel_hot,
            (((1,), (1,)), ((), ())),
            preferred_element_type=f32,
        )
        query_sums = jnp.einsum("kia,hij->khaj", query_hot, grad_scores, preferred_element_type=f32)
        grad_layout = grad_layout + jnp.einsum(
            "khaj,kjb->khab", query_sums, pos_hot_f32, precision=highest
        )
        return ((grad_key_rows, grad_value_rows, grad_rel, grad_layout), grad_query_rows)

    start_state = (
        jnp.zeros((tok_count, HEADS, HEAD_DIM), f32),
        jnp.zeros((tok_count, HEADS, HEAD_DIM), f32),
        jnp.zeros((HEADS, BUCKETS), f32),
        jnp.zeros((2, HEADS, LAYOUT_POS, LAYOUT_POS), f32),
    )
    (grad_key_rows, grad_value_rows, grad_rel, grad_layout), grad_query_blocks = lax.scan(
        backward_block, start_state, (block_starts, lse_blocks)
    )
    grad_projected = jnp.stack(
        [
            grad_query_blocks.reshape(tok_count, model_width),
            grad_key_rows.reshape(tok_count, model_width),
            grad_value_rows.reshape(tok_count, model_width),
        ]
    ).astype(bf16)
    grad_qkv = jnp.einsum("td,kte->kde", normed_one, grad_projected, preferred_element_type=f32)
    grad_normed_one = jnp.einsum(
        "kte,kde->td", grad_projected, w_attn[:3], preferred_element_type=f32
    )
    unused_first, norm_pull_one = jax.vjp(scaled_norm, stream, gain_one)
    grad_stream, grad_gain_one = norm_pull_one(grad_normed_one)
    grad_tokens = grad_residual + grad_stream
    grad_layout_tables = jnp.dot(
        grad_layout.reshape(2 * HEADS, LAYOUT_POS * LAYOUT_POS), layout_hot.T, precision=highest
    ).reshape(2, HEADS, BUCKETS)
    grad_tables = jnp.concatenate([grad_rel[None], grad_layout_tables], 0)
    grad_small = jnp.concatenate(
        [grad_gain_one, grad_gain_two, jnp.transpose(grad_tables, (0, 2, 1)).reshape(-1)]
    )
    grad_attn = jnp.concatenate([grad_qkv, grad_out_proj[None]], 0)
    owned_attn, owned_in, owned_down, owned_small = (
        lax.psum_scatter(grad_attn, ("dp", "fsdp"), scatter_dimension=1, tiled=True),
        lax.psum_scatter(grad_in, ("dp", "fsdp"), scatter_dimension=1, tiled=True),
        lax.psum_scatter(grad_down, ("dp", "fsdp"), scatter_dimension=0, tiled=True),
        lax.psum_scatter(grad_small, ("dp", "fsdp"), scatter_dimension=0, tiled=True),
    )
    local_squares = (
        jnp.sum(owned_attn * owned_attn)
        + jnp.sum(owned_in * owned_in)
        + jnp.sum(owned_down * owned_down)
        + jnp.sum(owned_small * owned_small)
    )
    grad_norm = jnp.sqrt(lax.psum(local_squares, ("dp", "fsdp")))
    clip_scale = clip_max / jnp.maximum(grad_norm, clip_max)
    attn_new = adamw_update(
        attn_master, attn_first, attn_second, owned_attn * clip_scale, matrix_rate, decay_rate
    )
    ffin_new = adamw_update(
        ffin_master, ffin_first, ffin_second, owned_in * clip_scale, matrix_rate, decay_rate
    )
    down_new = adamw_update(
        down_master, down_first, down_second, owned_down * clip_scale, matrix_rate, decay_rate
    )
    small_new = adamw_update(
        small_master, small_first, small_second, owned_small * clip_scale, small_rate, 0.0
    )
    return (
        block_out,
        grad_tokens,
        grad_norm,
        attn_new[0],
        attn_new[1],
        attn_new[2][1:],
        attn_new[2][0],
        ffin_new[0],
        ffin_new[1],
        ffin_new[2],
        down_new[0],
        down_new[1],
        down_new[2],
        small_new[0],
        small_new[1],
        small_new[2],
    )


MESH = pl.DeviceIdType.MESH
TILE = 256
HALF = 16
SLOTS = 4
VMEM_BYTES = 63 * 2**20
Z_SLOTS = 10
AHEAD = 3
LATE_GROUPS = 3
SUM_LAG = 5
Z_FIRST_SUMS = (1, 5, 9)
LAGS = (1, 2, 3, 5, 7)
LINE_LAG = 2
D_SLOTS = 4
VMEM_BYTES = 63 * 2**20
FIRST_AHEAD = 0
LINE = 4
QKV_GROUPS = 4
OUT_GROUPS = 2
OUT_START = 12
FF_START = 16


def bucket_limits(tok_count):
    buckets = relative_buckets(tok_count, BUCKETS)[:, 0]
    return [int(np.argmax(buckets >= k)) for k in range(1, BUCKETS // 2)]


def dot(a, b):
    return lax.dot_general(a, b, (((1,), (0,)), ((), ())), preferred_element_type=jnp.float32)


def dot_nt(a, b):
    return lax.dot_general(a, b, (((1,), (1,)), ((), ())), preferred_element_type=jnp.float32)


def split_dot(a, b):
    high = a.astype(jnp.bfloat16)
    rest = (a - high.astype(jnp.float32)).astype(jnp.bfloat16)
    return dot(high, b) + dot(rest, b)


def iota(shape, dim):
    return lax.broadcasted_iota(jnp.int32, shape, dim)


def layer_kernel(
    sizes,
    page_ref,
    pos_ref,
    small_ref,
    tok_hbm,
    cot_hbm,
    attn_hbm,
    ffin_hbm,
    down_hbm,
    out_hbm,
    gtok_ref,
    own,
    osmall_ref,
    norm_ref,
    w,
    rh,
    rd,
    re,
    rf,
    rbz,
    rbd,
    rbe,
    smb,
    sgr,
    sgz,
    nbr,
    nbz,
    tok,
    n1,
    n1t,
    qp,
    kp,
    vp,
    ctx,
    ctxt,
    res,
    n2,
    n2t,
    gout,
    goutt,
    gn,
    kxs,
    km,
    gv,
    lse,
    ggx,
    ggy,
    acc,
    hx,
    hxx,
    hq2,
    k2,
    hxt,
    hyt,
    dq,
    dk,
    dv,
    gains,
    gsum,
    load_sem,
    in_sem,
    ag_send,
    ag_recv,
    late_send,
    late_recv,
    bl_send,
    bl_recv,
    rs_send,
    rs_recv,
    sm_send,
    sm_recv,
):
    ny, nz, nx, per, ff_groups = sizes
    f32, bf16 = jnp.float32, jnp.bfloat16
    groups = QKV_GROUPS + OUT_GROUPS + ff_groups
    tok_count, width = tok.shape
    rows = w.shape[5]
    dp, fs = lax.axis_index("dp"), lax.axis_index("fsdp")
    y, c, z, x = dp // 2, dp % 2, fs // nx, fs % nx

    def device(yy, cc, zz, xx):
        return (yy * 2 + cc, zz * nx + xx)

    sib, xnb, ynb = device(y, 1 - c, z, x), device(y, c, z, 1 - x), device(1 - y, c, z, x)

    def zdev(k):
        return device(y, c, lax.rem(z + k, nz), x)

    inner = jnp.logical_and(z > 0, z < LINE - 1)
    across = lax.rem(z + 2, LINE)
    edge = jnp.where(z < 2, 0, LINE - 1)
    inward = jnp.where(z < 2, 1, LINE - 2)
    far_end = LINE - 1 - edge
    dev_up, dev_down = device(y, c, jnp.minimum(z + 1, LINE - 1), x), device(y, c, jnp.maximum(z - 1, 0), x)
    dev_across, dev_edge, dev_inward = (device(y, c, at, x) for at in (across, edge, inward))

    def to_sides(send_up, send_down):
        pl.when(z < LINE - 1)(send_up)
        pl.when(z > 0)(send_down)

    def remote(src, dst, send, recv, dev):
        return pltpu.make_async_remote_copy(
            src_ref=src, dst_ref=dst, send_sem=send, recv_sem=recv, device_id=dev, device_id_type=MESH
        )

    cube = [(a, b, d) for a in range(ny) for b in range(2) for d in range(nx)][1:]

    def cube_dev(step):
        return device(*(1 - at if turn else at for at, turn in zip((y, c), step)), z, 1 - x if step[2] else x)

    near = (y * 2 + c) * nx + x

    barrier = pltpu.get_barrier_semaphore()
    for dev in [cube_dev(step) for step in cube] + [zdev(k) for k in range(1, nz)]:
        pl.semaphore_signal(barrier, inc=1, device_id=dev, device_id_type=MESH)

    def on_group(g, fn):
        if isinstance(g, int):
            if 0 <= g < groups:
                if g < QKV_GROUPS:
                    fn(3 * g, 3, g)
                elif g < QKV_GROUPS + OUT_GROUPS:
                    fn(OUT_START + 2 * (g - QKV_GROUPS), 2, g)
                else:
                    fn(FF_START + 3 * (g - QKV_GROUPS - OUT_GROUPS), 3, g)
            return
        is_out = jnp.logical_and(g >= QKV_GROUPS, g < QKV_GROUPS + OUT_GROUPS)
        inside = jnp.logical_and(g >= 0, g < groups)

        @pl.when(is_out)
        def _():
            fn(OUT_START + 2 * (g - QKV_GROUPS), 2, g)

        @pl.when(jnp.logical_and(inside, jnp.logical_not(is_out)))
        def _():
            fn(jnp.where(g < QKV_GROUPS, 3 * g, FF_START + 3 * (g - QKV_GROUPS - OUT_GROUPS)), 3, g)

    def load(g):
        def go(t0, count, g):
            if count == 2:
                for i in range(2):
                    cols = pl.ds(pl.multiple_of((t0 - OUT_START + i) * TILE, TILE), TILE)
                    pltpu.make_async_copy(attn_hbm.at[3, :, cols], own.at[t0 + i], load_sem.at[g]).start()
            elif isinstance(g, int) and g < QKV_GROUPS:
                cols = pl.ds(g * TILE, TILE)
                pltpu.make_async_copy(
                    attn_hbm.at[pl.ds(0, 3), :, cols], own.at[pl.ds(t0, 3)], load_sem.at[g]
                ).start()
            else:
                cols = pl.ds((g - QKV_GROUPS - OUT_GROUPS) * TILE, TILE)
                pltpu.make_async_copy(
                    ffin_hbm.at[:, :, cols], own.at[pl.ds(t0, 2)], load_sem.at[g]
                ).start()
                pltpu.make_async_copy(down_hbm.at[:, cols], own.at[t0 + 2], load_sem.at[g]).start()

        on_group(g, go)

    def load_wait(g):
        def go(t0, count, g):
            tiles = own.at[pl.ds(t0, count)]
            pltpu.make_async_copy(tiles, tiles, load_sem.at[g]).wait()
            for i in range(count):
                w[t0 + i, y, c, z, x] = own[t0 + i].astype(bf16)

        on_group(g, go)

    for g in range(groups):
        load(g)
    tok_copy = pltpu.make_async_copy(tok_hbm, tok, in_sem.at[0])
    cot_copy = pltpu.make_async_copy(cot_hbm, gout, in_sem.at[1])
    tok_copy.start()
    cot_copy.start()

    def ag_parts(t0, count, g):
        t = pl.ds(t0, count)
        return t, (lambda i: ag_send.at[i, g]), (lambda i: ag_recv.at[i, g])

    late_start = groups - LATE_GROUPS

    def on_early(g, fn):
        if isinstance(g, int):
            if g < late_start:
                on_group(g, fn)
        else:
            on_group(jnp.where(g < late_start, g, -1), fn)

    def on_late(g, fn):
        if isinstance(g, int):
            if late_start <= g < groups:
                on_group(g, fn)
        else:

            @pl.when(jnp.logical_and(g >= late_start, g < groups))
            def _():
                fn(FF_START + 3 * (g - QKV_GROUPS - OUT_GROUPS), 3, g)

    def late1(g):
        def go(t0, count, g):
            t, s, r = ag_parts(t0, count, g)
            mine = w.at[t, y, c, z, x]
            remote(mine, mine, s(1), r(1), xnb).start()
            remote(mine, mine, s(2), r(2), ynb).start()

        on_late(g, go)

    def late2(g):
        def go(t0, count, g):
            t, s, r = ag_parts(t0, count, g)
            xpart = w.at[t, y, c, z, 1 - x]
            ypart = w.at[t, 1 - y, c, z, x]
            remote(xpart, xpart, s(1), r(1), xnb).wait_recv()
            remote(ypart, ypart, s(2), r(2), ynb).wait_recv()
            xhalf = w.at[t, y, c, z, 1 - x, pl.ds(0, HALF)]
            yhalf = w.at[t, 1 - y, c, z, x, pl.ds(HALF, HALF)]
            remote(xhalf, xhalf, s(4), r(4), ynb).start()
            remote(yhalf, yhalf, s(3), r(3), xnb).start()

        on_late(g, go)

    def late3(g):
        def go(t0, count, g):
            t, s, r = ag_parts(t0, count, g)
            low = w.at[t, 1 - y, c, z, 1 - x, pl.ds(0, HALF)]
            high = w.at[t, 1 - y, c, z, 1 - x, pl.ds(HALF, HALF)]
            remote(low, low, s(4), r(4), ynb).wait_recv()
            remote(high, high, s(3), r(3), xnb).wait_recv()

        on_late(g, go)

    def late_tile(b):
        return FF_START + 3 * (ff_groups - LATE_GROUPS) + b

    def late_line(b):
        square = w.at[late_tile(b), :, c, z]
        s, r = late_send, late_recv
        to_sides(
            lambda: remote(square, square, s.at[0, b], r.at[0, b], dev_up).start(),
            lambda: remote(square, square, s.at[0, b], r.at[0, b], dev_down).start(),
        )
        remote(square, square, s.at[1, b], r.at[1, b], dev_across).start()

    def late_relay(b):
        landed = w.at[late_tile(b), :, c, across]
        s, r = late_send, late_recv
        remote(landed, landed, s.at[1, b], r.at[1, b], dev_across).wait_recv()

        @pl.when(inner)
        def _():
            remote(landed, landed, s.at[0, b], r.at[0, b], dev_edge).start()

    def late_step(t, fn):
        ticks = 3 * LATE_GROUPS * 3 // 2
        if isinstance(t, int):
            if 1 <= t <= ticks and t % 3:
                fn(t - 1 - t // 3)
        else:
            inside = jnp.logical_and(jnp.logical_and(t >= 1, t <= ticks), lax.rem(t, 3) != 0)

            @pl.when(inside)
            def _():
                fn(t - 1 - t // 3)

    def late4(g):
        def go(t0, count, g):
            t, s, r = ag_parts(t0, count, g)
            for i in range(3):
                b = t0 + i - late_tile(0)
                two = w.at[t0 + i, :, c, pl.ds(0, 2)]
                remote(two, two, late_send.at[0, b], late_recv.at[0, b], dev_across).wait_recv()
            plane = w.at[t, :, c]
            remote(plane, plane, s(5), r(5), sib).start()

        on_late(g, go)

    def ag1(g):
        def go(t0, count, g):
            t, s, r = ag_parts(t0, count, g)
            mine = w.at[t, y, c, z, x]
            to_sides(
                lambda: remote(mine, mine, s(0), r(0), dev_up).start(),
                lambda: remote(mine, mine, s(0), r(0), dev_down).start(),
            )
            remote(mine, mine, s(6), r(6), dev_across).start()

        on_early(g, go)

    def ag1_relay(g):
        def go(t0, count, g):
            t, s, r = ag_parts(t0, count, g)
            landed = w.at[t, y, c, across, x]
            remote(landed, landed, s(6), r(6), dev_across).wait_recv()

            @pl.when(inner)
            def _():
                remote(landed, landed, s(0), r(0), dev_edge).start()

        on_early(g, go)

    def ag2(g):
        def go(t0, count, g):
            t, s, r = ag_parts(t0, count, g)
            two = w.at[t, y, c, pl.ds(0, 2), x]
            remote(two, two, s(0), r(0), dev_across).wait_recv()
            column = w.at[t, y, c, :, x]
            remote(column, column, s(1), r(1), xnb).start()
            remote(column, column, s(2), r(2), ynb).start()
            remote(column, column, s(5), r(5), sib).start()

        on_early(g, go)

    def ag3(g):
        def go(t0, count, g):
            t, s, r = ag_parts(t0, count, g)
            xcol = w.at[t, y, c, :, 1 - x]
            ycol = w.at[t, 1 - y, c, :, x]
            remote(xcol, xcol, s(1), r(1), xnb).wait_recv()
            xhalf = w.at[t, y, c, :, 1 - x, pl.ds(0, HALF)]
            remote(xhalf, xhalf, s(4), r(4), ynb).start()
            remote(xcol, xcol, s(5), r(5), sib).start()
            remote(ycol, ycol, s(2), r(2), ynb).wait_recv()
            yhalf = w.at[t, 1 - y, c, :, x, pl.ds(HALF, HALF)]
            remote(yhalf, yhalf, s(3), r(3), xnb).start()
            remote(ycol, ycol, s(5), r(5), sib).start()

        on_early(g, go)

    def ag4(g):
        def go(t0, count, g):
            t, s, r = ag_parts(t0, count, g)
            low = w.at[t, 1 - y, c, :, 1 - x, pl.ds(0, HALF)]
            high = w.at[t, 1 - y, c, :, 1 - x, pl.ds(HALF, HALF)]
            remote(low, low, s(4), r(4), ynb).wait_recv()
            remote(high, high, s(3), r(3), xnb).wait_recv()
            diag = w.at[t, 1 - y, c, :, 1 - x]
            remote(diag, diag, s(5), r(5), sib).start()

        on_early(g, go)

    def ag5(g):
        def go(t0, count, g):
            t, s, r = ag_parts(t0, count, g)
            plane = w.at[t, :, 1 - c]
            remote(plane, plane, s(5), r(5), sib).wait_recv()

        on_group(g, go)

    def ag_sent(g):
        def go(t0, count, g):
            t, s, r = ag_parts(t0, count, g)
            one = w.at[t, y, c, z, x]
            column = w.at[t, y, c, :, x]
            half = w.at[t, y, c, :, x, pl.ds(0, HALF)]
            plane = w.at[t, :, c]
            for i, part in ((1, column), (2, column), (3, half), (4, half), (5, plane), (6, one)):
                remote(part, part, s(i), r(i), sib).wait_send()
            sent_sides(w.at[t, y, c, pl.ds(0, 3), x], one, s(0), r(0))

        on_early(g, go)

        def go_late(t0, count, g):
            t, s, r = ag_parts(t0, count, g)
            one = w.at[t, y, c, z, x]
            half = w.at[t, y, c, z, x, pl.ds(0, HALF)]
            plane = w.at[t, :, c]
            for i, part in ((1, one), (2, one), (3, half), (4, half), (5, plane)):
                remote(part, part, s(i), r(i), sib).wait_send()
            for i in range(3):
                b = t0 + i - late_tile(0)
                square = w.at[t0 + i, :, c, z]
                remote(square, square, late_send.at[1, b], late_recv.at[1, b], sib).wait_send()
                sent_sides(
                    w.at[t0 + i, :, c, pl.ds(0, 3)], square, late_send.at[0, b], late_recv.at[0, b]
                )

        on_late(g, go_late)

    def sent_sides(three, one, s, r):
        @pl.when(inner)
        def _():
            remote(three, three, s, r, sib).wait_send()

        @pl.when(jnp.logical_not(inner))
        def _():
            remote(one, one, s, r, sib).wait_send()

    def ag_tick(t):
        ag1(t + AHEAD)
        ag1_relay(t + FIRST_AHEAD + 1)
        ag2(t + FIRST_AHEAD)
        late_step(t, late_line)
        ag3(t - 1)
        late_step(t - 3, late_relay)
        ag4(t - 2)
        late4(t - 2)
        ag5(t - 3)

    def rs_group(n):
        if isinstance(n, int):
            if n < 0 or n >= groups:
                return -1
            tail = n - ff_groups
            if tail < 0:
                return QKV_GROUPS + OUT_GROUPS + n
            return QKV_GROUPS + tail if tail < OUT_GROUPS else tail - OUT_GROUPS
        tail = n - ff_groups
        g = jnp.where(
            tail < 0,
            QKV_GROUPS + OUT_GROUPS + n,
            jnp.where(tail < OUT_GROUPS, QKV_GROUPS + tail, tail - OUT_GROUPS),
        )
        return jnp.where(jnp.logical_or(n < 0, n >= groups), -1, g)

    def z_first(n):
        if isinstance(n, int):
            return n in Z_FIRST_SUMS
        return functools.reduce(jnp.logical_or, [n == m for m in Z_FIRST_SUMS])

    def on_sum(n, fn, kind=None):
        which = z_first(n)
        if isinstance(n, int):
            if kind is not None and which != kind:
                return
            slots = (n % SLOTS, n % Z_SLOTS, sum(n > m for m in Z_FIRST_SUMS), n % D_SLOTS)
            g = rs_group(n)
        else:
            bank = sum((n > m).astype(jnp.int32) for m in Z_FIRST_SUMS)
            slots = tuple(lax.rem(n + 10 * k, k) for k in (SLOTS, Z_SLOTS)) + (bank, lax.rem(n + 10 * D_SLOTS, D_SLOTS))
            g = rs_group(n)
            if kind is not None:
                g = jnp.where(which if kind else jnp.logical_not(which), g, -1)

        def go(t0, count, g):
            fn(t0, count, slots, (lambda i: rs_send.at[i, g]), (lambda i: rs_recv.at[i, g]))

        if kind:
            if isinstance(n, int):
                on_group(g, go)
            else:

                @pl.when(g >= 0)
                def _():
                    go(FF_START + 3 * (g - QKV_GROUPS - OUT_GROUPS), 3, g)

        else:
            on_group(g, go)

    def rs0(n):
        def go(t0, count, slots, s, r):
            slot = slots[0]
            remote(
                w.at[pl.ds(t0, count), :, 1 - c], rh.at[slot, pl.ds(0, count)], s(0), r(0), sib
            ).start()

        on_sum(n, go)

    def rs1(n):
        def go(t0, count, slots, s, r):
            slot = slots[0]
            t = pl.ds(t0, count)
            landed = rh.at[slot, pl.ds(0, count)]
            remote(w.at[t, :, 1 - c], landed, s(0), r(0), sib).wait_recv()

            def add(i, carry):
                for yy in range(ny):
                    w[t0 + i, yy, c] = w[t0 + i, yy, c] + rh[slot, i, yy]
                return carry

            lax.fori_loop(0, count, add, 0)

        on_sum(n, go)

        def go_early(t0, count, slots, s, r):
            for k, dev in ((0, xnb), (1, ynb)):
                remote(
                    w.at[pl.ds(t0, count), 1 - y, c, :, 1 - x, pl.ds(k * HALF, HALF)],
                    rd.at[slots[3], k, pl.ds(0, count)],
                    s(1 + k),
                    r(1 + k),
                    dev,
                ).start()

        on_sum(n, go_early, False)

    def rs1_line(n, i):
        def go_line(t0, count, slots, s, r):
            bank = slots[2]
            sems = line_sems(bank, i)
            line_sends(lambda at: w.at[t0 + i, :, c, at], lambda kind: rbz.at[bank, kind, i], *sems)

        on_sum(n, go_line, True)

    def line_sems(bank, i):
        return (lambda kind: bl_send.at[kind - 5, 3 * bank + i]), (lambda kind: bl_recv.at[kind - 5, 3 * bank + i])

    def line_sends(part, landed, s, r):
        to_sides(
            lambda: remote(part(dev_at(z + 1)), landed(0), s(5), r(5), dev_up).start(),
            lambda: remote(part(dev_at(z - 1)), landed(1), s(6), r(6), dev_down).start(),
        )

        @pl.when(jnp.logical_not(inner))
        def _():
            remote(part(across), landed(2), s(7), r(7), dev_across).start()
            remote(part(far_end), landed(3), s(8), r(8), dev_inward).start()

    def dev_at(at):
        return jnp.clip(at, 0, LINE - 1)

    def line_merge(part, landed, s, r, add):
        @pl.when(inner)
        def _():
            remote(part(across), landed(3), s(8), r(8), dev_edge).wait_recv()
            add()
            remote(part(across), landed(2), s(7), r(7), dev_across).start()

    def line_wait(part, landed, s, r, add):
        @pl.when(z > 0)
        def _():
            remote(part(z), landed(0), s(5), r(5), dev_down).wait_recv()
            add(0)

        @pl.when(z < LINE - 1)
        def _():
            remote(part(z), landed(1), s(6), r(6), dev_up).wait_recv()
            add(1)

        remote(part(z), landed(2), s(7), r(7), dev_across).wait_recv()
        add(2)

    def line_sent(part, s, r):
        pl.when(z < LINE - 1)(lambda: remote(part, part, s(5), r(5), sib).wait_send())
        pl.when(z > 0)(lambda: remote(part, part, s(6), r(6), sib).wait_send())
        remote(part, part, s(7), r(7), sib).wait_send()
        pl.when(jnp.logical_not(inner))(lambda: remote(part, part, s(8), r(8), sib).wait_send())

    def rs_merge(n):
        def go(t0, count, slots, s, r):
            t = pl.ds(t0, count)

            def add():
                for i in range(count):
                    w[t0 + i, y, c, across, x] = w[t0 + i, y, c, across, x] + rf[slots[1], 3, i]

            line_merge(
                lambda at: w.at[t, y, c, at, x], lambda kind: rf.at[slots[1], kind, pl.ds(0, count)], s, r, add
            )

        on_sum(n, go, False)

    def rs_line_merge(n, i):
        def go(t0, count, slots, s, r):
            bank = slots[2]

            def add():
                for yy in range(ny):
                    w[t0 + i, yy, c, across] = w[t0 + i, yy, c, across] + rbz[bank, 3, i, yy]

            sems = line_sems(bank, i)
            line_merge(lambda at: w.at[t0 + i, :, c, at], lambda kind: rbz.at[bank, kind, i], *sems, add)

        on_sum(n, go, True)

    def rs2(n):
        def go(t0, count, slots, s, r):
            slot = slots[3]
            t = pl.ds(t0, count)
            for k, dev, yy, xx in ((0, xnb, 1 - y, x), (1, ynb, y, 1 - x)):
                landed = rd.at[slot, k, pl.ds(0, count)]
                rows_k = pl.ds(k * HALF, HALF)
                remote(w.at[t, 1 - y, c, :, 1 - x, rows_k], landed, s(1 + k), r(1 + k), dev).wait_recv()
                for i in range(count):
                    w[t0 + i, yy, c, :, xx, rows_k] = w[t0 + i, yy, c, :, xx, rows_k] + rd[slot, k, i]
            for k, dev, yy, xx in ((0, xnb, y, 1 - x), (1, ynb, 1 - y, x)):
                remote(
                    w.at[t, yy, c, :, xx], re.at[slot, k, pl.ds(0, count)], s(3 + k), r(3 + k), dev
                ).start()

        on_sum(n, go, False)

    def rs2_line(n):
        def go_line(t0, count, slots, s, r):
            t = pl.ds(t0, count)
            bank = slots[2]
            for i in range(count):

                def add(kind, i=i):
                    for yy in range(ny):
                        w[t0 + i, yy, c, z] = w[t0 + i, yy, c, z] + rbz[bank, kind, i, yy]

                line_wait(
                    lambda at, i=i: w.at[t0 + i, :, c, at],
                    lambda kind, i=i: rbz.at[bank, kind, i],
                    *line_sems(bank, i),
                    add,
                )
            for k, dev in ((0, xnb), (1, ynb)):
                remote(
                    w.at[t, 1 - y, c, z, 1 - x, pl.ds(k * HALF, HALF)],
                    rbd.at[slots[2], k],
                    s(1 + k),
                    r(1 + k),
                    dev,
                ).start()

        on_sum(n, go_line, True)

    def rs3(n):
        def go(t0, count, slots, s, r):
            slot = slots[3]
            t = pl.ds(t0, count)
            for k, dev in ((0, xnb), (1, ynb)):
                landed = re.at[slot, k, pl.ds(0, count)]
                remote(w.at[t, y, c, :, x], landed, s(3 + k), r(3 + k), dev).wait_recv()
            for i in range(count):
                total = (
                    w[t0 + i, y, c, z, x].astype(f32)
                    + re[slot, 0, i, z].astype(f32)
                    + re[slot, 1, i, z].astype(f32)
                )
                own[t0 + i] = total
                for zz in range(nz):
                    w[t0 + i, y, c, zz, x] = (
                        w[t0 + i, y, c, zz, x].astype(f32)
                        + re[slot, 0, i, zz].astype(f32)
                        + re[slot, 1, i, zz].astype(f32)
                    ).astype(bf16)
            line_sends(
                lambda at: w.at[t, y, c, at, x], lambda kind: rf.at[slots[1], kind, pl.ds(0, count)], s, r
            )

        on_sum(n, go, False)

    def rs3_line(n):
        def go_line(t0, count, slots, s, r):
            t = pl.ds(t0, count)
            for k, dev, yy, xx in ((0, xnb, 1 - y, x), (1, ynb, y, 1 - x)):
                landed = rbd.at[slots[2], k]
                rows_k = pl.ds(k * HALF, HALF)
                remote(w.at[t, 1 - y, c, z, 1 - x, rows_k], landed, s(1 + k), r(1 + k), dev).wait_recv()
                for i in range(count):
                    w[t0 + i, yy, c, z, xx, rows_k] = w[t0 + i, yy, c, z, xx, rows_k] + rbd[slots[2], k, i]
            for k, dev, yy, xx in ((0, xnb, y, 1 - x), (1, ynb, 1 - y, x)):
                remote(w.at[t, yy, c, z, xx], rbe.at[slots[2], k], s(3 + k), r(3 + k), dev).start()

        on_sum(n, go_line, True)

    def rs4(n):
        def go(t0, count, slots, s, r):
            t = pl.ds(t0, count)

            def add(kind):
                for i in range(count):
                    own[t0 + i] += rf[slots[1], kind, i].astype(f32)

            line_wait(
                lambda at: w.at[t, y, c, at, x], lambda kind: rf.at[slots[1], kind, pl.ds(0, count)], s, r, add
            )

        on_sum(n, go, False)

    def rs4_line(n):
        def go_line(t0, count, slots, s, r):
            for k, dev in ((0, xnb), (1, ynb)):
                landed = rbe.at[slots[2], k]
                remote(landed, landed, s(3 + k), r(3 + k), dev).wait_recv()
            for i in range(count):
                own[t0 + i] = (
                    w[t0 + i, y, c, z, x].astype(f32)
                    + rbe[slots[2], 0, i].astype(f32)
                    + rbe[slots[2], 1, i].astype(f32)
                )

        on_sum(n, go_line, True)

    def rs_sent(n):
        def go(t0, count, slots, s, r):
            t = pl.ds(t0, count)
            plane = w.at[t, :, c]
            half = w.at[t, y, c, :, x, pl.ds(0, HALF)]
            column = w.at[t, y, c, :, x]
            for i, part in enumerate((plane, half, half, column, column)):
                remote(part, part, s(i), r(i), sib).wait_send()
            line_sent(w.at[t, y, c, z, x], s, r)

        on_sum(n, go, False)

        def go_line(t0, count, slots, s, r):
            t = pl.ds(t0, count)
            plane = w.at[t, :, c]
            half = w.at[t, y, c, z, x, pl.ds(0, HALF)]
            one = w.at[t, y, c, z, x]
            for i, part in enumerate((plane, half, half, one, one)):
                remote(part, part, s(i), r(i), sib).wait_send()
            for i in range(count):
                line_sent(w.at[t0 + i, :, c, z], *line_sems(slots[2], i))

        on_sum(n, go_line, True)

    def rs_tick(n):
        rs0(n)
        rs1(n - LAGS[0])
        for i in range(3):
            rs1_line(n - LAGS[0] - i, i)
        rs2(n - LAGS[1])
        rs3(n - LAGS[2])
        for i in range(3):
            rs_line_merge(n - LAGS[0] - LINE_LAG - i, i)
        rs_merge(n - LAGS[3])
        rs4(n - LAGS[4])
        rs2_line(n - LAGS[0] - 2 * LINE_LAG - 2)
        rs3_line(n - LAGS[0] - 2 * LINE_LAG - 3)
        rs4_line(n - LAGS[0] - 2 * LINE_LAG - 4)

    def cast_wait(copy):
        copy.wait_send()
        copy.wait_recv()

    def sm_start(i):
        if i == 0:
            part = smb.at[near, z]
            for k in range(1, nz):
                remote(part, part, sm_send.at[0], sm_recv.at[0], zdev(k)).start()
        else:
            part = smb.at[near]
            for step in cube:
                remote(part, part, sm_send.at[1], sm_recv.at[1], cube_dev(step)).start()

    def sm_wait(i):
        part = smb.at[near, pl.ds(0, nz - 1)] if i == 0 else smb.at[pl.ds(0, len(cube))]
        cast_wait(remote(part, part, sm_send.at[i], sm_recv.at[i], sib))

    smb[near, z] = jnp.zeros(smb.shape[2:], f32)
    smb[near, z, 0:1, 0:per] = small_ref[...].astype(bf16).astype(f32)
    load_wait(0)
    pl.semaphore_wait(barrier, len(cube) + nz - 1)
    sm_start(0)
    ag1(0)
    for g in range(1, AHEAD):
        load_wait(g)
        ag1(g)
    for g in range(late_start, groups):
        load_wait(g)
        late1(g)
    for g in range(AHEAD, late_start):
        load_wait(g)

    lane = iota((tok_count, 128), 1)
    row = iota((tok_count, 128), 0)
    first_len = page_ref[0, 0]
    both_len = page_ref[0, 0] + page_ref[1, 0]

    def pos_rows(k):
        line = pos_ref[k : k + 1, :].astype(f32)
        return jnp.broadcast_to(line, (128, tok_count)).T.astype(jnp.int32)

    pos_x, pos_y = pos_rows(0), pos_rows(1)
    hot_x = (pos_x == lane).astype(f32)
    hot_y = (pos_y == lane).astype(f32)
    page = jnp.where(row < first_len, 0, jnp.where(row < both_len, 1, 2))
    hx[...] = hot_x.astype(bf16)
    hxx[...] = (pos_x == lax.rem(lane, 64)).astype(f32).astype(bf16)
    hq2[...] = jnp.where(lane < 64, hot_y, (page == lane - 64).astype(f32)).astype(bf16)
    barred = jnp.where(jnp.logical_and(page == lane - 64, page < 2), 0.0, far_negative)
    k2[...] = jnp.where(lane < 64, hot_y, jnp.where(lane < 67, barred, 0.0)).astype(bf16)
    hxt[...] = hot_x.T[0:64].astype(bf16)
    hyt[...] = hot_y.T[0:64].astype(bf16)
    sm_wait(0)
    sm_start(1)
    for g in range(FIRST_AHEAD + 1):
        ag1_relay(g)
        if g < FIRST_AHEAD:
            ag2(g)
    ag_tick(0)
    for g in range(late_start, groups):
        late2(g)
    cot_copy.wait()

    def mask_out(i, carry):
        at = pl.ds(pl.multiple_of(i * 128, 128), 128)
        valid = (iota((128, width), 0) + i * 128 < both_len).astype(f32)
        masked = valid * gout[at, :].astype(f32)
        gout[at, :] = masked.astype(bf16)
        goutt[:, at] = masked.T.astype(bf16)
        return carry

    lax.fori_loop(0, tok_count // 128, mask_out, 0)
    for g in range(late_start, groups):
        late3(g)
    ag_tick(1)
    sm_wait(1)

    devs = [(a, b, d, e) for a in range(ny) for b in range(2) for d in range(nz) for e in range(nx)]
    lane1 = iota((1, 128), 1)

    def flat_tile(n):
        tile = jnp.zeros((1, 128), f32)
        for d in range(128 * n // per, (128 * n + 127) // per + 1):
            shift = d * per - 128 * n
            a, b, at_z, at_x = devs[d]
            line = smb[(a * 2 + b) * nx + at_x, at_z, 0:1, :]
            line = pltpu.roll(line, shift % 128, 1)
            inside = jnp.logical_and(lane1 >= shift, lane1 < shift + per)
            tile = jnp.where(inside, line, tile)
        return tile

    for n in range(2 * width // 128):
        gains[n // (width // 128), :, pl.ds(128 * (n % (width // 128)), 128)] = flat_tile(n)
    first_table = 2 * width // 128

    def table(k):
        flat = jnp.concatenate([flat_tile(first_table + 4 * k + i) for i in range(4)], axis=1)
        keep = lax.rem(iota((HEADS, 512), 1), HEADS) == iota((HEADS, 512), 0)
        return jnp.where(keep, jnp.broadcast_to(flat, (HEADS, 512)), 0.0).astype(bf16)

    def hot(bucket_line, count):
        return (iota((512, count), 0) // HEADS == bucket_line).astype(f32).astype(bf16)

    limits = bucket_limits(tok_count)
    span = 2 * tok_count

    def rel_bucket(offset):
        distance = jnp.abs(offset)
        bucket = jnp.where(offset > 0, BUCKETS // 2, 0)
        for limit in limits:
            bucket = bucket + (distance >= limit).astype(jnp.int32)
        return bucket

    def layout_bucket(offset):
        return jnp.clip(offset, -(BUCKETS // 2), BUCKETS // 2 - 1) + BUCKETS // 2

    rel_values = dot(table(0), hot(rel_bucket(tok_count - iota((1, span), 1)), span))
    for h in range(HEADS):
        gv[h, 0:1, :] = rel_values[h : h + 1]
    turned = jnp.where(lane1 < 64, lane1, lane1 - 128)
    x_even = dot(table(1), hot(layout_bucket(lane1 - 64), 128))
    x_odd = dot(table(1), hot(layout_bucket(turned), 128))
    y_any = dot(table(2), hot(layout_bucket(turned), 128))
    sq_lane, sq_row = iota((128, 128), 1), iota((128, 128), 0)

    def slope(line):
        return pltpu.roll(jnp.broadcast_to(line, (128, line.shape[1])), 0, 1, stride=1, stride_axis=0)

    for p in range(HEADS // 2):
        a, b = 2 * p, 2 * p + 1
        both = jnp.where(sq_lane < 64, slope(x_odd[b : b + 1]), slope(x_even[a : a + 1]))
        kxs[p] = jnp.where(sq_row < 64, both, 0.0).astype(bf16)
        for h in (a, b):
            part = jnp.where(sq_lane < 64, slope(y_any[h : h + 1]), 0.0)
            km[h] = jnp.where(sq_row < 64, part, (sq_lane == sq_row).astype(f32)).astype(bf16)

    tok_copy.wait()

    def norm_one(i, carry):
        at = pl.ds(pl.multiple_of(i * 128, 128), 128)
        stream = tok[at, :].astype(f32)
        scale = lax.rsqrt(jnp.mean(stream * stream, axis=-1, keepdims=True) + norm_eps)
        low = (stream * scale * gains[0]).astype(bf16)
        n1[at, :] = low
        n1t[:, at] = low.astype(f32).T.astype(bf16)
        return carry

    lax.fori_loop(0, tok_count // 128, norm_one, 0)
    ag_tick(2)

    def tile_of(t):
        return w[t].reshape(width, TILE)

    half_lane = iota((tok_count, 128), 1) < 64

    def pick(low, high):
        return jnp.where(half_lane, low.astype(f32), high.astype(f32)).astype(bf16)

    def augmented(p, e):
        shift = dot(hx[...], kxs[p])
        q_own, k_own = qp[p], kp[p]
        q_first = pick(q_own, shift) if e == 0 else pick(shift, q_own)
        k_first = pick(k_own, hxx[...]) if e == 0 else pick(hxx[...], k_own)
        q_second = dot(hq2[...], km[2 * p + e]).astype(bf16)
        return (
            jnp.concatenate([q_first, q_second], axis=1),
            jnp.concatenate([k_first, k2[...]], axis=1),
        )

    blocks = tok_count // 128
    half_rows = tok_count // 2

    def rel_bias(steep, part):
        return jnp.concatenate(
            [
                steep[:, tok_count - 128 * jb + half_rows * part : tok_count - 128 * jb + half_rows * (part + 1)]
                for jb in range(blocks)
            ],
            axis=0,
        )

    def forward_pair(p):
        v_turned = vp[p].astype(f32).T.astype(bf16)
        pieces = []
        for e in range(2):
            q_all, k_all = augmented(p, e)
            steep = slope(gv[2 * p + e, 0:1, :])
            parts = []
            for part in range(2):
                cols = slice(half_rows * part, half_rows * (part + 1))
                scores = dot_nt(k_all, q_all[cols]) + rel_bias(steep, part)
                top = jnp.max(scores, axis=0, keepdims=True)
                exponent = jnp.exp(scores - top)
                total = jnp.sum(exponent, axis=0, keepdims=True)
                probs = (exponent * (1.0 / total)).astype(bf16)
                lse[2 * p + e, 0:1, cols] = top + jnp.log(total)
                parts.append(dot(v_turned[64 * e : 64 * (e + 1)], probs))
            pieces.append(jnp.concatenate(parts, axis=1))
        turned = jnp.concatenate(pieces, axis=0)
        at = pl.ds(pl.multiple_of(p * 128, 128), 128)
        ctxt[at, :] = turned.astype(bf16)
        ctx[:, at] = turned.T.astype(bf16)

    def project(j):
        for i, dest in enumerate((qp, kp, vp)):
            result = dot(n1[...], tile_of(3 * j + i)).astype(bf16)
            dest[2 * j] = result[:, 0:128]
            dest[2 * j + 1] = result[:, 128:256]

    def forward_heads(j, carry):
        ag_tick(j + 3)
        project(j)

        def one(i, inner):
            forward_pair(2 * j + i)
            return inner

        lax.fori_loop(0, 2, one, 0)
        return carry

    lax.fori_loop(0, QKV_GROUPS, forward_heads, 0)
    ag_tick(7)
    ag_tick(8)

    for e in range(4):
        cols = pl.ds(e * TILE, TILE)
        res[:, cols] = tok[:, cols].astype(f32) + dot(ctx[...], tile_of(OUT_START + e))

    mix = gtok_ref

    def norm_two(i, carry):
        at = pl.ds(pl.multiple_of(i * 128, 128), 128)
        stream = res[at, :]
        scale = lax.rsqrt(jnp.mean(stream * stream, axis=-1, keepdims=True) + norm_eps)
        low = (stream * scale * gains[1]).astype(bf16)
        n2[at, :] = low
        n2t[:, at] = low.astype(f32).T.astype(bf16)
        mix[at, :] = stream
        gn[at, :] = jnp.zeros((128, width), f32)
        return carry

    lax.fori_loop(0, tok_count // 128, norm_two, 0)

    root = float(np.sqrt(2.0 / np.pi))

    def feed(f, carry):
        ag_tick(f + 9)
        t0 = FF_START + 3 * f
        gate_w, up_w, down_w = tile_of(t0), tile_of(t0 + 1), tile_of(t0 + 2)
        gate = dot(n2[...], gate_w)
        up = dot(n2[...], up_w)
        grad_hidden = dot(gout[...], down_w)
        square = gate * gate
        turn = jnp.tanh(root * gate * (1.0 + 0.044715 * square))
        half = 0.5 * (1.0 + turn)
        active = gate * half
        slope_of = half + 0.5 * gate * (1.0 - turn * turn) * (root * (1.0 + 3 * 0.044715 * square))
        hidden = (active * up).astype(bf16)
        grad_gate = (grad_hidden * up * slope_of).astype(bf16)
        grad_up = (grad_hidden * active).astype(bf16)
        mix[...] += dot_nt(hidden, down_w)
        gn[...] += dot_nt(grad_gate, gate_w) + dot_nt(grad_up, up_w)
        ag_sent(f + QKV_GROUPS + OUT_GROUPS)
        shape = w.shape[1:]
        w[t0] = dot(n2t[...], grad_gate).astype(bf16).reshape(shape)
        w[t0 + 1] = dot(n2t[...], grad_up).astype(bf16).reshape(shape)
        w[t0 + 2] = dot(goutt[...], hidden).astype(bf16).reshape(shape)
        rs_tick(f - SUM_LAG)
        return carry

    lax.fori_loop(0, ff_groups, feed, 0)

    gsum[...] = jnp.zeros_like(gsum)
    grad_res, gctx = mix, gout

    def norm_two_back(i, carry):
        at = pl.ds(pl.multiple_of(i * 128, 128), 128)
        valid = (iota((128, width), 0) + i * 128 < both_len).astype(f32)
        ctx[at, :] = (valid * mix[at, :]).astype(bf16)
        stream = res[at, :]
        scale = lax.rsqrt(jnp.mean(stream * stream, axis=-1, keepdims=True) + norm_eps)
        got = gn[at, :]
        gsum[1] += jnp.sum((got * stream * scale).reshape(16, 8, width), axis=0)
        scaled = gains[1] * got
        inner = jnp.mean(scaled * stream, axis=-1, keepdims=True)
        total = gout[at, :].astype(f32) + scale * scaled - stream * (scale * scale * scale * inner)
        grad_res[at, :] = total
        n2[at, :] = total.astype(bf16)
        gn[at, :] = jnp.zeros((128, width), f32)
        return carry

    lax.fori_loop(0, tok_count // 128, norm_two_back, 0)
    out_copy = pltpu.make_async_copy(ctx, out_hbm, in_sem.at[0])
    out_copy.start()
    attended = n2
    shape = w.shape[1:]
    done = ff_groups - SUM_LAG
    rs_tick(done)
    done += 1
    for yy in range(ny):
        for cc in range(2):
            part = jnp.zeros((tok_count, TILE), f32)
            for e in range(4):
                block = w[OUT_START + e, yy, cc].reshape(TILE, TILE)
                part = part + dot_nt(attended[:, pl.ds(e * TILE, TILE)], block)
            gctx[:, pl.ds((yy * 2 + cc) * TILE, TILE)] = part.astype(bf16)
    for i in range(OUT_GROUPS):
        ag_sent(QKV_GROUPS + i)
        for e in (2 * i, 2 * i + 1):
            w[OUT_START + e] = (
                dot(ctxt[...], attended[:, pl.ds(e * TILE, TILE)]).astype(bf16).reshape(shape)
            )
        rs_tick(done)
        done += 1

    flip = (sq_row + sq_lane == 127).astype(f32).astype(bf16)
    flip_halves = jnp.where(
        (sq_row < 64) == (sq_lane < 64), (lax.rem(sq_row, 64) + lax.rem(sq_lane, 64) == 63).astype(f32), 0.0
    ).astype(bf16)

    def split_left(matrix, value):
        high = value.astype(bf16)
        rest = (value - high.astype(f32)).astype(bf16)
        return dot(matrix, high) + dot(matrix, rest)

    def backward_pair(p, local):
        at = pl.ds(pl.multiple_of(p * 128, 128), 128)
        k_turned = kp[p].astype(f32).T.astype(bf16)
        grad_rows = gctx[:, at]
        dv_parts, dk_parts, dq_parts, x_parts, y_parts = [], [], [], [], []
        for e in range(2):
            h = 2 * p + e
            q_all, k_all = augmented(p, e)
            steep = slope(gv[h, 0:1, :])
            zero = jnp.zeros((tok_count, 128), f32)
            one_head = pick(grad_rows, zero) if e == 0 else pick(zero, grad_rows)
            left = jnp.concatenate([k_turned[64 * e : 64 * (e + 1)], hxt[...], hyt[...]], axis=0)
            acc[...] = jnp.zeros_like(acc)
            dv_e = jnp.zeros((tok_count, 128), f32)
            dk_e = jnp.zeros((tok_count, 128), f32)
            turned = []
            for part in range(2):
                cols = slice(half_rows * part, half_rows * (part + 1))
                scores = dot_nt(k_all, q_all[cols]) + rel_bias(steep, part)
                probs = jnp.exp(scores - lse[h, 0:1, cols])
                grad_probs = dot_nt(vp[p], one_head[cols])
                inner = jnp.sum(grad_probs * probs, axis=0, keepdims=True)
                grad_scores = (probs * (grad_probs - inner)).astype(bf16)
                dv_e = dv_e + dot(probs.astype(bf16), grad_rows[cols])
                dk_e = dk_e + dot(grad_scores, qp[p, cols])
                turned.append(dot(left, grad_scores))
                for jb in range(blocks):
                    start = tok_count - 128 * jb + half_rows * part
                    acc[:, start : start + half_rows] += grad_scores[128 * jb : 128 * (jb + 1)].astype(f32)
            all_turned = jnp.concatenate(turned, axis=1)
            dq_parts.append(all_turned[0:64])
            x_parts.append(all_turned[64:128])
            y_parts.append(all_turned[128:192])
            dv_parts.append(dv_e)
            dk_parts.append(dk_e)
            rolled = pltpu.roll(split_left(flip, acc[...]), 0, 1, stride=1, stride_axis=0)
            gv[h, 0:1, :] = jnp.sum(rolled, axis=0, keepdims=True)
        low = half_lane
        cols = pl.ds(local * 128, 128)
        dq[:, cols] = jnp.concatenate(dq_parts, axis=0).T.astype(bf16)
        dk[:, cols] = jnp.where(low, dk_parts[0], dk_parts[1]).astype(bf16)
        dv[:, cols] = jnp.where(low, dv_parts[0], dv_parts[1]).astype(bf16)
        for parts, hots, dest in ((x_parts, hx, ggx), (y_parts, hq2, ggy)):
            table_grad = dot(jnp.concatenate(parts, axis=0).astype(bf16), hots[...])
            table_grad = jnp.where(sq_lane < 64, table_grad, 0.0)
            rolled = pltpu.roll(split_left(flip_halves, table_grad), 0, 1, stride=1, stride_axis=0)
            dest[2 * p, 0:1, :] = jnp.sum(rolled[0:64], axis=0, keepdims=True)
            dest[2 * p + 1, 0:1, :] = jnp.sum(rolled[64:128], axis=0, keepdims=True)

    def backward_heads(j, carry):
        backward_pair(2 * j, 0)
        rs_tick(done + 2 * j)
        backward_pair(2 * j + 1, 1)
        gn[...] += (
            dot_nt(dq[...], tile_of(3 * j))
            + dot_nt(dk[...], tile_of(3 * j + 1))
            + dot_nt(dv[...], tile_of(3 * j + 2))
        )
        ag_sent(j)
        for i, part in enumerate((dq, dk, dv)):
            w[3 * j + i] = dot(n1t[...], part[...]).astype(bf16).reshape(shape)
        rs_tick(done + 2 * j + 1)
        return carry

    lax.fori_loop(0, QKV_GROUPS, backward_heads, 0)
    done += 2 * QKV_GROUPS
    rs_tick(done)

    def norm_one_back(i, carry):
        at = pl.ds(pl.multiple_of(i * 128, 128), 128)
        stream = tok[at, :].astype(f32)
        scale = lax.rsqrt(jnp.mean(stream * stream, axis=-1, keepdims=True) + norm_eps)
        got = gn[at, :]
        gsum[0] += jnp.sum((got * stream * scale).reshape(16, 8, width), axis=0)
        scaled = gains[0] * got
        inner = jnp.mean(scaled * stream, axis=-1, keepdims=True)
        gtok_ref[at, :] = (
            grad_res[at, :] + scale * scaled - stream * (scale * scale * scale * inner)
        )
        return carry

    lax.fori_loop(0, tok_count // 128, norm_one_back, 0)
    rs_tick(done + 1)

    def unhot(bucket_col, count):
        return (bucket_col == iota((count, 128), 1)).astype(f32).astype(bf16)

    def head_rows(ref, start=0):
        return jnp.concatenate([ref[h, 0:1, :] for h in range(start, HEADS, 1)], axis=0)

    col_span = iota((span, 128), 0)
    rel_source = lax.rem(col_span - 127 + span, span)
    rel_sum = split_dot(head_rows(gv), unhot(rel_bucket(tok_count - rel_source), span))
    col_square = iota((128, 128), 0)
    low_source = lax.rem(col_square - 63 + 128, 128)
    high_source = lax.rem(col_square - 127 + 128, 128)

    def signed(source):
        return jnp.where(source < 64, source, source - 128)

    low_hot = unhot(layout_bucket(-signed(low_source)), 128)
    high_hot = unhot(layout_bucket(-signed(high_source)), 128)
    odd = lax.rem(iota((HEADS, 128), 0), 2) == 1

    def layout_sum(ref):
        lines = head_rows(ref)
        return jnp.where(odd, split_dot(lines, high_hot), split_dot(lines, low_hot))

    spread = (iota((128, 512), 0) == iota((128, 512), 1) // HEADS).astype(f32).astype(bf16)
    keep = lax.rem(iota((HEADS, 512), 1), HEADS) == iota((HEADS, 512), 0)

    def flat_table(value):
        high = value.astype(bf16)
        rest = (value - high.astype(f32)).astype(bf16)
        rest_two = (value - high.astype(f32) - rest.astype(f32)).astype(bf16)
        wide = dot(high, spread) + dot(rest, spread) + dot(rest_two, spread)
        return jnp.sum(jnp.where(keep, wide, 0.0), axis=0, keepdims=True)

    tiles = []
    for k in range(2):
        line = jnp.sum(gsum[k], axis=0, keepdims=True)
        tiles += [line[:, 128 * n : 128 * (n + 1)] for n in range(width // 128)]
    for value in (rel_sum, layout_sum(ggx), layout_sum(ggy)):
        line = flat_table(value)
        tiles += [line[:, 128 * n : 128 * (n + 1)] for n in range(4)]
    for d in range(len(devs)):
        line = jnp.zeros((1, 128), f32)
        for n in range(d * per // 128, (d * per + per - 1) // 128 + 1):
            shift = 128 * n - d * per
            moved = pltpu.roll(tiles[n], shift % 128, 1)
            inside = jnp.logical_and(lane1 >= shift, lane1 < min(shift + 128, per))
            line = jnp.where(inside, moved, line)
        sgr[near, d : d + 1, :] = line

    def near_start(k, landed):
        part = landed.at[near]
        for step in cube:
            remote(part, part, sm_send.at[k], sm_recv.at[k], cube_dev(step)).start()

    def near_sum(k, landed, lined):
        part = landed.at[pl.ds(0, len(cube))]
        cast_wait(remote(part, part, sm_send.at[k], sm_recv.at[k], sib))
        total = landed[0]
        for i in range(1, len(cube) + 1):
            total = total + landed[i]
        lined[z] = total
        for i in range(1, nz):
            remote(lined.at[z], lined.at[z], sm_send.at[k + 1], sm_recv.at[k + 1], zdev(i)).start()

    def line_sum(k, lined):
        part = lined.at[pl.ds(0, nz - 1)]
        cast_wait(remote(part, part, sm_send.at[k + 1], sm_recv.at[k + 1], sib))
        total = lined[0]
        for i in range(1, nz):
            total = total + lined[i]
        return total

    near_start(2, sgr)
    rs_tick(done + 2)
    near_sum(2, sgr, sgz)
    for n in range(done + 3, groups + LAGS[4]):
        rs_tick(n)
    small_total = line_sum(2, sgz)
    me = ((y * 2 + c) * nz + z) * nx + x
    mine = iota(small_total.shape, 0) == me
    osmall_ref[...] = jnp.sum(jnp.where(mine, small_total, 0.0), axis=0, keepdims=True)

    squares = jnp.zeros((8, TILE), f32)
    for t in range(own.shape[0]):
        value = own[t]
        squares = squares + jnp.sum((value * value).reshape(rows // 8, 8, TILE), axis=0)
    nbr[near] = squares[:, 0:128] + squares[:, 128:256]
    near_start(4, nbr)
    out_copy.wait()
    for n in range(groups):
        rs_sent(n)
    near_sum(4, nbr, nbz)
    total = jnp.sum(line_sum(4, nbz)) + jnp.sum(small_total * small_total)
    norm_ref[...] = jnp.full((8, 128), 1.0, f32) * total


def update_kernel(
    sizes,
    total_ref,
    small_grad,
    small_master,
    small_first,
    small_second,
    own_hbm,
    block_hbm,
    gtok_hbm,
    attn_hbm,
    attn_first_hbm,
    attn_second_hbm,
    ffin_hbm,
    ffin_first_hbm,
    ffin_second_hbm,
    down_hbm,
    down_first_hbm,
    down_second_hbm,
    norm_out,
    small_master_out,
    small_first_out,
    small_second_out,
    block_out,
    gtok_out,
    attn_out,
    attn_first_out,
    attn_second_out,
    query_second_out,
    ffin_out,
    ffin_first_out,
    ffin_second_out,
    down_out,
    down_first_out,
    down_second_out,
    own,
    attn,
    ffin,
    down,
    block,
    gtok,
    in_sem,
    out_sem,
    pass_sem,
):
    (ff_groups,) = sizes
    passing = [
        pltpu.make_async_copy(block_hbm, block, pass_sem.at[0]),
        pltpu.make_async_copy(gtok_hbm, gtok, pass_sem.at[1]),
    ]
    passed = [
        pltpu.make_async_copy(block, block_out, pass_sem.at[2]),
        pltpu.make_async_copy(gtok, gtok_out, pass_sem.at[3]),
    ]
    first_tiles, other_tiles = pl.ds(0, FF_START), pl.ds(FF_START, 3 * ff_groups)
    loads = [
        [pltpu.make_async_copy(own_hbm.at[first_tiles], own.at[first_tiles], in_sem.at[0])],
        [pltpu.make_async_copy(own_hbm.at[other_tiles], own.at[other_tiles], in_sem.at[1])],
        [],
    ]
    sources = (
        (attn_hbm, attn_first_hbm, attn_second_hbm),
        (ffin_hbm, ffin_first_hbm, ffin_second_hbm),
        (down_hbm, down_first_hbm, down_second_hbm),
    )
    state = (attn, ffin, down)
    for i in range(3):
        loads[i] += [
            pltpu.make_async_copy(src, state[i].at[k], in_sem.at[2 + 3 * i + k])
            for k, src in enumerate(sources[i])
        ]
    for part in loads:
        for copy in part:
            copy.start()
    for copy in passing:
        copy.start()
    norm = jnp.sqrt(total_ref[0:1, 0:1])
    norm_out[...] = norm
    clip = clip_max / jnp.maximum(norm, clip_max)
    per = small_master.shape[1]
    results = adamw_update(
        small_master[...], small_first[...], small_second[...], small_grad[:, 0:per] * clip, small_rate, 0.0
    )
    for ref, value in zip((small_master_out, small_first_out, small_second_out), results):
        ref[...] = value

    def update(ref, at, tile):
        results = adamw_update(
            ref[(0,) + at], ref[(1,) + at], ref[(2,) + at], own[tile] * clip, matrix_rate, decay_rate
        )
        for k in range(3):
            ref[(k,) + at] = results[k]

    every = slice(None)
    stores = []

    def store(i, pairs):
        for src, dst in pairs:
            copy = pltpu.make_async_copy(src, dst, out_sem.at[len(stores)])
            copy.start()
            stores.append(copy)

    for copy in loads[0]:
        copy.wait()
    for j in range(QKV_GROUPS):
        cols = pl.ds(j * TILE, TILE)
        for i in range(3):
            update(attn, (i, every, cols), 3 * j + i)
        update(attn, (3, every, cols), OUT_START + j)
    store(
        0,
        [
            (attn.at[0], attn_out),
            (attn.at[1], attn_first_out),
            (attn.at[2, pl.ds(1, 3)], attn_second_out),
            (attn.at[2, 0], query_second_out),
        ],
    )
    for copy in loads[1]:
        copy.wait()

    def update_in(f, carry):
        cols = pl.ds(pl.multiple_of(f * TILE, TILE), TILE)
        for i in range(2):
            update(ffin, (i, every, cols), FF_START + 3 * f + i)
        return carry

    lax.fori_loop(0, ff_groups, update_in, 0)
    store(1, [(ffin.at[k], ref) for k, ref in enumerate((ffin_out, ffin_first_out, ffin_second_out))])
    for copy in loads[2]:
        copy.wait()

    def update_down(f, carry):
        cols = pl.ds(pl.multiple_of(f * TILE, TILE), TILE)
        update(down, (every, cols), FF_START + 3 * f + 2)
        return carry

    lax.fori_loop(0, ff_groups, update_down, 0)
    store(2, [(down.at[k], ref) for k, ref in enumerate((down_out, down_first_out, down_second_out))])
    for arrived, copy in zip(passing, passed):
        arrived.wait()
        copy.start()
    for copy in stores + passed:
        copy.wait()


def fused_on_device(
    tokens,
    cotangent,
    page_lengths,
    layout_pos,
    attn_master,
    attn_first,
    attn_second,
    ffin_master,
    ffin_first,
    ffin_second,
    down_master,
    down_first,
    down_second,
    small_master,
    small_first,
    small_second,
    *,
    ny,
    nz,
    nx,
):
    f32, bf16 = jnp.float32, jnp.bfloat16
    tok_count, width = tokens.shape
    rows, ff = down_master.shape
    per = small_master.shape[0]
    ff_groups = ff // TILE
    tiles = FF_START + 3 * ff_groups
    groups = QKV_GROUPS + OUT_GROUPS + ff_groups
    pairs = HEADS // 2
    vmem, dma = pltpu.VMEM, pltpu.SemaphoreType.DMA
    square = (tok_count, width)
    banks = len(Z_FIRST_SUMS)
    scratch = [
        vmem((tiles, ny, 2, nz, nx, rows, TILE), bf16),
        vmem((SLOTS, 3, ny, nz, nx, rows, TILE), bf16),
        vmem((D_SLOTS, 2, 3, nz, HALF, TILE), bf16),
        vmem((D_SLOTS, 2, 3, nz, rows, TILE), bf16),
        vmem((Z_SLOTS, 4, 3, rows, TILE), bf16),
        vmem((banks, 4, 3, ny, nx, rows, TILE), bf16),
        vmem((banks, 2, 3, HALF, TILE), bf16),
        vmem((banks, 2, 3, rows, TILE), bf16),
        vmem((ny * 2 * nx, nz, 8, 128), f32),
        vmem((ny * 2 * nx, ny * 2 * nz * nx, 128), f32),
        vmem((nz, ny * 2 * nz * nx, 128), f32),
        vmem((ny * 2 * nx, 8, 128), f32),
        vmem((nz, 8, 128), f32),
        vmem(square, bf16),
        vmem(square, bf16),
        vmem((width, tok_count), bf16),
        vmem((pairs, tok_count, 128), bf16),
        vmem((pairs, tok_count, 128), bf16),
        vmem((pairs, tok_count, 128), bf16),
        vmem(square, bf16),
        vmem((width, tok_count), bf16),
        vmem(square, f32),
        vmem(square, bf16),
        vmem((width, tok_count), bf16),
        vmem(square, bf16),
        vmem((width, tok_count), bf16),
        vmem(square, f32),
        vmem((pairs, 128, 128), bf16),
        vmem((HEADS, 128, 128), bf16),
        vmem((HEADS, 8, 2 * tok_count), f32),
        vmem((HEADS, 8, tok_count), f32),
        vmem((HEADS, 8, 128), f32),
        vmem((HEADS, 8, 128), f32),
        vmem((128, 2 * tok_count), f32),
        vmem((tok_count, 128), bf16),
        vmem((tok_count, 128), bf16),
        vmem((tok_count, 128), bf16),
        vmem((tok_count, 128), bf16),
        vmem((64, tok_count), bf16),
        vmem((64, tok_count), bf16),
        vmem((tok_count, TILE), bf16),
        vmem((tok_count, TILE), bf16),
        vmem((tok_count, TILE), bf16),
        vmem((2, 1, width), f32),
        vmem((2, 8, width), f32),
        dma((groups,)),
        dma((2,)),
        dma((7, groups)),
        dma((7, groups)),
        dma((2, 3 * LATE_GROUPS)),
        dma((2, 3 * LATE_GROUPS)),
        dma((4, 3 * banks)),
        dma((4, 3 * banks)),
        dma((9, groups)),
        dma((9, groups)),
        dma((6,)),
        dma((6,)),
    ]
    in_vmem = pl.BlockSpec(memory_space=pltpu.VMEM)
    in_hbm = pl.BlockSpec(memory_space=pl.ANY)
    weights = attn_master.size + ffin_master.size + down_master.size
    block_out, grad_tokens, owned, owned_small, squares = pl.pallas_call(
        functools.partial(layer_kernel, (ny, nz, nx, per, ff_groups)),
        out_shape=[
            jax.ShapeDtypeStruct(square, bf16),
            jax.ShapeDtypeStruct(square, f32),
            jax.ShapeDtypeStruct((tiles, rows, TILE), f32),
            jax.ShapeDtypeStruct((1, 128), f32),
            jax.ShapeDtypeStruct((8, 128), f32),
        ],
        in_specs=[pl.BlockSpec(memory_space=pltpu.SMEM), in_vmem, in_vmem] + [in_hbm] * 5,
        out_specs=[in_hbm] + [in_vmem] * 4,
        scratch_shapes=scratch,
        compiler_params=pltpu.CompilerParams(
            collective_id=0, has_side_effects=True, vmem_limit_bytes=VMEM_BYTES
        ),
        cost_estimate=pl.CostEstimate(
            flops=6 * tok_count * weights * ny * 2 * nz * nx,
            bytes_accessed=24 * weights,
            transcendentals=3 * tok_count * tok_count * HEADS,
        ),
    )(
        page_lengths,
        layout_pos,
        small_master.reshape(1, per),
        tokens,
        cotangent,
        attn_master,
        ffin_master,
        down_master,
    )
    like = [
        jax.ShapeDtypeStruct((1, 1), f32),
        *[jax.ShapeDtypeStruct((1, per), f32)] * 3,
        jax.ShapeDtypeStruct(square, bf16),
        jax.ShapeDtypeStruct(square, f32),
        jax.ShapeDtypeStruct(attn_master.shape, f32),
        jax.ShapeDtypeStruct(attn_master.shape, f32),
        jax.ShapeDtypeStruct((3,) + attn_master.shape[1:], f32),
        jax.ShapeDtypeStruct(attn_master.shape[1:], f32),
        *[jax.ShapeDtypeStruct(ffin_master.shape, f32)] * 3,
        *[jax.ShapeDtypeStruct(down_master.shape, f32)] * 3,
    ]
    results = pl.pallas_call(
        functools.partial(update_kernel, (ff_groups,)),
        out_shape=like,
        in_specs=[in_vmem] * 5 + [in_hbm] * 12,
        out_specs=[in_vmem] * 4 + [in_hbm] * 12,
        scratch_shapes=[
            vmem((tiles, rows, TILE), f32),
            vmem((3,) + attn_master.shape, f32),
            vmem((3,) + ffin_master.shape, f32),
            vmem((3,) + down_master.shape, f32),
            vmem(square, bf16),
            vmem(square, f32),
            dma((11,)),
            dma((10,)),
            dma((4,)),
        ],
        compiler_params=pltpu.CompilerParams(vmem_limit_bytes=VMEM_BYTES),
        cost_estimate=pl.CostEstimate(
            flops=20 * weights, bytes_accessed=28 * weights, transcendentals=2 * weights
        ),
    )(
        squares,
        owned_small,
        small_master.reshape(1, per),
        small_first.reshape(1, per),
        small_second.reshape(1, per),
        owned,
        block_out,
        grad_tokens,
        attn_master,
        attn_first,
        attn_second,
        ffin_master,
        ffin_first,
        ffin_second,
        down_master,
        down_first,
        down_second,
    )
    norm, small_new, small_one, small_two = results[:4]
    return (
        results[4],
        results[5],
        norm.reshape(()),
        *results[6:],
        small_new.reshape(per),
        small_one.reshape(per),
        small_two.reshape(per),
    )


def choose(mesh, width):
    n_dp, n_fsdp = mesh.shape["dp"], mesh.shape["fsdp"]
    rows = width // (n_dp * n_fsdp)
    if n_dp == 4 and n_fsdp == 2 * LINE and rows % (2 * HALF) == 0:
        return functools.partial(fused_on_device, ny=n_dp // 2, nz=n_fsdp // 2, nx=2)
    return on_device


def sharded(mesh, program):
    return jax.shard_map(
        program,
        mesh=mesh,
        in_specs=(
            P(("dp", "fsdp"), None),
            P(("dp", "fsdp"), None),
            P(None, ("dp", "fsdp")),
            P(None, ("dp", "fsdp")),
            P(None, ("dp", "fsdp"), None),
            P(None, ("dp", "fsdp"), None),
            P(None, ("dp", "fsdp"), None),
            P(None, ("dp", "fsdp"), None),
            P(None, ("dp", "fsdp"), None),
            P(None, ("dp", "fsdp"), None),
            P(("dp", "fsdp"), None),
            P(("dp", "fsdp"), None),
            P(("dp", "fsdp"), None),
            P(("dp", "fsdp")),
            P(("dp", "fsdp")),
            P(("dp", "fsdp")),
        ),
        out_specs=(
            P(("dp", "fsdp"), None),
            P(("dp", "fsdp"), None),
            P(),
            P(None, ("dp", "fsdp"), None),
            P(None, ("dp", "fsdp"), None),
            P(None, ("dp", "fsdp"), None),
            P(("dp", "fsdp"), None),
            P(None, ("dp", "fsdp"), None),
            P(None, ("dp", "fsdp"), None),
            P(None, ("dp", "fsdp"), None),
            P(("dp", "fsdp"), None),
            P(("dp", "fsdp"), None),
            P(("dp", "fsdp"), None),
            P(("dp", "fsdp")),
            P(("dp", "fsdp")),
            P(("dp", "fsdp")),
        ),
        check_vma=False,
    )


def solution(mesh):
    def step(*args):
        return sharded(mesh, choose(mesh, args[0].shape[1]))(*args)

    return step
```

```python
import functools

import jax
import jax.numpy as jnp
import numpy as np
from jax import lax
from jax.experimental import pallas as pl
from jax.experimental.pallas import tpu as pltpu
from jax.sharding import PartitionSpec as P

HEADS = 16
HEAD_DIM = 64
BUCKETS = 32
LAYOUT_POS = 64
STEP = 10


norm_eps = 1e-06
adam_eps = 1e-08
beta_one = 0.5
beta_two = 0.5
clip_max = 1.0
matrix_rate = 0.02
small_rate = 0.4
decay_rate = 0.01
far_negative = -1e30
max_distance = 128
block_rows = 512


def relative_buckets(tok_count, buckets):
    offsets = np.arange(tok_count)[None, :] - np.arange(tok_count)[:, None]
    half_count = buckets // 2
    exact_count = half_count // 2
    distance = np.abs(offsets)
    far_bucket = exact_count + (
        np.log(np.maximum(distance, 1) / exact_count)
        / np.log(max_distance / exact_count)
        * (half_count - exact_count)
    ).astype(np.int64)
    far_bucket = np.minimum(far_bucket, half_count - 1)
    bucket_ids = (offsets > 0).astype(np.int64) * half_count + np.where(
        distance < exact_count, distance, far_bucket
    )
    return bucket_ids.astype(np.int32)


def layout_table(positions, buckets):
    offsets = np.arange(positions)[None, :] - np.arange(positions)[:, None]
    half_count = buckets // 2
    bucket_ids = np.clip(offsets, -half_count, half_count - 1) + half_count
    return (np.arange(buckets)[:, None] == bucket_ids.reshape(1, -1)).astype(np.float32)


def scaled_norm(values, gain):
    return values * lax.rsqrt(jnp.mean(values * values, axis=-1, keepdims=True) + norm_eps) * gain


def gated_gelu(gate_pre, up_pre):
    return jax.nn.gelu(gate_pre, approximate=True) * up_pre


def adamw_update(master, first_state, second_state, gradient, step_rate, weight_decay):
    first_new = beta_one * first_state + (1.0 - beta_one) * gradient
    second_new = beta_two * second_state + (1.0 - beta_two) * gradient * gradient
    first_hat = first_new / (1.0 - beta_one**STEP)
    second_hat = second_new / (1.0 - beta_two**STEP)
    master_new = master - step_rate * (
        first_hat / (jnp.sqrt(second_hat) + adam_eps) + weight_decay * master
    )
    return (master_new, first_new, second_new)


def on_device(
    tokens,
    cotangent,
    page_lengths,
    layout_pos,
    attn_master,
    attn_first,
    attn_second,
    ffin_master,
    ffin_first,
    ffin_second,
    down_master,
    down_first,
    down_second,
    small_master,
    small_first,
    small_second,
):
    f32 = jnp.float32
    bf16 = jnp.bfloat16
    highest = lax.Precision.HIGHEST
    tok_count, model_width = tokens.shape
    attn_low = attn_master.astype(bf16)
    ffin_low = ffin_master.astype(bf16)
    down_low = down_master.astype(bf16)
    small_low = small_master.astype(bf16)
    w_attn, w_in, w_down, small_all = (
        lax.all_gather(attn_low, ("dp", "fsdp"), axis=1, tiled=True),
        lax.all_gather(ffin_low, ("dp", "fsdp"), axis=1, tiled=True),
        lax.all_gather(down_low, ("dp", "fsdp"), axis=0, tiled=True),
        lax.all_gather(small_low, ("dp", "fsdp"), axis=0, tiled=True),
    )
    gain_one = small_all[:model_width].astype(f32)
    gain_two = small_all[model_width : 2 * model_width].astype(f32)
    tables_t = jnp.transpose(small_all[2 * model_width :].reshape(3, BUCKETS, HEADS), (0, 2, 1))
    layout_hot = jnp.asarray(layout_table(LAYOUT_POS, BUCKETS))
    kernels = jnp.einsum(
        "khn,nm->khm", tables_t[1:], layout_hot.astype(bf16), preferred_element_type=f32
    )
    kernels = kernels.reshape(2, HEADS, LAYOUT_POS, LAYOUT_POS).astype(bf16)
    first_len = page_lengths[0, 0]
    both_len = page_lengths[0, 0] + page_lengths[1, 0]
    tok_index = jnp.arange(tok_count)
    page_ids = jnp.where(tok_index < first_len, 0, jnp.where(tok_index < both_len, 1, 2))
    valid_mask = tok_index < both_len
    valid_rows = valid_mask.astype(f32)[:, None]
    pos_grid = jnp.arange(LAYOUT_POS)
    pos_hot = (layout_pos[:, :, None] == pos_grid[None, None, :]).astype(bf16)
    pos_hot_f32 = pos_hot.astype(f32)
    rel_rows = jnp.asarray(relative_buckets(tok_count, BUCKETS))
    bucket_grid = jnp.arange(BUCKETS)
    rows_per_block = min(tok_count, block_rows)
    block_count = tok_count // rows_per_block
    block_starts = jnp.arange(block_count) * rows_per_block
    stream = tokens.astype(f32)
    normed_one = scaled_norm(stream, gain_one).astype(bf16)
    projected = jnp.einsum(
        "td,kde->kte", normed_one, w_attn[:3], preferred_element_type=f32
    ).astype(bf16)
    shaped = projected.reshape(3, tok_count, HEADS, HEAD_DIM)
    queries = shaped[0]
    key_rows = shaped[1]
    values = shaped[2]

    def block_scores(block_start, query_rows):
        rel_idx = lax.dynamic_slice_in_dim(rel_rows, block_start, rows_per_block, 0)
        rel_hot = (bucket_grid[:, None] == rel_idx.reshape(1, -1)).astype(bf16)
        bias_all = jnp.dot(tables_t[0], rel_hot, preferred_element_type=f32).reshape(
            HEADS, rows_per_block, tok_count
        )
        layout_rows = jnp.einsum(
            "kia,khab->khib", pos_hot, kernels, preferred_element_type=f32
        ).astype(bf16)
        bias_all = bias_all + jnp.einsum(
            "khib,kjb->hij", layout_rows, pos_hot, preferred_element_type=f32
        )
        scores = (
            jnp.einsum("ihe,jhe->hij", query_rows, key_rows, preferred_element_type=f32) + bias_all
        )
        allowed = (page_ids[:, None] == page_ids[None, :]) & valid_mask[None, :]
        masked = jnp.where(allowed[None], scores, far_negative)
        return (masked, allowed, rel_hot, pos_hot)

    def forward_block(running, block_start):
        masked, allowed, rel_hot, query_hot = block_scores(block_start, queries)
        row_max = jnp.max(masked, axis=-1, keepdims=True)
        exponent = jnp.exp(masked - row_max)
        row_total = jnp.sum(exponent, axis=-1, keepdims=True)
        weights_low = (exponent / row_total).astype(bf16)
        block_context = jnp.einsum("hij,jhe->ihe", weights_low, values, preferred_element_type=f32)
        return (running, (block_context, row_max + jnp.log(row_total)))

    unused_carry, (context_blocks, lse_blocks) = lax.scan(
        forward_block, jnp.zeros((), f32), block_starts
    )
    context = context_blocks.reshape(tok_count, model_width).astype(bf16)
    attended = jnp.dot(context, w_attn[3], preferred_element_type=f32)
    residual = stream + attended
    normed_two = scaled_norm(residual, gain_two).astype(bf16)
    gate_up = jnp.einsum("td,kdf->ktf", normed_two, w_in, preferred_element_type=f32)
    hidden = gated_gelu(gate_up[0], gate_up[1]).astype(bf16)
    mixed = jnp.einsum("tf,df->td", hidden, w_down, preferred_element_type=f32)
    block_out = (valid_rows * (residual + mixed)).astype(bf16)
    w_attn, w_in, w_down = (
        lax.all_gather(attn_low, ("dp", "fsdp"), axis=1, tiled=True),
        lax.all_gather(ffin_low, ("dp", "fsdp"), axis=1, tiled=True),
        lax.all_gather(down_low, ("dp", "fsdp"), axis=0, tiled=True),
    )
    grad_out = valid_rows * cotangent.astype(f32)
    grad_out_low = grad_out.astype(bf16)
    grad_down = jnp.einsum("td,tf->df", grad_out_low, hidden, preferred_element_type=f32)
    grad_hidden = jnp.einsum("td,df->tf", grad_out_low, w_down, preferred_element_type=f32)
    unused_gated, gated_pull = jax.vjp(gated_gelu, gate_up[0], gate_up[1])
    grad_gate, grad_up = gated_pull(grad_hidden)
    grad_gate_up = jnp.stack([grad_gate, grad_up]).astype(bf16)
    grad_in = jnp.einsum("td,ktf->kdf", normed_two, grad_gate_up, preferred_element_type=f32)
    grad_normed_two = jnp.einsum("ktf,kdf->td", grad_gate_up, w_in, preferred_element_type=f32)
    unused_second, norm_pull_two = jax.vjp(scaled_norm, residual, gain_two)
    grad_residual_norm, grad_gain_two = norm_pull_two(grad_normed_two)
    grad_residual = grad_out + grad_residual_norm
    grad_attended = grad_residual.astype(bf16)
    grad_out_proj = jnp.einsum("td,te->de", context, grad_attended, preferred_element_type=f32)
    grad_context = jnp.einsum(
        "te,de->td", grad_attended, w_attn[3], preferred_element_type=f32
    ).astype(bf16)
    grad_context = grad_context.reshape(tok_count, HEADS, HEAD_DIM)

    def backward_block(running, block_item):
        grad_key_rows, grad_value_rows, grad_rel, grad_layout = running
        block_start, lse_rows = block_item
        masked, allowed, rel_hot, query_hot = block_scores(block_start, queries)
        probs_f32 = jnp.exp(masked - lse_rows)
        grad_probs = jnp.einsum("ihe,jhe->hij", grad_context, values, preferred_element_type=f32)
        row_dot = jnp.sum(grad_probs * probs_f32, axis=-1, keepdims=True)
        grad_scores = jnp.where(allowed[None], probs_f32 * (grad_probs - row_dot), 0.0).astype(bf16)
        grad_query_rows = jnp.einsum(
            "hij,jhe->ihe", grad_scores, key_rows, preferred_element_type=f32
        )
        grad_key_rows = grad_key_rows + jnp.einsum(
            "hij,ihe->jhe", grad_scores, queries, preferred_element_type=f32
        )
        grad_value_rows = grad_value_rows + jnp.einsum(
            "hij,ihe->jhe", probs_f32.astype(bf16), grad_context, preferred_element_type=f32
        )
        grad_rel = grad_rel + lax.dot_general(
            grad_scores.reshape(HEADS, -1),
            rel_hot,
            (((1,), (1,)), ((), ())),
            preferred_element_type=f32,
        )
        query_sums = jnp.einsum("kia,hij->khaj", query_hot, grad_scores, preferred_element_type=f32)
        grad_layout = grad_layout + jnp.einsum(
            "khaj,kjb->khab", query_sums, pos_hot_f32, precision=highest
        )
        return ((grad_key_rows, grad_value_rows, grad_rel, grad_layout), grad_query_rows)

    start_state = (
        jnp.zeros((tok_count, HEADS, HEAD_DIM), f32),
        jnp.zeros((tok_count, HEADS, HEAD_DIM), f32),
        jnp.zeros((HEADS, BUCKETS), f32),
        jnp.zeros((2, HEADS, LAYOUT_POS, LAYOUT_POS), f32),
    )
    (grad_key_rows, grad_value_rows, grad_rel, grad_layout), grad_query_blocks = lax.scan(
        backward_block, start_state, (block_starts, lse_blocks)
    )
    grad_projected = jnp.stack(
        [
            grad_query_blocks.reshape(tok_count, model_width),
            grad_key_rows.reshape(tok_count, model_width),
            grad_value_rows.reshape(tok_count, model_width),
        ]
    ).astype(bf16)
    grad_qkv = jnp.einsum("td,kte->kde", normed_one, grad_projected, preferred_element_type=f32)
    grad_normed_one = jnp.einsum(
        "kte,kde->td", grad_projected, w_attn[:3], preferred_element_type=f32
    )
    unused_first, norm_pull_one = jax.vjp(scaled_norm, stream, gain_one)
    grad_stream, grad_gain_one = norm_pull_one(grad_normed_one)
    grad_tokens = grad_residual + grad_stream
    grad_layout_tables = jnp.dot(
        grad_layout.reshape(2 * HEADS, LAYOUT_POS * LAYOUT_POS), layout_hot.T, precision=highest
    ).reshape(2, HEADS, BUCKETS)
    grad_tables = jnp.concatenate([grad_rel[None], grad_layout_tables], 0)
    grad_small = jnp.concatenate(
        [grad_gain_one, grad_gain_two, jnp.transpose(grad_tables, (0, 2, 1)).reshape(-1)]
    )
    grad_attn = jnp.concatenate([grad_qkv, grad_out_proj[None]], 0)
    owned_attn, owned_in, owned_down, owned_small = (
        lax.psum_scatter(grad_attn, ("dp", "fsdp"), scatter_dimension=1, tiled=True),
        lax.psum_scatter(grad_in, ("dp", "fsdp"), scatter_dimension=1, tiled=True),
        lax.psum_scatter(grad_down, ("dp", "fsdp"), scatter_dimension=0, tiled=True),
        lax.psum_scatter(grad_small, ("dp", "fsdp"), scatter_dimension=0, tiled=True),
    )
    local_squares = (
        jnp.sum(owned_attn * owned_attn)
        + jnp.sum(owned_in * owned_in)
        + jnp.sum(owned_down * owned_down)
        + jnp.sum(owned_small * owned_small)
    )
    grad_norm = jnp.sqrt(lax.psum(local_squares, ("dp", "fsdp")))
    clip_scale = clip_max / jnp.maximum(grad_norm, clip_max)
    attn_new = adamw_update(
        attn_master, attn_first, attn_second, owned_attn * clip_scale, matrix_rate, decay_rate
    )
    ffin_new = adamw_update(
        ffin_master, ffin_first, ffin_second, owned_in * clip_scale, matrix_rate, decay_rate
    )
    down_new = adamw_update(
        down_master, down_first, down_second, owned_down * clip_scale, matrix_rate, decay_rate
    )
    small_new = adamw_update(
        small_master, small_first, small_second, owned_small * clip_scale, small_rate, 0.0
    )
    return (
        block_out,
        grad_tokens,
        grad_norm,
        attn_new[0],
        attn_new[1],
        attn_new[2][1:],
        attn_new[2][0],
        ffin_new[0],
        ffin_new[1],
        ffin_new[2],
        down_new[0],
        down_new[1],
        down_new[2],
        small_new[0],
        small_new[1],
        small_new[2],
    )


MESH = pl.DeviceIdType.MESH
TILE = 256
HALF = 16
SLOTS = 4
VMEM_BYTES = 63 * 2**20
Z_SLOTS = 12
AHEAD = 3
LATE_GROUPS = 3
SUM_LAG = 5
Z_FIRST_SUMS = (1, 5, 9)
LAGS = (1, 2, 3, 5, 7)
LINE_LAG = 3
D_SLOTS = 4
VMEM_BYTES = 63 * 2**20
FIRST_AHEAD = 0
DIRECT = 3
SKIP = 1000
AG_LAGS = (1, 2, 3)
LATE_TICK = 10
LATE_STEP = 2
LINE = 4
QKV_GROUPS = 4
OUT_GROUPS = 2
OUT_START = 12
FF_START = 16


def bucket_limits(tok_count):
    buckets = relative_buckets(tok_count, BUCKETS)[:, 0]
    return [int(np.argmax(buckets >= k)) for k in range(1, BUCKETS // 2)]


def dot(a, b):
    return lax.dot_general(a, b, (((1,), (0,)), ((), ())), preferred_element_type=jnp.float32)


def dot_nt(a, b):
    return lax.dot_general(a, b, (((1,), (1,)), ((), ())), preferred_element_type=jnp.float32)


def split_dot(a, b):
    high = a.astype(jnp.bfloat16)
    rest = (a - high.astype(jnp.float32)).astype(jnp.bfloat16)
    return dot(high, b) + dot(rest, b)


def iota(shape, dim):
    return lax.broadcasted_iota(jnp.int32, shape, dim)


def layer_kernel(
    sizes,
    page_ref,
    pos_ref,
    small_ref,
    tok_hbm,
    cot_hbm,
    attn_hbm,
    ffin_hbm,
    down_hbm,
    out_hbm,
    gtok_hbm,
    own_hbm,
    osmall_ref,
    norm_ref,
    w,
    rh,
    rd,
    re,
    rf,
    rbz,
    rbd,
    rbe,
    own,
    mix,
    smb,
    sgr,
    sgz,
    nbr,
    nbz,
    tok,
    n1,
    n1t,
    qp,
    kp,
    vp,
    ctx,
    ctxt,
    res,
    n2,
    n2t,
    gout,
    goutt,
    gn,
    kxs,
    km,
    gv,
    lse,
    ggx,
    ggy,
    acc,
    hx,
    hxx,
    hq2,
    k2,
    hxt,
    hyt,
    dq,
    dk,
    dv,
    gains,
    gsum,
    load_sem,
    in_sem,
    ag_send,
    ag_recv,
    late_send,
    late_recv,
    bl_send,
    bl_recv,
    rs_send,
    rs_recv,
    sm_send,
    sm_recv,
):
    ny, nz, nx, per, ff_groups = sizes
    f32, bf16 = jnp.float32, jnp.bfloat16
    groups = QKV_GROUPS + OUT_GROUPS + ff_groups
    tok_count, width = tok.shape
    rows = w.shape[5]
    dp, fs = lax.axis_index("dp"), lax.axis_index("fsdp")
    y, c, z, x = dp // 2, dp % 2, fs // nx, fs % nx

    def device(yy, cc, zz, xx):
        return (yy * 2 + cc, zz * nx + xx)

    sib, xnb, ynb = device(y, 1 - c, z, x), device(y, c, z, 1 - x), device(1 - y, c, z, x)

    def zdev(k):
        return device(y, c, lax.rem(z + k, nz), x)

    inner = jnp.logical_and(z > 0, z < LINE - 1)
    across = lax.rem(z + 2, LINE)
    edge = jnp.where(z < 2, 0, LINE - 1)
    inward = jnp.where(z < 2, 1, LINE - 2)
    far_end = LINE - 1 - edge
    dev_up, dev_down = device(y, c, jnp.minimum(z + 1, LINE - 1), x), device(y, c, jnp.maximum(z - 1, 0), x)
    dev_across, dev_edge, dev_inward, dev_far = (
        device(y, c, at, x) for at in (across, edge, inward, far_end)
    )

    def to_sides(send_up, send_down):
        pl.when(z < LINE - 1)(send_up)
        pl.when(z > 0)(send_down)

    def remote(src, dst, send, recv, dev):
        return pltpu.make_async_remote_copy(
            src_ref=src, dst_ref=dst, send_sem=send, recv_sem=recv, device_id=dev, device_id_type=MESH
        )

    cube = [(a, b, d) for a in range(ny) for b in range(2) for d in range(nx)][1:]

    def cube_dev(step):
        return device(*(1 - at if turn else at for at, turn in zip((y, c), step)), z, 1 - x if step[2] else x)

    near = (y * 2 + c) * nx + x

    barrier = pltpu.get_barrier_semaphore()
    for dev in [cube_dev(step) for step in cube] + [zdev(k) for k in range(1, nz)]:
        pl.semaphore_signal(barrier, inc=1, device_id=dev, device_id_type=MESH)

    def on_group(g, fn):
        if isinstance(g, int):
            if 0 <= g < groups:
                if g < QKV_GROUPS:
                    fn(3 * g, 3, g)
                elif g < QKV_GROUPS + OUT_GROUPS:
                    fn(OUT_START + 2 * (g - QKV_GROUPS), 2, g)
                else:
                    fn(FF_START + 3 * (g - QKV_GROUPS - OUT_GROUPS), 3, g)
            return
        is_out = jnp.logical_and(g >= QKV_GROUPS, g < QKV_GROUPS + OUT_GROUPS)
        inside = jnp.logical_and(g >= 0, g < groups)

        @pl.when(is_out)
        def _():
            fn(OUT_START + 2 * (g - QKV_GROUPS), 2, g)

        @pl.when(jnp.logical_and(inside, jnp.logical_not(is_out)))
        def _():
            fn(jnp.where(g < QKV_GROUPS, 3 * g, FF_START + 3 * (g - QKV_GROUPS - OUT_GROUPS)), 3, g)

    def load(g):
        def go(t0, count, g):
            if count == 2:
                for i in range(2):
                    cols = pl.ds(pl.multiple_of((t0 - OUT_START + i) * TILE, TILE), TILE)
                    pltpu.make_async_copy(attn_hbm.at[3, :, cols], own.at[t0 + i], load_sem.at[g]).start()
            elif isinstance(g, int) and g < QKV_GROUPS:
                cols = pl.ds(g * TILE, TILE)
                pltpu.make_async_copy(
                    attn_hbm.at[pl.ds(0, 3), :, cols], own.at[pl.ds(t0, 3)], load_sem.at[g]
                ).start()
            else:
                cols = pl.ds((g - QKV_GROUPS - OUT_GROUPS) * TILE, TILE)
                pltpu.make_async_copy(
                    ffin_hbm.at[:, :, cols], own.at[pl.ds(t0, 2)], load_sem.at[g]
                ).start()
                pltpu.make_async_copy(down_hbm.at[:, cols], own.at[t0 + 2], load_sem.at[g]).start()

        on_group(g, go)

    def load_wait(g):
        def go(t0, count, g):
            tiles = own.at[pl.ds(t0, count)]
            pltpu.make_async_copy(tiles, tiles, load_sem.at[g]).wait()
            for i in range(count):
                w[t0 + i, y, c, z, x] = own[t0 + i].astype(bf16)

        on_group(g, go)

    for g in range(groups):
        load(g)
    tok_copy = pltpu.make_async_copy(tok_hbm, tok, in_sem.at[0])
    cot_copy = pltpu.make_async_copy(cot_hbm, gout, in_sem.at[1])
    tok_copy.start()
    cot_copy.start()

    def ag_parts(t0, count, g):
        t = pl.ds(t0, count)
        return t, (lambda i: ag_send.at[i, g]), (lambda i: ag_recv.at[i, g])

    late_start = groups - LATE_GROUPS

    def on_early(g, fn):
        if isinstance(g, int):
            if g < late_start:
                on_group(g, fn)
        else:
            on_group(jnp.where(g < late_start, g, -1), fn)

    def on_late(g, fn):
        if isinstance(g, int):
            if late_start <= g < groups:
                on_group(g, fn)
        else:

            @pl.when(jnp.logical_and(g >= late_start, g < groups))
            def _():
                fn(FF_START + 3 * (g - QKV_GROUPS - OUT_GROUPS), 3, g)

    def late1(g):
        def go(t0, count, g):
            t, s, r = ag_parts(t0, count, g)
            mine = w.at[t, y, c, z, x]
            remote(mine, mine, s(1), r(1), xnb).start()
            remote(mine, mine, s(2), r(2), ynb).start()

        on_late(g, go)

    def late2(g):
        def go(t0, count, g):
            t, s, r = ag_parts(t0, count, g)
            xpart = w.at[t, y, c, z, 1 - x]
            ypart = w.at[t, 1 - y, c, z, x]
            remote(xpart, xpart, s(1), r(1), xnb).wait_recv()
            remote(ypart, ypart, s(2), r(2), ynb).wait_recv()
            xhalf = w.at[t, y, c, z, 1 - x, pl.ds(0, HALF)]
            yhalf = w.at[t, 1 - y, c, z, x, pl.ds(HALF, HALF)]
            remote(xhalf, xhalf, s(4), r(4), ynb).start()
            remote(yhalf, yhalf, s(3), r(3), xnb).start()

        on_late(g, go)

    def late3(g):
        def go(t0, count, g):
            t, s, r = ag_parts(t0, count, g)
            low = w.at[t, 1 - y, c, z, 1 - x, pl.ds(0, HALF)]
            high = w.at[t, 1 - y, c, z, 1 - x, pl.ds(HALF, HALF)]
            remote(low, low, s(4), r(4), ynb).wait_recv()
            remote(high, high, s(3), r(3), xnb).wait_recv()

        on_late(g, go)

    def late_tile(b):
        return FF_START + 3 * (ff_groups - LATE_GROUPS) + b

    def late_line(b):
        square = w.at[late_tile(b), :, c, z]
        s, r = late_send, late_recv
        to_sides(
            lambda: remote(square, square, s.at[0, b], r.at[0, b], dev_up).start(),
            lambda: remote(square, square, s.at[0, b], r.at[0, b], dev_down).start(),
        )
        remote(square, square, s.at[1, b], r.at[1, b], dev_across).start()

    def late_relay(b):
        landed = w.at[late_tile(b), :, c, across]
        s, r = late_send, late_recv
        remote(landed, landed, s.at[1, b], r.at[1, b], dev_across).wait_recv()

        @pl.when(inner)
        def _():
            remote(landed, landed, s.at[0, b], r.at[0, b], dev_edge).start()

    def late_step(t, fn):
        if isinstance(t, int):
            if 1 <= t <= 3 * LATE_GROUPS:
                fn(t - 1)
        else:

            @pl.when(jnp.logical_and(t >= 1, t <= 3 * LATE_GROUPS))
            def _():
                fn(t - 1)

    def late4(g):
        def go(t0, count, g):
            t, s, r = ag_parts(t0, count, g)
            for i in range(3):
                b = t0 + i - late_tile(0)
                two = w.at[t0 + i, :, c, pl.ds(0, 2)]
                remote(two, two, late_send.at[0, b], late_recv.at[0, b], dev_across).wait_recv()
            plane = w.at[t, :, c]
            remote(plane, plane, s(5), r(5), sib).start()

        on_late(g, go)

    def ag1(g):
        def go(t0, count, g):
            t, s, r = ag_parts(t0, count, g)
            mine = w.at[t, y, c, z, x]
            to_sides(
                lambda: remote(mine, mine, s(0), r(0), dev_up).start(),
                lambda: remote(mine, mine, s(0), r(0), dev_down).start(),
            )
            remote(mine, mine, s(6), r(6), dev_across).start()

        on_early(g, go)

    def ag1_relay(g):
        def go(t0, count, g):
            t, s, r = ag_parts(t0, count, g)
            landed = w.at[t, y, c, across, x]
            remote(landed, landed, s(6), r(6), dev_across).wait_recv()

            @pl.when(inner)
            def _():
                remote(landed, landed, s(0), r(0), dev_edge).start()

        on_early(g, go)

    def ag2(g):
        def go(t0, count, g):
            t, s, r = ag_parts(t0, count, g)
            two = w.at[t, y, c, pl.ds(0, 2), x]
            remote(two, two, s(0), r(0), dev_across).wait_recv()
            column = w.at[t, y, c, :, x]
            remote(column, column, s(1), r(1), xnb).start()
            remote(column, column, s(2), r(2), ynb).start()
            remote(column, column, s(5), r(5), sib).start()

        on_early(g, go)

    def ag3(g):
        def go(t0, count, g):
            t, s, r = ag_parts(t0, count, g)
            xcol = w.at[t, y, c, :, 1 - x]
            ycol = w.at[t, 1 - y, c, :, x]
            remote(xcol, xcol, s(1), r(1), xnb).wait_recv()
            xhalf = w.at[t, y, c, :, 1 - x, pl.ds(0, HALF)]
            remote(xhalf, xhalf, s(4), r(4), ynb).start()
            remote(xcol, xcol, s(5), r(5), sib).start()
            remote(ycol, ycol, s(2), r(2), ynb).wait_recv()
            yhalf = w.at[t, 1 - y, c, :, x, pl.ds(HALF, HALF)]
            remote(yhalf, yhalf, s(3), r(3), xnb).start()
            remote(ycol, ycol, s(5), r(5), sib).start()

        on_early(g, go)

    def ag4(g):
        def go(t0, count, g):
            t, s, r = ag_parts(t0, count, g)
            low = w.at[t, 1 - y, c, :, 1 - x, pl.ds(0, HALF)]
            high = w.at[t, 1 - y, c, :, 1 - x, pl.ds(HALF, HALF)]
            remote(low, low, s(4), r(4), ynb).wait_recv()
            remote(high, high, s(3), r(3), xnb).wait_recv()
            diag = w.at[t, 1 - y, c, :, 1 - x]
            remote(diag, diag, s(5), r(5), sib).start()

        on_early(g, go)

    def ag5(g):
        def go(t0, count, g):
            t, s, r = ag_parts(t0, count, g)
            plane = w.at[t, :, 1 - c]
            remote(plane, plane, s(5), r(5), sib).wait_recv()

        on_group(g, go)

    def ag_sent(g):
        def go(t0, count, g):
            t, s, r = ag_parts(t0, count, g)
            one = w.at[t, y, c, z, x]
            column = w.at[t, y, c, :, x]
            half = w.at[t, y, c, :, x, pl.ds(0, HALF)]
            plane = w.at[t, :, c]
            for i, part in ((1, column), (2, column), (3, half), (4, half), (5, plane), (6, one)):
                remote(part, part, s(i), r(i), sib).wait_send()
            sent_sides(w.at[t, y, c, pl.ds(0, 3), x], one, s(0), r(0))

        on_early(g, go)

        def go_late(t0, count, g):
            t, s, r = ag_parts(t0, count, g)
            one = w.at[t, y, c, z, x]
            half = w.at[t, y, c, z, x, pl.ds(0, HALF)]
            plane = w.at[t, :, c]
            for i, part in ((1, one), (2, one), (3, half), (4, half), (5, plane)):
                remote(part, part, s(i), r(i), sib).wait_send()
            for i in range(3):
                b = t0 + i - late_tile(0)
                square = w.at[t0 + i, :, c, z]
                remote(square, square, late_send.at[1, b], late_recv.at[1, b], sib).wait_send()
                sent_sides(
                    w.at[t0 + i, :, c, pl.ds(0, 3)], square, late_send.at[0, b], late_recv.at[0, b]
                )

        on_late(g, go_late)

    def sent_sides(three, one, s, r):
        @pl.when(inner)
        def _():
            remote(three, three, s, r, sib).wait_send()

        @pl.when(jnp.logical_not(inner))
        def _():
            remote(one, one, s, r, sib).wait_send()

    def ag_front(t):
        ag1(t + AHEAD)
        ag1_relay(t + FIRST_AHEAD + 1)
        ag2(t + FIRST_AHEAD)
        late_step(t, late_line)
        ag3(t - AG_LAGS[0])

    def ag_back(t):
        late_step(t - 3, late_relay)
        ag4(t - AG_LAGS[1])
        late4(late_start + t - LATE_TICK)
        ag5(jnp.where(t - AG_LAGS[2] < late_start, t - AG_LAGS[2], -1) if not isinstance(t, int) else (t - AG_LAGS[2] if t - AG_LAGS[2] < late_start else -1))

    early_ff = ff_groups - LATE_GROUPS

    def ff_step(s):
        over = s - LATE_STEP
        if isinstance(s, int):
            if over < 0 or over >= 2 * LATE_GROUPS:
                before = s if over < 0 else s - LATE_GROUPS
                return before, False, before
            late = over % 2 == 0
            before = LATE_STEP + over // 2
            return (early_ff + over // 2 if late else before), late, before
        inside = jnp.logical_and(over >= 0, over < 2 * LATE_GROUPS)
        late = jnp.logical_and(inside, lax.rem(over + 2 * LATE_GROUPS, 2) == 0)
        before = jnp.where(over < 0, s, jnp.where(inside, LATE_STEP + over // 2, s - LATE_GROUPS))
        return jnp.where(late, early_ff + over // 2, before), late, before

    def rs_group(n):
        if isinstance(n, int):
            if n < 0 or n >= groups:
                return -1
            tail = n - ff_groups
            if tail < 0:
                return QKV_GROUPS + OUT_GROUPS + ff_step(n)[0]
            return QKV_GROUPS + tail if tail < OUT_GROUPS else tail - OUT_GROUPS
        tail = n - ff_groups
        g = jnp.where(
            tail < 0,
            QKV_GROUPS + OUT_GROUPS + ff_step(n)[0],
            jnp.where(tail < OUT_GROUPS, QKV_GROUPS + tail, tail - OUT_GROUPS),
        )
        return jnp.where(jnp.logical_or(n < 0, n >= groups), -1, g)

    def z_first(n):
        if isinstance(n, int):
            return n in Z_FIRST_SUMS
        return functools.reduce(jnp.logical_or, [n == m for m in Z_FIRST_SUMS])

    def on_sum(n, fn, kind=None):
        which = z_first(n)
        if isinstance(n, int):
            if kind is not None and which != kind:
                return
            slots = (n % SLOTS, n % Z_SLOTS, sum(n > m for m in Z_FIRST_SUMS), n % D_SLOTS)
            g = rs_group(n)
        else:
            bank = sum((n > m).astype(jnp.int32) for m in Z_FIRST_SUMS)
            slots = tuple(lax.rem(n + 10 * k, k) for k in (SLOTS, Z_SLOTS)) + (bank, lax.rem(n + 10 * D_SLOTS, D_SLOTS))
            g = rs_group(n)
            if kind is not None:
                g = jnp.where(which if kind else jnp.logical_not(which), g, -1)

        def go(t0, count, g):
            fn(t0, count, slots, (lambda i: rs_send.at[i, g]), (lambda i: rs_recv.at[i, g]))

        if kind:
            if isinstance(n, int):
                on_group(g, go)
            else:

                @pl.when(g >= 0)
                def _():
                    go(FF_START + 3 * (g - QKV_GROUPS - OUT_GROUPS), 3, g)

        else:
            on_group(g, go)

    def rs0(n):
        def go(t0, count, slots, s, r):
            slot = slots[0]
            remote(
                w.at[pl.ds(t0, count), :, 1 - c], rh.at[slot, pl.ds(0, count)], s(0), r(0), sib
            ).start()

        on_sum(n, go)

    def rs1(n):
        def go(t0, count, slots, s, r):
            slot = slots[0]
            t = pl.ds(t0, count)
            landed = rh.at[slot, pl.ds(0, count)]
            remote(w.at[t, :, 1 - c], landed, s(0), r(0), sib).wait_recv()

            def add(i, carry):
                for yy in range(ny):
                    w[t0 + i, yy, c] = w[t0 + i, yy, c] + rh[slot, i, yy]
                return carry

            lax.fori_loop(0, count, add, 0)

        on_sum(n, go)

        def go_early(t0, count, slots, s, r):
            for k, dev in ((0, xnb), (1, ynb)):
                remote(
                    w.at[pl.ds(t0, count), 1 - y, c, :, 1 - x, pl.ds(k * HALF, HALF)],
                    rd.at[slots[3], k, pl.ds(0, count)],
                    s(1 + k),
                    r(1 + k),
                    dev,
                ).start()

        on_sum(n, go_early, False)

    def rs1_line(n, i):
        def go_line(t0, count, slots, s, r):
            bank = slots[2]
            sems = line_sems(bank, i)
            line_sends(lambda at: w.at[t0 + i, :, c, at], lambda kind: rbz.at[bank, kind, i], *sems)

        on_sum(n, go_line, True)

    def line_sems(bank, i):
        return (lambda kind: bl_send.at[kind - 5, 3 * bank + i]), (lambda kind: bl_recv.at[kind - 5, 3 * bank + i])

    def line_sends(part, landed, s, r):
        to_sides(
            lambda: remote(part(dev_at(z + 1)), landed(0), s(5), r(5), dev_up).start(),
            lambda: remote(part(dev_at(z - 1)), landed(1), s(6), r(6), dev_down).start(),
        )

        @pl.when(jnp.logical_not(inner))
        def _():
            remote(part(across), landed(2), s(7), r(7), dev_across).start()
            remote(part(far_end), landed(3), s(8), r(8), dev_inward).start()

    def dev_at(at):
        return jnp.clip(at, 0, LINE - 1)

    def line_direct(part, landed, s, r):
        to_sides(
            lambda: remote(part(dev_at(z + 1)), landed(0), s(5), r(5), dev_up).start(),
            lambda: remote(part(dev_at(z - 1)), landed(1), s(6), r(6), dev_down).start(),
        )
        remote(part(across), landed(2), s(7), r(7), dev_across).start()

        @pl.when(jnp.logical_not(inner))
        def _():
            remote(part(far_end), landed(3), s(8), r(8), dev_far).start()

    def is_direct(n):
        return isinstance(n, int) and n >= groups - DIRECT

    def line_merge(part, landed, s, r, add):
        @pl.when(inner)
        def _():
            remote(part(across), landed(3), s(8), r(8), dev_edge).wait_recv()
            add()
            remote(part(across), landed(2), s(7), r(7), dev_across).start()

    def line_wait(part, landed, s, r, add):
        @pl.when(z > 0)
        def _():
            remote(part(z), landed(0), s(5), r(5), dev_down).wait_recv()
            add(0)

        @pl.when(z < LINE - 1)
        def _():
            remote(part(z), landed(1), s(6), r(6), dev_up).wait_recv()
            add(1)

        remote(part(z), landed(2), s(7), r(7), dev_across).wait_recv()
        add(2)

    def line_sent(part, s, r):
        pl.when(z < LINE - 1)(lambda: remote(part, part, s(5), r(5), sib).wait_send())
        pl.when(z > 0)(lambda: remote(part, part, s(6), r(6), sib).wait_send())
        remote(part, part, s(7), r(7), sib).wait_send()
        pl.when(jnp.logical_not(inner))(lambda: remote(part, part, s(8), r(8), sib).wait_send())

    def rs_merge(n):
        if is_direct(n):
            return

        def go(t0, count, slots, s, r):
            t = pl.ds(t0, count)

            def add():
                for i in range(count):
                    w[t0 + i, y, c, across, x] = w[t0 + i, y, c, across, x] + rf[slots[1], 3, i]

            line_merge(
                lambda at: w.at[t, y, c, at, x], lambda kind: rf.at[slots[1], kind, pl.ds(0, count)], s, r, add
            )

        on_sum(n, go, False)

    def rs_line_merge(n, i):
        def go(t0, count, slots, s, r):
            bank = slots[2]

            def add():
                for yy in range(ny):
                    w[t0 + i, yy, c, across] = w[t0 + i, yy, c, across] + rbz[bank, 3, i, yy]

            sems = line_sems(bank, i)
            line_merge(lambda at: w.at[t0 + i, :, c, at], lambda kind: rbz.at[bank, kind, i], *sems, add)

        on_sum(n, go, True)

    def rs2(n):
        def go(t0, count, slots, s, r):
            slot = slots[3]
            t = pl.ds(t0, count)
            for k, dev, yy, xx in ((0, xnb, 1 - y, x), (1, ynb, y, 1 - x)):
                landed = rd.at[slot, k, pl.ds(0, count)]
                rows_k = pl.ds(k * HALF, HALF)
                remote(w.at[t, 1 - y, c, :, 1 - x, rows_k], landed, s(1 + k), r(1 + k), dev).wait_recv()
                for i in range(count):
                    w[t0 + i, yy, c, :, xx, rows_k] = w[t0 + i, yy, c, :, xx, rows_k] + rd[slot, k, i]
            for k, dev, yy, xx in ((0, xnb, y, 1 - x), (1, ynb, 1 - y, x)):
                remote(
                    w.at[t, yy, c, :, xx], re.at[slot, k, pl.ds(0, count)], s(3 + k), r(3 + k), dev
                ).start()

        on_sum(n, go, False)

    def rs2_line(n):
        def go_line(t0, count, slots, s, r):
            t = pl.ds(t0, count)
            bank = slots[2]
            for i in range(count):

                def add(kind, i=i):
                    for yy in range(ny):
                        w[t0 + i, yy, c, z] = w[t0 + i, yy, c, z] + rbz[bank, kind, i, yy]

                line_wait(
                    lambda at, i=i: w.at[t0 + i, :, c, at],
                    lambda kind, i=i: rbz.at[bank, kind, i],
                    *line_sems(bank, i),
                    add,
                )
            for k, dev in ((0, xnb), (1, ynb)):
                remote(
                    w.at[t, 1 - y, c, z, 1 - x, pl.ds(k * HALF, HALF)],
                    rbd.at[slots[2], k],
                    s(1 + k),
                    r(1 + k),
                    dev,
                ).start()

        on_sum(n, go_line, True)

    def rs3(n):
        def go(t0, count, slots, s, r):
            slot = slots[3]
            t = pl.ds(t0, count)
            for k, dev in ((0, xnb), (1, ynb)):
                landed = re.at[slot, k, pl.ds(0, count)]
                remote(w.at[t, y, c, :, x], landed, s(3 + k), r(3 + k), dev).wait_recv()
            for i in range(count):
                total = (
                    w[t0 + i, y, c, z, x].astype(f32)
                    + re[slot, 0, i, z].astype(f32)
                    + re[slot, 1, i, z].astype(f32)
                )
                own[t0 + i] = total
                for zz in range(nz):
                    w[t0 + i, y, c, zz, x] = (
                        w[t0 + i, y, c, zz, x].astype(f32)
                        + re[slot, 0, i, zz].astype(f32)
                        + re[slot, 1, i, zz].astype(f32)
                    ).astype(bf16)
            (line_direct if is_direct(n) else line_sends)(
                lambda at: w.at[t, y, c, at, x], lambda kind: rf.at[slots[1], kind, pl.ds(0, count)], s, r
            )

        on_sum(n, go, False)

    def rs3_line(n):
        def go_line(t0, count, slots, s, r):
            t = pl.ds(t0, count)
            for k, dev, yy, xx in ((0, xnb, 1 - y, x), (1, ynb, y, 1 - x)):
                landed = rbd.at[slots[2], k]
                rows_k = pl.ds(k * HALF, HALF)
                remote(w.at[t, 1 - y, c, z, 1 - x, rows_k], landed, s(1 + k), r(1 + k), dev).wait_recv()
                for i in range(count):
                    w[t0 + i, yy, c, z, xx, rows_k] = w[t0 + i, yy, c, z, xx, rows_k] + rbd[slots[2], k, i]
            for k, dev, yy, xx in ((0, xnb, y, 1 - x), (1, ynb, 1 - y, x)):
                remote(w.at[t, yy, c, z, xx], rbe.at[slots[2], k], s(3 + k), r(3 + k), dev).start()

        on_sum(n, go_line, True)

    def rs4(n):
        def go(t0, count, slots, s, r):
            t = pl.ds(t0, count)

            def add(kind):
                for i in range(count):
                    own[t0 + i] += rf[slots[1], kind, i].astype(f32)

            line_wait(
                lambda at: w.at[t, y, c, at, x], lambda kind: rf.at[slots[1], kind, pl.ds(0, count)], s, r, add
            )
            if is_direct(n):

                @pl.when(jnp.logical_not(inner))
                def _():
                    landed = rf.at[slots[1], 3, pl.ds(0, count)]
                    remote(w.at[t, y, c, z, x], landed, s(8), r(8), dev_far).wait_recv()
                    add(3)

        on_sum(n, go, False)

    def rs4_line(n):
        def go_line(t0, count, slots, s, r):
            for k, dev in ((0, xnb), (1, ynb)):
                landed = rbe.at[slots[2], k]
                remote(landed, landed, s(3 + k), r(3 + k), dev).wait_recv()
            for i in range(count):
                own[t0 + i] = (
                    w[t0 + i, y, c, z, x].astype(f32)
                    + rbe[slots[2], 0, i].astype(f32)
                    + rbe[slots[2], 1, i].astype(f32)
                )

        on_sum(n, go_line, True)

    def rs_sent(n):
        def go(t0, count, slots, s, r):
            t = pl.ds(t0, count)
            plane = w.at[t, :, c]
            half = w.at[t, y, c, :, x, pl.ds(0, HALF)]
            column = w.at[t, y, c, :, x]
            for i, part in enumerate((plane, half, half, column, column)):
                remote(part, part, s(i), r(i), sib).wait_send()
            line_sent(w.at[t, y, c, z, x], s, r)

        on_sum(n, go, False)

        def go_line(t0, count, slots, s, r):
            t = pl.ds(t0, count)
            plane = w.at[t, :, c]
            half = w.at[t, y, c, z, x, pl.ds(0, HALF)]
            one = w.at[t, y, c, z, x]
            for i, part in enumerate((plane, half, half, one, one)):
                remote(part, part, s(i), r(i), sib).wait_send()
            for i in range(count):
                line_sent(w.at[t0 + i, :, c, z], *line_sems(slots[2], i))

        on_sum(n, go_line, True)

    def rs_front(n):
        rs0(n)
        rs1(n - LAGS[0])
        for i in range(3):
            rs1_line(n - LAGS[0] - i, i)
        rs2(n - LAGS[1])

    def rs_back(n):
        rs3(n - LAGS[2])
        for i in range(3):
            rs_line_merge(n - LAGS[0] - LINE_LAG - i, i)
        rs_merge(n - LAGS[3])
        rs4(n - LAGS[4])
        rs2_line(n - LAGS[0] - 2 * LINE_LAG - 2)
        rs3_line(n - LAGS[0] - 2 * LINE_LAG - 3)
        rs4_line(n - LAGS[0] - 2 * LINE_LAG - 4)

    def rs_tick(n):
        rs_front(n)
        rs_back(n)

    def cast_wait(copy):
        copy.wait_send()
        copy.wait_recv()

    def sm_start(i):
        if i == 0:
            part = smb.at[near, z]
            for k in range(1, nz):
                remote(part, part, sm_send.at[0], sm_recv.at[0], zdev(k)).start()
        else:
            part = smb.at[near]
            for step in cube:
                remote(part, part, sm_send.at[1], sm_recv.at[1], cube_dev(step)).start()

    def sm_wait(i):
        part = smb.at[near, pl.ds(0, nz - 1)] if i == 0 else smb.at[pl.ds(0, len(cube))]
        cast_wait(remote(part, part, sm_send.at[i], sm_recv.at[i], sib))

    smb[near, z] = jnp.zeros(smb.shape[2:], f32)
    smb[near, z, 0:1, 0:per] = small_ref[...].astype(bf16).astype(f32)
    load_wait(0)
    pl.semaphore_wait(barrier, len(cube) + nz - 1)
    ag1(0)
    sm_start(0)
    for g in range(1, AHEAD):
        load_wait(g)
        ag1(g)
    for g in range(late_start, groups):
        load_wait(g)
        late1(g)
    load_wait(AHEAD)

    lane = iota((tok_count, 128), 1)
    row = iota((tok_count, 128), 0)
    first_len = page_ref[:, 0:1]
    both_len = first_len + page_ref[:, 1:2]

    def pos_rows(k):
        line = pos_ref[k : k + 1, :].astype(f32)
        return jnp.broadcast_to(line, (128, tok_count)).T.astype(jnp.int32)

    pos_x, pos_y = pos_rows(0), pos_rows(1)
    hot_x = (pos_x == lane).astype(f32)
    hot_y = (pos_y == lane).astype(f32)
    page = jnp.where(row < first_len, 0, jnp.where(row < both_len, 1, 2))
    hx[...] = hot_x.astype(bf16)
    hxx[...] = (pos_x == lax.rem(lane, 64)).astype(f32).astype(bf16)
    hq2[...] = jnp.where(lane < 64, hot_y, (page == lane - 64).astype(f32)).astype(bf16)
    barred = jnp.where(jnp.logical_and(page == lane - 64, page < 2), 0.0, far_negative)
    k2[...] = jnp.where(lane < 64, hot_y, jnp.where(lane < 67, barred, 0.0)).astype(bf16)
    hxt[...] = hot_x.T[0:64].astype(bf16)
    hyt[...] = hot_y.T[0:64].astype(bf16)
    for g in range(FIRST_AHEAD + 1):
        ag1_relay(g)
        if g < FIRST_AHEAD:
            ag2(g)
    ag_front(0)
    ag_back(0)
    sm_wait(0)
    sm_start(1)
    for g in range(late_start, groups):
        late2(g)
    for g in range(AHEAD + 1, late_start):
        load_wait(g)
    cot_copy.wait()

    def mask_out(i, carry):
        at = pl.ds(pl.multiple_of(i * 128, 128), 128)
        valid = (iota((128, width), 0) + i * 128 < both_len).astype(f32)
        masked = valid * gout[at, :].astype(f32)
        gout[at, :] = masked.astype(bf16)
        goutt[:, at] = masked.T.astype(bf16)
        return carry

    lax.fori_loop(0, tok_count // 128, mask_out, 0)
    for g in range(late_start, groups):
        late3(g)
    ag_front(1)
    ag_back(1)
    sm_wait(1)

    devs = [(a, b, d, e) for a in range(ny) for b in range(2) for d in range(nz) for e in range(nx)]
    lane1 = iota((1, 128), 1)

    def flat_tile(n):
        tile = jnp.zeros((1, 128), f32)
        for d in range(128 * n // per, (128 * n + 127) // per + 1):
            shift = d * per - 128 * n
            a, b, at_z, at_x = devs[d]
            line = smb[(a * 2 + b) * nx + at_x, at_z, 0:1, :]
            line = pltpu.roll(line, shift % 128, 1)
            inside = jnp.logical_and(lane1 >= shift, lane1 < shift + per)
            tile = jnp.where(inside, line, tile)
        return tile

    for n in range(2 * width // 128):
        gains[n // (width // 128), :, pl.ds(128 * (n % (width // 128)), 128)] = flat_tile(n)
    first_table = 2 * width // 128

    def table(k):
        flat = jnp.concatenate([flat_tile(first_table + 4 * k + i) for i in range(4)], axis=1)
        keep = lax.rem(iota((HEADS, 512), 1), HEADS) == iota((HEADS, 512), 0)
        return jnp.where(keep, jnp.broadcast_to(flat, (HEADS, 512)), 0.0).astype(bf16)

    def hot(bucket_line, count):
        return (iota((512, count), 0) // HEADS == bucket_line).astype(f32).astype(bf16)

    limits = bucket_limits(tok_count)
    span = 2 * tok_count

    def rel_bucket(offset):
        distance = jnp.abs(offset)
        bucket = jnp.where(offset > 0, BUCKETS // 2, 0)
        for limit in limits:
            bucket = bucket + (distance >= limit).astype(jnp.int32)
        return bucket

    def layout_bucket(offset):
        return jnp.clip(offset, -(BUCKETS // 2), BUCKETS // 2 - 1) + BUCKETS // 2

    rel_values = dot(table(0), hot(rel_bucket(tok_count - iota((1, span), 1)), span))
    for h in range(HEADS):
        gv[h, 0:1, :] = rel_values[h : h + 1]
    turned = jnp.where(lane1 < 64, lane1, lane1 - 128)
    x_even = dot(table(1), hot(layout_bucket(lane1 - 64), 128))
    x_odd = dot(table(1), hot(layout_bucket(turned), 128))
    y_any = dot(table(2), hot(layout_bucket(turned), 128))
    sq_lane, sq_row = iota((128, 128), 1), iota((128, 128), 0)

    def slope(line):
        return pltpu.roll(jnp.broadcast_to(line, (128, line.shape[1])), 0, 1, stride=1, stride_axis=0)

    for p in range(HEADS // 2):
        a, b = 2 * p, 2 * p + 1
        both = jnp.where(sq_lane < 64, slope(x_odd[b : b + 1]), slope(x_even[a : a + 1]))
        kxs[p] = jnp.where(sq_row < 64, both, 0.0).astype(bf16)
        for h in (a, b):
            part = jnp.where(sq_lane < 64, slope(y_any[h : h + 1]), 0.0)
            km[h] = jnp.where(sq_row < 64, part, (sq_lane == sq_row).astype(f32)).astype(bf16)

    tok_copy.wait()

    def norm_one(i, carry):
        at = pl.ds(pl.multiple_of(i * 128, 128), 128)
        stream = tok[at, :].astype(f32)
        scale = lax.rsqrt(jnp.mean(stream * stream, axis=-1, keepdims=True) + norm_eps)
        low = (stream * scale * gains[0]).astype(bf16)
        n1[at, :] = low
        n1t[:, at] = low.astype(f32).T.astype(bf16)
        return carry

    lax.fori_loop(0, tok_count // 128, norm_one, 0)
    for t in range(2, AG_LAGS[2]):
        ag_front(t)
        ag_back(t)
    ag_front(AG_LAGS[2])

    def tile_of(t):
        return w[t].reshape(width, TILE)

    half_lane = iota((tok_count, 128), 1) < 64

    def pick(low, high):
        return jnp.where(half_lane, low.astype(f32), high.astype(f32)).astype(bf16)

    def augmented(p, e):
        shift = dot(hx[...], kxs[p])
        q_own, k_own = qp[p], kp[p]
        q_first = pick(q_own, shift) if e == 0 else pick(shift, q_own)
        k_first = pick(k_own, hxx[...]) if e == 0 else pick(hxx[...], k_own)
        q_second = dot(hq2[...], km[2 * p + e]).astype(bf16)
        return (
            jnp.concatenate([q_first, q_second], axis=1),
            jnp.concatenate([k_first, k2[...]], axis=1),
        )

    blocks = tok_count // 128
    half_rows = tok_count // 2

    def rel_bias(steep, part):
        return jnp.concatenate(
            [
                steep[:, tok_count - 128 * jb + half_rows * part : tok_count - 128 * jb + half_rows * (part + 1)]
                for jb in range(blocks)
            ],
            axis=0,
        )

    def forward_pair(p):
        v_turned = vp[p].astype(f32).T.astype(bf16)
        pieces = []
        for e in range(2):
            q_all, k_all = augmented(p, e)
            steep = slope(gv[2 * p + e, 0:1, :])
            parts = []
            for part in range(2):
                cols = slice(half_rows * part, half_rows * (part + 1))
                scores = dot_nt(k_all, q_all[cols]) + rel_bias(steep, part)
                top = jnp.max(scores, axis=0, keepdims=True)
                exponent = jnp.exp(scores - top)
                total = jnp.sum(exponent, axis=0, keepdims=True)
                probs = (exponent * (1.0 / total)).astype(bf16)
                lse[2 * p + e, 0:1, cols] = top + jnp.log(total)
                parts.append(dot(v_turned[64 * e : 64 * (e + 1)], probs))
            pieces.append(jnp.concatenate(parts, axis=1))
        turned = jnp.concatenate(pieces, axis=0)
        at = pl.ds(pl.multiple_of(p * 128, 128), 128)
        ctxt[at, :] = turned.astype(bf16)
        ctx[:, at] = turned.T.astype(bf16)

    def project(j):
        for i, dest in enumerate((qp, kp, vp)):
            result = dot(n1[...], tile_of(3 * j + i)).astype(bf16)
            dest[2 * j] = result[:, 0:128]
            dest[2 * j + 1] = result[:, 128:256]

    def forward_heads(j, carry):
        ag_back(j + AG_LAGS[2])
        project(j)
        forward_pair(2 * j)
        ag_front(j + AG_LAGS[2] + 1)
        forward_pair(2 * j + 1)
        return carry

    lax.fori_loop(0, QKV_GROUPS, forward_heads, 0)
    tick = AG_LAGS[2] + QKV_GROUPS
    for i in range(OUT_GROUPS):
        ag_back(tick)
        tick += 1
        ag_front(tick)

    for e in range(4):
        cols = pl.ds(e * TILE, TILE)
        res[:, cols] = tok[:, cols].astype(f32) + dot(ctx[...], tile_of(OUT_START + e))

    def norm_two(i, carry):
        at = pl.ds(pl.multiple_of(i * 128, 128), 128)
        stream = res[at, :]
        scale = lax.rsqrt(jnp.mean(stream * stream, axis=-1, keepdims=True) + norm_eps)
        low = (stream * scale * gains[1]).astype(bf16)
        n2[at, :] = low
        n2t[:, at] = low.astype(f32).T.astype(bf16)
        mix[at, :] = stream
        gn[at, :] = jnp.zeros((128, width), f32)
        return carry

    lax.fori_loop(0, tok_count // 128, norm_two, 0)

    root = float(np.sqrt(2.0 / np.pi))

    def feed(step, carry):
        f, late, before = ff_step(step)

        @pl.when(late)
        def _():
            ag5(jnp.where(late, QKV_GROUPS + OUT_GROUPS + f, -1))

        @pl.when(jnp.logical_not(late))
        def _():
            ag_back(before + tick)

        t0 = FF_START + 3 * f
        gate_w, up_w, down_w = tile_of(t0), tile_of(t0 + 1), tile_of(t0 + 2)
        gate = dot(n2[...], gate_w)
        up = dot(n2[...], up_w)
        grad_hidden = dot(gout[...], down_w)
        square = gate * gate
        turn = jnp.tanh(root * gate * (1.0 + 0.044715 * square))
        half = 0.5 * (1.0 + turn)
        active = gate * half
        slope_of = half + 0.5 * gate * (1.0 - turn * turn) * (root * (1.0 + 3 * 0.044715 * square))
        hidden = (active * up).astype(bf16)

        @pl.when(jnp.logical_not(late))
        def _():
            ag_front(before + tick + 1)

        grad_gate = (grad_hidden * up * slope_of).astype(bf16)
        grad_up = (grad_hidden * active).astype(bf16)
        mix[...] += dot_nt(hidden, down_w)
        gn[...] += dot_nt(grad_gate, gate_w) + dot_nt(grad_up, up_w)
        ag_sent(f + QKV_GROUPS + OUT_GROUPS)
        shape = w.shape[1:]
        w[t0] = dot(n2t[...], grad_gate).astype(bf16).reshape(shape)
        w[t0 + 1] = dot(n2t[...], grad_up).astype(bf16).reshape(shape)
        w[t0 + 2] = dot(goutt[...], hidden).astype(bf16).reshape(shape)
        rs_tick(step - SUM_LAG)
        return carry

    lax.fori_loop(0, ff_groups, feed, 0)

    gsum[...] = jnp.zeros_like(gsum)
    grad_res, gctx = mix, gout

    def norm_two_back(i, carry):
        at = pl.ds(pl.multiple_of(i * 128, 128), 128)
        valid = (iota((128, width), 0) + i * 128 < both_len).astype(f32)
        ctx[at, :] = (valid * mix[at, :]).astype(bf16)
        stream = res[at, :]
        scale = lax.rsqrt(jnp.mean(stream * stream, axis=-1, keepdims=True) + norm_eps)
        got = gn[at, :]
        gsum[1] += jnp.sum((got * stream * scale).reshape(16, 8, width), axis=0)
        scaled = gains[1] * got
        inner = jnp.mean(scaled * stream, axis=-1, keepdims=True)
        total = gout[at, :].astype(f32) + scale * scaled - stream * (scale * scale * scale * inner)
        grad_res[at, :] = total
        n2[at, :] = total.astype(bf16)
        gn[at, :] = jnp.zeros((128, width), f32)
        return carry

    lax.fori_loop(0, tok_count // 128, norm_two_back, 0)
    out_copy = pltpu.make_async_copy(ctx, out_hbm, in_sem.at[0])
    out_copy.start()
    attended = n2
    shape = w.shape[1:]
    done = ff_groups - SUM_LAG
    rs_tick(done)
    done += 1
    for yy in range(ny):
        for cc in range(2):
            part = jnp.zeros((tok_count, TILE), f32)
            for e in range(4):
                block = w[OUT_START + e, yy, cc].reshape(TILE, TILE)
                part = part + dot_nt(attended[:, pl.ds(e * TILE, TILE)], block)
            gctx[:, pl.ds((yy * 2 + cc) * TILE, TILE)] = part.astype(bf16)
    for i in range(OUT_GROUPS):
        ag_sent(QKV_GROUPS + i)
        for e in (2 * i, 2 * i + 1):
            w[OUT_START + e] = (
                dot(ctxt[...], attended[:, pl.ds(e * TILE, TILE)]).astype(bf16).reshape(shape)
            )
        rs_front(done)
        if i < OUT_GROUPS - 1:
            rs_back(done)
        done += 1

    flip = (sq_row + sq_lane == 127).astype(f32).astype(bf16)
    flip_halves = jnp.where(
        (sq_row < 64) == (sq_lane < 64), (lax.rem(sq_row, 64) + lax.rem(sq_lane, 64) == 63).astype(f32), 0.0
    ).astype(bf16)

    def split_left(matrix, value):
        high = value.astype(bf16)
        rest = (value - high.astype(f32)).astype(bf16)
        return dot(matrix, high) + dot(matrix, rest)

    def backward_pair(p, local, between):
        at = pl.ds(pl.multiple_of(p * 128, 128), 128)
        k_turned = kp[p].astype(f32).T.astype(bf16)
        grad_rows = gctx[:, at]
        dv_parts, dk_parts, dq_parts, x_parts, y_parts = [], [], [], [], []
        for e in range(2):
            h = 2 * p + e
            q_all, k_all = augmented(p, e)
            steep = slope(gv[h, 0:1, :])
            zero = jnp.zeros((tok_count, 128), f32)
            one_head = pick(grad_rows, zero) if e == 0 else pick(zero, grad_rows)
            left = jnp.concatenate([k_turned[64 * e : 64 * (e + 1)], hxt[...], hyt[...]], axis=0)
            acc[...] = jnp.zeros_like(acc)
            dv_e = jnp.zeros((tok_count, 128), f32)
            dk_e = jnp.zeros((tok_count, 128), f32)
            turned = []
            for part in range(2):
                cols = slice(half_rows * part, half_rows * (part + 1))
                scores = dot_nt(k_all, q_all[cols]) + rel_bias(steep, part)
                probs = jnp.exp(scores - lse[h, 0:1, cols])
                grad_probs = dot_nt(vp[p], one_head[cols])
                inner = jnp.sum(grad_probs * probs, axis=0, keepdims=True)
                grad_scores = (probs * (grad_probs - inner)).astype(bf16)
                dv_e = dv_e + dot(probs.astype(bf16), grad_rows[cols])
                dk_e = dk_e + dot(grad_scores, qp[p, cols])
                turned.append(dot(left, grad_scores))
                for jb in range(blocks):
                    start = tok_count - 128 * jb + half_rows * part
                    acc[:, start : start + half_rows] += grad_scores[128 * jb : 128 * (jb + 1)].astype(f32)
            all_turned = jnp.concatenate(turned, axis=1)
            dq_parts.append(all_turned[0:64])
            x_parts.append(all_turned[64:128])
            y_parts.append(all_turned[128:192])
            dv_parts.append(dv_e)
            dk_parts.append(dk_e)
            rolled = pltpu.roll(split_left(flip, acc[...]), 0, 1, stride=1, stride_axis=0)
            gv[h, 0:1, :] = jnp.sum(rolled, axis=0, keepdims=True)
            if e == 0:
                between()
        low = half_lane
        cols = pl.ds(local * 128, 128)
        dq[:, cols] = jnp.concatenate(dq_parts, axis=0).T.astype(bf16)
        dk[:, cols] = jnp.where(low, dk_parts[0], dk_parts[1]).astype(bf16)
        dv[:, cols] = jnp.where(low, dv_parts[0], dv_parts[1]).astype(bf16)
        for parts, hots, dest in ((x_parts, hx, ggx), (y_parts, hq2, ggy)):
            table_grad = dot(jnp.concatenate(parts, axis=0).astype(bf16), hots[...])
            table_grad = jnp.where(sq_lane < 64, table_grad, 0.0)
            rolled = pltpu.roll(split_left(flip_halves, table_grad), 0, 1, stride=1, stride_axis=0)
            dest[2 * p, 0:1, :] = jnp.sum(rolled[0:64], axis=0, keepdims=True)
            dest[2 * p + 1, 0:1, :] = jnp.sum(rolled[64:128], axis=0, keepdims=True)

    first_head = ff_groups + OUT_GROUPS

    def end_tick(j):
        return jnp.minimum(done + 2 * j + 1, first_head + j)

    def backward_heads(j, carry):
        middle = jnp.where(j <= first_head - 1 - done, done + 2 * j, -SKIP)
        backward_pair(2 * j, 0, lambda: rs_back(end_tick(j - 1)))
        rs_front(middle)
        backward_pair(2 * j + 1, 1, lambda: rs_back(middle))
        gn[...] += (
            dot_nt(dq[...], tile_of(3 * j))
            + dot_nt(dk[...], tile_of(3 * j + 1))
            + dot_nt(dv[...], tile_of(3 * j + 2))
        )
        ag_sent(j)
        for i, part in enumerate((dq, dk, dv)):
            w[3 * j + i] = dot(n1t[...], part[...]).astype(bf16).reshape(shape)
        rs_front(end_tick(j))
        return carry

    lax.fori_loop(0, QKV_GROUPS, backward_heads, 0)
    done = min(done + 2 * QKV_GROUPS, groups)
    rs_back(done - 1)
    rs_tick(done)

    def norm_one_back(i, carry):
        at = pl.ds(pl.multiple_of(i * 128, 128), 128)
        stream = tok[at, :].astype(f32)
        scale = lax.rsqrt(jnp.mean(stream * stream, axis=-1, keepdims=True) + norm_eps)
        got = gn[at, :]
        gsum[0] += jnp.sum((got * stream * scale).reshape(16, 8, width), axis=0)
        scaled = gains[0] * got
        inner = jnp.mean(scaled * stream, axis=-1, keepdims=True)
        grad_res[at, :] = (
            grad_res[at, :] + scale * scaled - stream * (scale * scale * scale * inner)
        )
        return carry

    lax.fori_loop(0, tok_count // 128, norm_one_back, 0)
    gtok_copy = pltpu.make_async_copy(grad_res, gtok_hbm, in_sem.at[1])
    gtok_copy.start()
    rs_tick(done + 1)

    def unhot(bucket_col, count):
        return (bucket_col == iota((count, 128), 1)).astype(f32).astype(bf16)

    def head_rows(ref, start=0):
        return jnp.concatenate([ref[h, 0:1, :] for h in range(start, HEADS, 1)], axis=0)

    col_span = iota((span, 128), 0)
    rel_source = lax.rem(col_span - 127 + span, span)
    rel_sum = split_dot(head_rows(gv), unhot(rel_bucket(tok_count - rel_source), span))
    col_square = iota((128, 128), 0)
    low_source = lax.rem(col_square - 63 + 128, 128)
    high_source = lax.rem(col_square - 127 + 128, 128)

    def signed(source):
        return jnp.where(source < 64, source, source - 128)

    low_hot = unhot(layout_bucket(-signed(low_source)), 128)
    high_hot = unhot(layout_bucket(-signed(high_source)), 128)
    odd = lax.rem(iota((HEADS, 128), 0), 2) == 1

    def layout_sum(ref):
        lines = head_rows(ref)
        return jnp.where(odd, split_dot(lines, high_hot), split_dot(lines, low_hot))

    spread = (iota((128, 512), 0) == iota((128, 512), 1) // HEADS).astype(f32).astype(bf16)
    keep = lax.rem(iota((HEADS, 512), 1), HEADS) == iota((HEADS, 512), 0)

    def flat_table(value):
        high = value.astype(bf16)
        rest = (value - high.astype(f32)).astype(bf16)
        rest_two = (value - high.astype(f32) - rest.astype(f32)).astype(bf16)
        wide = dot(high, spread) + dot(rest, spread) + dot(rest_two, spread)
        return jnp.sum(jnp.where(keep, wide, 0.0), axis=0, keepdims=True)

    tiles = []
    for k in range(2):
        line = jnp.sum(gsum[k], axis=0, keepdims=True)
        tiles += [line[:, 128 * n : 128 * (n + 1)] for n in range(width // 128)]
    for value in (rel_sum, layout_sum(ggx), layout_sum(ggy)):
        line = flat_table(value)
        tiles += [line[:, 128 * n : 128 * (n + 1)] for n in range(4)]
    for d in range(len(devs)):
        line = jnp.zeros((1, 128), f32)
        for n in range(d * per // 128, (d * per + per - 1) // 128 + 1):
            shift = 128 * n - d * per
            moved = pltpu.roll(tiles[n], shift % 128, 1)
            inside = jnp.logical_and(lane1 >= shift, lane1 < min(shift + 128, per))
            line = jnp.where(inside, moved, line)
        sgr[near, d : d + 1, :] = line

    def near_start(k, landed):
        part = landed.at[near]
        for step in cube:
            remote(part, part, sm_send.at[k], sm_recv.at[k], cube_dev(step)).start()

    def near_sum(k, landed, lined):
        part = landed.at[pl.ds(0, len(cube))]
        cast_wait(remote(part, part, sm_send.at[k], sm_recv.at[k], sib))
        total = landed[0]
        for i in range(1, len(cube) + 1):
            total = total + landed[i]
        lined[z] = total
        for i in range(1, nz):
            remote(lined.at[z], lined.at[z], sm_send.at[k + 1], sm_recv.at[k + 1], zdev(i)).start()

    def line_sum(k, lined):
        part = lined.at[pl.ds(0, nz - 1)]
        cast_wait(remote(part, part, sm_send.at[k + 1], sm_recv.at[k + 1], sib))
        total = lined[0]
        for i in range(1, nz):
            total = total + lined[i]
        return total

    near_start(2, sgr)
    rs_tick(done + 2)
    near_sum(2, sgr, sgz)
    for n in range(done + 3, groups + LAGS[4]):
        rs_tick(n)
    small_total = line_sum(2, sgz)
    me = ((y * 2 + c) * nz + z) * nx + x
    mine = iota(small_total.shape, 0) == me
    osmall_ref[...] = jnp.sum(jnp.where(mine, small_total, 0.0), axis=0, keepdims=True)

    own_copy = pltpu.make_async_copy(own, own_hbm, in_sem.at[2])
    own_copy.start()
    squares = jnp.zeros((8, TILE), f32)
    for t in range(own.shape[0]):
        value = own[t]
        squares = squares + jnp.sum((value * value).reshape(rows // 8, 8, TILE), axis=0)
    nbr[near] = squares[:, 0:128] + squares[:, 128:256]
    near_start(4, nbr)
    out_copy.wait()
    gtok_copy.wait()
    for n in range(groups):
        rs_sent(n)
    near_sum(4, nbr, nbz)
    total = jnp.sum(line_sum(4, nbz)) + jnp.sum(small_total * small_total)
    norm_ref[...] = jnp.full((8, 128), 1.0, f32) * total
    own_copy.wait()


def update_kernel(
    sizes,
    total_ref,
    small_grad,
    small_master,
    small_first,
    small_second,
    own_hbm,
    block_hbm,
    gtok_hbm,
    attn_hbm,
    attn_first_hbm,
    attn_second_hbm,
    ffin_hbm,
    ffin_first_hbm,
    ffin_second_hbm,
    down_hbm,
    down_first_hbm,
    down_second_hbm,
    norm_out,
    small_master_out,
    small_first_out,
    small_second_out,
    block_out,
    gtok_out,
    attn_out,
    attn_first_out,
    attn_second_out,
    query_second_out,
    ffin_out,
    ffin_first_out,
    ffin_second_out,
    down_out,
    down_first_out,
    down_second_out,
    own,
    attn,
    ffin,
    down,
    block,
    gtok,
    in_sem,
    out_sem,
    pass_sem,
):
    (ff_groups,) = sizes
    passing = [
        pltpu.make_async_copy(block_hbm, block, pass_sem.at[0]),
        pltpu.make_async_copy(gtok_hbm, gtok, pass_sem.at[1]),
    ]
    passed = [
        pltpu.make_async_copy(block, block_out, pass_sem.at[2]),
        pltpu.make_async_copy(gtok, gtok_out, pass_sem.at[3]),
    ]
    first_tiles, other_tiles = pl.ds(0, FF_START), pl.ds(FF_START, 3 * ff_groups)
    loads = [
        [pltpu.make_async_copy(own_hbm.at[first_tiles], own.at[first_tiles], in_sem.at[0])],
        [pltpu.make_async_copy(own_hbm.at[other_tiles], own.at[other_tiles], in_sem.at[1])],
        [],
    ]
    sources = (
        (attn_hbm, attn_first_hbm, attn_second_hbm),
        (ffin_hbm, ffin_first_hbm, ffin_second_hbm),
        (down_hbm, down_first_hbm, down_second_hbm),
    )
    state = (attn, ffin, down)
    for i in range(3):
        loads[i] += [
            pltpu.make_async_copy(src, state[i].at[k], in_sem.at[2 + 3 * i + k])
            for k, src in enumerate(sources[i])
        ]
    for part in (*loads, passing):
        for copy in part:
            copy.start()
    norm = jnp.sqrt(total_ref[0:1, 0:1])
    norm_out[...] = norm
    clip = clip_max / jnp.maximum(norm, clip_max)
    per = small_master.shape[1]
    results = adamw_update(
        small_master[...], small_first[...], small_second[...], small_grad[:, 0:per] * clip, small_rate, 0.0
    )
    for ref, value in zip((small_master_out, small_first_out, small_second_out), results):
        ref[...] = value

    def update(ref, at, tile):
        results = adamw_update(
            ref[(0,) + at], ref[(1,) + at], ref[(2,) + at], own[tile] * clip, matrix_rate, decay_rate
        )
        for k in range(3):
            ref[(k,) + at] = results[k]

    every = slice(None)
    stores = []

    def store(i, pairs):
        for src, dst in pairs:
            copy = pltpu.make_async_copy(src, dst, out_sem.at[len(stores)])
            copy.start()
            stores.append(copy)

    for copy in loads[0]:
        copy.wait()
    for j in range(QKV_GROUPS):
        cols = pl.ds(j * TILE, TILE)
        for i in range(3):
            update(attn, (i, every, cols), 3 * j + i)
        update(attn, (3, every, cols), OUT_START + j)
    store(
        0,
        [
            (attn.at[0], attn_out),
            (attn.at[1], attn_first_out),
            (attn.at[2, pl.ds(1, 3)], attn_second_out),
            (attn.at[2, 0], query_second_out),
        ],
    )
    for copy in loads[1]:
        copy.wait()

    def update_in(f, carry):
        cols = pl.ds(pl.multiple_of(f * TILE, TILE), TILE)
        for i in range(2):
            update(ffin, (i, every, cols), FF_START + 3 * f + i)
        return carry

    lax.fori_loop(0, ff_groups, update_in, 0)
    store(1, [(ffin.at[k], ref) for k, ref in enumerate((ffin_out, ffin_first_out, ffin_second_out))])
    for copy in loads[2]:
        copy.wait()

    def update_down(f, carry):
        cols = pl.ds(pl.multiple_of(f * TILE, TILE), TILE)
        update(down, (every, cols), FF_START + 3 * f + 2)
        return carry

    lax.fori_loop(0, ff_groups, update_down, 0)
    store(2, [(down.at[k], ref) for k, ref in enumerate((down_out, down_first_out, down_second_out))])
    for arrived, copy in zip(passing, passed):
        arrived.wait()
        copy.start()
    for copy in stores + passed:
        copy.wait()


def fused_on_device(
    tokens,
    cotangent,
    page_lengths,
    layout_pos,
    attn_master,
    attn_first,
    attn_second,
    ffin_master,
    ffin_first,
    ffin_second,
    down_master,
    down_first,
    down_second,
    small_master,
    small_first,
    small_second,
    *,
    ny,
    nz,
    nx,
):
    f32, bf16 = jnp.float32, jnp.bfloat16
    tok_count, width = tokens.shape
    rows, ff = down_master.shape
    per = small_master.shape[0]
    ff_groups = ff // TILE
    tiles = FF_START + 3 * ff_groups
    groups = QKV_GROUPS + OUT_GROUPS + ff_groups
    pairs = HEADS // 2
    vmem, dma = pltpu.VMEM, pltpu.SemaphoreType.DMA
    square = (tok_count, width)
    banks = len(Z_FIRST_SUMS)
    scratch = [
        vmem((tiles, ny, 2, nz, nx, rows, TILE), bf16),
        vmem((SLOTS, 3, ny, nz, nx, rows, TILE), bf16),
        vmem((D_SLOTS, 2, 3, nz, HALF, TILE), bf16),
        vmem((D_SLOTS, 2, 3, nz, rows, TILE), bf16),
        vmem((Z_SLOTS, 4, 3, rows, TILE), bf16),
        vmem((banks, 4, 3, ny, nx, rows, TILE), bf16),
        vmem((banks, 2, 3, HALF, TILE), bf16),
        vmem((banks, 2, 3, rows, TILE), bf16),
        vmem((tiles, rows, TILE), f32),
        vmem(square, f32),
        vmem((ny * 2 * nx, nz, 8, 128), f32),
        vmem((ny * 2 * nx, ny * 2 * nz * nx, 128), f32),
        vmem((nz, ny * 2 * nz * nx, 128), f32),
        vmem((ny * 2 * nx, 8, 128), f32),
        vmem((nz, 8, 128), f32),
        vmem(square, bf16),
        vmem(square, bf16),
        vmem((width, tok_count), bf16),
        vmem((pairs, tok_count, 128), bf16),
        vmem((pairs, tok_count, 128), bf16),
        vmem((pairs, tok_count, 128), bf16),
        vmem(square, bf16),
        vmem((width, tok_count), bf16),
        vmem(square, f32),
        vmem(square, bf16),
        vmem((width, tok_count), bf16),
        vmem(square, bf16),
        vmem((width, tok_count), bf16),
        vmem(square, f32),
        vmem((pairs, 128, 128), bf16),
        vmem((HEADS, 128, 128), bf16),
        vmem((HEADS, 8, 2 * tok_count), f32),
        vmem((HEADS, 8, tok_count), f32),
        vmem((HEADS, 8, 128), f32),
        vmem((HEADS, 8, 128), f32),
        vmem((128, 2 * tok_count), f32),
        vmem((tok_count, 128), bf16),
        vmem((tok_count, 128), bf16),
        vmem((tok_count, 128), bf16),
        vmem((tok_count, 128), bf16),
        vmem((64, tok_count), bf16),
        vmem((64, tok_count), bf16),
        vmem((tok_count, TILE), bf16),
        vmem((tok_count, TILE), bf16),
        vmem((tok_count, TILE), bf16),
        vmem((2, 1, width), f32),
        vmem((2, 8, width), f32),
        dma((groups,)),
        dma((3,)),
        dma((7, groups)),
        dma((7, groups)),
        dma((2, 3 * LATE_GROUPS)),
        dma((2, 3 * LATE_GROUPS)),
        dma((4, 3 * banks)),
        dma((4, 3 * banks)),
        dma((9, groups)),
        dma((9, groups)),
        dma((6,)),
        dma((6,)),
    ]
    in_vmem = pl.BlockSpec(memory_space=pltpu.VMEM)
    in_hbm = pl.BlockSpec(memory_space=pl.ANY)
    weights = attn_master.size + ffin_master.size + down_master.size
    block_out, grad_tokens, owned, owned_small, squares = pl.pallas_call(
        functools.partial(layer_kernel, (ny, nz, nx, per, ff_groups)),
        out_shape=[
            jax.ShapeDtypeStruct(square, bf16),
            jax.ShapeDtypeStruct(square, f32),
            jax.ShapeDtypeStruct((tiles, rows, TILE), f32),
            jax.ShapeDtypeStruct((1, 128), f32),
            jax.ShapeDtypeStruct((8, 128), f32),
        ],
        in_specs=[in_vmem] * 3 + [in_hbm] * 5,
        out_specs=[in_hbm] * 3 + [in_vmem] * 2,
        scratch_shapes=scratch,
        compiler_params=pltpu.CompilerParams(
            collective_id=0, has_side_effects=True, vmem_limit_bytes=VMEM_BYTES
        ),
        cost_estimate=pl.CostEstimate(
            flops=6 * tok_count * weights * ny * 2 * nz * nx,
            bytes_accessed=24 * weights,
            transcendentals=3 * tok_count * tok_count * HEADS,
        ),
    )(
        page_lengths.T,
        layout_pos,
        small_master.reshape(1, per),
        tokens,
        cotangent,
        attn_master,
        ffin_master,
        down_master,
    )
    like = [
        jax.ShapeDtypeStruct((1, 1), f32),
        *[jax.ShapeDtypeStruct((1, per), f32)] * 3,
        jax.ShapeDtypeStruct(square, bf16),
        jax.ShapeDtypeStruct(square, f32),
        jax.ShapeDtypeStruct(attn_master.shape, f32),
        jax.ShapeDtypeStruct(attn_master.shape, f32),
        jax.ShapeDtypeStruct((3,) + attn_master.shape[1:], f32),
        jax.ShapeDtypeStruct(attn_master.shape[1:], f32),
        *[jax.ShapeDtypeStruct(ffin_master.shape, f32)] * 3,
        *[jax.ShapeDtypeStruct(down_master.shape, f32)] * 3,
    ]
    results = pl.pallas_call(
        functools.partial(update_kernel, (ff_groups,)),
        out_shape=like,
        in_specs=[in_vmem] * 5 + [in_hbm] * 12,
        out_specs=[in_vmem] * 4 + [in_hbm] * 12,
        scratch_shapes=[
            vmem((tiles, rows, TILE), f32),
            vmem((3,) + attn_master.shape, f32),
            vmem((3,) + ffin_master.shape, f32),
            vmem((3,) + down_master.shape, f32),
            vmem(square, bf16),
            vmem(square, f32),
            dma((11,)),
            dma((10,)),
            dma((4,)),
        ],
        compiler_params=pltpu.CompilerParams(vmem_limit_bytes=VMEM_BYTES),
        cost_estimate=pl.CostEstimate(
            flops=20 * weights, bytes_accessed=28 * weights, transcendentals=2 * weights
        ),
    )(
        squares,
        owned_small,
        small_master.reshape(1, per),
        small_first.reshape(1, per),
        small_second.reshape(1, per),
        owned,
        block_out,
        grad_tokens,
        attn_master,
        attn_first,
        attn_second,
        ffin_master,
        ffin_first,
        ffin_second,
        down_master,
        down_first,
        down_second,
    )
    norm, small_new, small_one, small_two = results[:4]
    return (
        results[4],
        results[5],
        norm.reshape(()),
        *results[6:],
        small_new.reshape(per),
        small_one.reshape(per),
        small_two.reshape(per),
    )


def choose(mesh, width):
    n_dp, n_fsdp = mesh.shape["dp"], mesh.shape["fsdp"]
    rows = width // (n_dp * n_fsdp)
    if n_dp == 4 and n_fsdp == 2 * LINE and rows % (2 * HALF) == 0:
        return functools.partial(fused_on_device, ny=n_dp // 2, nz=n_fsdp // 2, nx=2)
    return on_device


def sharded(mesh, program):
    return jax.shard_map(
        program,
        mesh=mesh,
        in_specs=(
            P(("dp", "fsdp"), None),
            P(("dp", "fsdp"), None),
            P(None, ("dp", "fsdp")),
            P(None, ("dp", "fsdp")),
            P(None, ("dp", "fsdp"), None),
            P(None, ("dp", "fsdp"), None),
            P(None, ("dp", "fsdp"), None),
            P(None, ("dp", "fsdp"), None),
            P(None, ("dp", "fsdp"), None),
            P(None, ("dp", "fsdp"), None),
            P(("dp", "fsdp"), None),
            P(("dp", "fsdp"), None),
            P(("dp", "fsdp"), None),
            P(("dp", "fsdp")),
            P(("dp", "fsdp")),
            P(("dp", "fsdp")),
        ),
        out_specs=(
            P(("dp", "fsdp"), None),
            P(("dp", "fsdp"), None),
            P(),
            P(None, ("dp", "fsdp"), None),
            P(None, ("dp", "fsdp"), None),
            P(None, ("dp", "fsdp"), None),
            P(("dp", "fsdp"), None),
            P(None, ("dp", "fsdp"), None),
            P(None, ("dp", "fsdp"), None),
            P(None, ("dp", "fsdp"), None),
            P(("dp", "fsdp"), None),
            P(("dp", "fsdp"), None),
            P(("dp", "fsdp"), None),
            P(("dp", "fsdp")),
            P(("dp", "fsdp")),
            P(("dp", "fsdp")),
        ),
        check_vma=False,
    )


def solution(mesh):
    def step(*args):
        return sharded(mesh, choose(mesh, args[0].shape[1]))(*args)

    return step
```

```python
import functools

import jax
import jax.numpy as jnp
import numpy as np
from jax import lax
from jax.experimental import pallas as pl
from jax.experimental.pallas import tpu as pltpu
from jax.sharding import PartitionSpec as P

HEADS = 16
HEAD_DIM = 64
BUCKETS = 32
LAYOUT_POS = 64
STEP = 10


norm_eps = 1e-06
adam_eps = 1e-08
beta_one = 0.5
beta_two = 0.5
clip_max = 1.0
matrix_rate = 0.02
small_rate = 0.4
decay_rate = 0.01
far_negative = -1e30
max_distance = 128
block_rows = 512


def relative_buckets(tok_count, buckets):
    offsets = np.arange(tok_count)[None, :] - np.arange(tok_count)[:, None]
    half_count = buckets // 2
    exact_count = half_count // 2
    distance = np.abs(offsets)
    far_bucket = exact_count + (
        np.log(np.maximum(distance, 1) / exact_count)
        / np.log(max_distance / exact_count)
        * (half_count - exact_count)
    ).astype(np.int64)
    far_bucket = np.minimum(far_bucket, half_count - 1)
    bucket_ids = (offsets > 0).astype(np.int64) * half_count + np.where(
        distance < exact_count, distance, far_bucket
    )
    return bucket_ids.astype(np.int32)


def layout_table(positions, buckets):
    offsets = np.arange(positions)[None, :] - np.arange(positions)[:, None]
    half_count = buckets // 2
    bucket_ids = np.clip(offsets, -half_count, half_count - 1) + half_count
    return (np.arange(buckets)[:, None] == bucket_ids.reshape(1, -1)).astype(np.float32)


def scaled_norm(values, gain):
    return values * lax.rsqrt(jnp.mean(values * values, axis=-1, keepdims=True) + norm_eps) * gain


def gated_gelu(gate_pre, up_pre):
    return jax.nn.gelu(gate_pre, approximate=True) * up_pre


def adamw_update(master, first_state, second_state, gradient, step_rate, weight_decay):
    first_new = beta_one * first_state + (1.0 - beta_one) * gradient
    second_new = beta_two * second_state + (1.0 - beta_two) * gradient * gradient
    first_hat = first_new / (1.0 - beta_one**STEP)
    second_hat = second_new / (1.0 - beta_two**STEP)
    master_new = master - step_rate * (
        first_hat / (jnp.sqrt(second_hat) + adam_eps) + weight_decay * master
    )
    return (master_new, first_new, second_new)


def on_device(
    tokens,
    cotangent,
    page_lengths,
    layout_pos,
    attn_master,
    attn_first,
    attn_second,
    ffin_master,
    ffin_first,
    ffin_second,
    down_master,
    down_first,
    down_second,
    small_master,
    small_first,
    small_second,
):
    f32 = jnp.float32
    bf16 = jnp.bfloat16
    highest = lax.Precision.HIGHEST
    tok_count, model_width = tokens.shape
    attn_low = attn_master.astype(bf16)
    ffin_low = ffin_master.astype(bf16)
    down_low = down_master.astype(bf16)
    small_low = small_master.astype(bf16)
    w_attn, w_in, w_down, small_all = (
        lax.all_gather(attn_low, ("dp", "fsdp"), axis=1, tiled=True),
        lax.all_gather(ffin_low, ("dp", "fsdp"), axis=1, tiled=True),
        lax.all_gather(down_low, ("dp", "fsdp"), axis=0, tiled=True),
        lax.all_gather(small_low, ("dp", "fsdp"), axis=0, tiled=True),
    )
    gain_one = small_all[:model_width].astype(f32)
    gain_two = small_all[model_width : 2 * model_width].astype(f32)
    tables_t = jnp.transpose(small_all[2 * model_width :].reshape(3, BUCKETS, HEADS), (0, 2, 1))
    layout_hot = jnp.asarray(layout_table(LAYOUT_POS, BUCKETS))
    kernels = jnp.einsum(
        "khn,nm->khm", tables_t[1:], layout_hot.astype(bf16), preferred_element_type=f32
    )
    kernels = kernels.reshape(2, HEADS, LAYOUT_POS, LAYOUT_POS).astype(bf16)
    first_len = page_lengths[0, 0]
    both_len = page_lengths[0, 0] + page_lengths[1, 0]
    tok_index = jnp.arange(tok_count)
    page_ids = jnp.where(tok_index < first_len, 0, jnp.where(tok_index < both_len, 1, 2))
    valid_mask = tok_index < both_len
    valid_rows = valid_mask.astype(f32)[:, None]
    pos_grid = jnp.arange(LAYOUT_POS)
    pos_hot = (layout_pos[:, :, None] == pos_grid[None, None, :]).astype(bf16)
    pos_hot_f32 = pos_hot.astype(f32)
    rel_rows = jnp.asarray(relative_buckets(tok_count, BUCKETS))
    bucket_grid = jnp.arange(BUCKETS)
    rows_per_block = min(tok_count, block_rows)
    block_count = tok_count // rows_per_block
    block_starts = jnp.arange(block_count) * rows_per_block
    stream = tokens.astype(f32)
    normed_one = scaled_norm(stream, gain_one).astype(bf16)
    projected = jnp.einsum(
        "td,kde->kte", normed_one, w_attn[:3], preferred_element_type=f32
    ).astype(bf16)
    shaped = projected.reshape(3, tok_count, HEADS, HEAD_DIM)
    queries = shaped[0]
    key_rows = shaped[1]
    values = shaped[2]

    def block_scores(block_start, query_rows):
        rel_idx = lax.dynamic_slice_in_dim(rel_rows, block_start, rows_per_block, 0)
        rel_hot = (bucket_grid[:, None] == rel_idx.reshape(1, -1)).astype(bf16)
        bias_all = jnp.dot(tables_t[0], rel_hot, preferred_element_type=f32).reshape(
            HEADS, rows_per_block, tok_count
        )
        layout_rows = jnp.einsum(
            "kia,khab->khib", pos_hot, kernels, preferred_element_type=f32
        ).astype(bf16)
        bias_all = bias_all + jnp.einsum(
            "khib,kjb->hij", layout_rows, pos_hot, preferred_element_type=f32
        )
        scores = (
            jnp.einsum("ihe,jhe->hij", query_rows, key_rows, preferred_element_type=f32) + bias_all
        )
        allowed = (page_ids[:, None] == page_ids[None, :]) & valid_mask[None, :]
        masked = jnp.where(allowed[None], scores, far_negative)
        return (masked, allowed, rel_hot, pos_hot)

    def forward_block(running, block_start):
        masked, allowed, rel_hot, query_hot = block_scores(block_start, queries)
        row_max = jnp.max(masked, axis=-1, keepdims=True)
        exponent = jnp.exp(masked - row_max)
        row_total = jnp.sum(exponent, axis=-1, keepdims=True)
        weights_low = (exponent / row_total).astype(bf16)
        block_context = jnp.einsum("hij,jhe->ihe", weights_low, values, preferred_element_type=f32)
        return (running, (block_context, row_max + jnp.log(row_total)))

    unused_carry, (context_blocks, lse_blocks) = lax.scan(
        forward_block, jnp.zeros((), f32), block_starts
    )
    context = context_blocks.reshape(tok_count, model_width).astype(bf16)
    attended = jnp.dot(context, w_attn[3], preferred_element_type=f32)
    residual = stream + attended
    normed_two = scaled_norm(residual, gain_two).astype(bf16)
    gate_up = jnp.einsum("td,kdf->ktf", normed_two, w_in, preferred_element_type=f32)
    hidden = gated_gelu(gate_up[0], gate_up[1]).astype(bf16)
    mixed = jnp.einsum("tf,df->td", hidden, w_down, preferred_element_type=f32)
    block_out = (valid_rows * (residual + mixed)).astype(bf16)
    w_attn, w_in, w_down = (
        lax.all_gather(attn_low, ("dp", "fsdp"), axis=1, tiled=True),
        lax.all_gather(ffin_low, ("dp", "fsdp"), axis=1, tiled=True),
        lax.all_gather(down_low, ("dp", "fsdp"), axis=0, tiled=True),
    )
    grad_out = valid_rows * cotangent.astype(f32)
    grad_out_low = grad_out.astype(bf16)
    grad_down = jnp.einsum("td,tf->df", grad_out_low, hidden, preferred_element_type=f32)
    grad_hidden = jnp.einsum("td,df->tf", grad_out_low, w_down, preferred_element_type=f32)
    unused_gated, gated_pull = jax.vjp(gated_gelu, gate_up[0], gate_up[1])
    grad_gate, grad_up = gated_pull(grad_hidden)
    grad_gate_up = jnp.stack([grad_gate, grad_up]).astype(bf16)
    grad_in = jnp.einsum("td,ktf->kdf", normed_two, grad_gate_up, preferred_element_type=f32)
    grad_normed_two = jnp.einsum("ktf,kdf->td", grad_gate_up, w_in, preferred_element_type=f32)
    unused_second, norm_pull_two = jax.vjp(scaled_norm, residual, gain_two)
    grad_residual_norm, grad_gain_two = norm_pull_two(grad_normed_two)
    grad_residual = grad_out + grad_residual_norm
    grad_attended = grad_residual.astype(bf16)
    grad_out_proj = jnp.einsum("td,te->de", context, grad_attended, preferred_element_type=f32)
    grad_context = jnp.einsum(
        "te,de->td", grad_attended, w_attn[3], preferred_element_type=f32
    ).astype(bf16)
    grad_context = grad_context.reshape(tok_count, HEADS, HEAD_DIM)

    def backward_block(running, block_item):
        grad_key_rows, grad_value_rows, grad_rel, grad_layout = running
        block_start, lse_rows = block_item
        masked, allowed, rel_hot, query_hot = block_scores(block_start, queries)
        probs_f32 = jnp.exp(masked - lse_rows)
        grad_probs = jnp.einsum("ihe,jhe->hij", grad_context, values, preferred_element_type=f32)
        row_dot = jnp.sum(grad_probs * probs_f32, axis=-1, keepdims=True)
        grad_scores = jnp.where(allowed[None], probs_f32 * (grad_probs - row_dot), 0.0).astype(bf16)
        grad_query_rows = jnp.einsum(
            "hij,jhe->ihe", grad_scores, key_rows, preferred_element_type=f32
        )
        grad_key_rows = grad_key_rows + jnp.einsum(
            "hij,ihe->jhe", grad_scores, queries, preferred_element_type=f32
        )
        grad_value_rows = grad_value_rows + jnp.einsum(
            "hij,ihe->jhe", probs_f32.astype(bf16), grad_context, preferred_element_type=f32
        )
        grad_rel = grad_rel + lax.dot_general(
            grad_scores.reshape(HEADS, -1),
            rel_hot,
            (((1,), (1,)), ((), ())),
            preferred_element_type=f32,
        )
        query_sums = jnp.einsum("kia,hij->khaj", query_hot, grad_scores, preferred_element_type=f32)
        grad_layout = grad_layout + jnp.einsum(
            "khaj,kjb->khab", query_sums, pos_hot_f32, precision=highest
        )
        return ((grad_key_rows, grad_value_rows, grad_rel, grad_layout), grad_query_rows)

    start_state = (
        jnp.zeros((tok_count, HEADS, HEAD_DIM), f32),
        jnp.zeros((tok_count, HEADS, HEAD_DIM), f32),
        jnp.zeros((HEADS, BUCKETS), f32),
        jnp.zeros((2, HEADS, LAYOUT_POS, LAYOUT_POS), f32),
    )
    (grad_key_rows, grad_value_rows, grad_rel, grad_layout), grad_query_blocks = lax.scan(
        backward_block, start_state, (block_starts, lse_blocks)
    )
    grad_projected = jnp.stack(
        [
            grad_query_blocks.reshape(tok_count, model_width),
            grad_key_rows.reshape(tok_count, model_width),
            grad_value_rows.reshape(tok_count, model_width),
        ]
    ).astype(bf16)
    grad_qkv = jnp.einsum("td,kte->kde", normed_one, grad_projected, preferred_element_type=f32)
    grad_normed_one = jnp.einsum(
        "kte,kde->td", grad_projected, w_attn[:3], preferred_element_type=f32
    )
    unused_first, norm_pull_one = jax.vjp(scaled_norm, stream, gain_one)
    grad_stream, grad_gain_one = norm_pull_one(grad_normed_one)
    grad_tokens = grad_residual + grad_stream
    grad_layout_tables = jnp.dot(
        grad_layout.reshape(2 * HEADS, LAYOUT_POS * LAYOUT_POS), layout_hot.T, precision=highest
    ).reshape(2, HEADS, BUCKETS)
    grad_tables = jnp.concatenate([grad_rel[None], grad_layout_tables], 0)
    grad_small = jnp.concatenate(
        [grad_gain_one, grad_gain_two, jnp.transpose(grad_tables, (0, 2, 1)).reshape(-1)]
    )
    grad_attn = jnp.concatenate([grad_qkv, grad_out_proj[None]], 0)
    owned_attn, owned_in, owned_down, owned_small = (
        lax.psum_scatter(grad_attn, ("dp", "fsdp"), scatter_dimension=1, tiled=True),
        lax.psum_scatter(grad_in, ("dp", "fsdp"), scatter_dimension=1, tiled=True),
        lax.psum_scatter(grad_down, ("dp", "fsdp"), scatter_dimension=0, tiled=True),
        lax.psum_scatter(grad_small, ("dp", "fsdp"), scatter_dimension=0, tiled=True),
    )
    local_squares = (
        jnp.sum(owned_attn * owned_attn)
        + jnp.sum(owned_in * owned_in)
        + jnp.sum(owned_down * owned_down)
        + jnp.sum(owned_small * owned_small)
    )
    grad_norm = jnp.sqrt(lax.psum(local_squares, ("dp", "fsdp")))
    clip_scale = clip_max / jnp.maximum(grad_norm, clip_max)
    attn_new = adamw_update(
        attn_master, attn_first, attn_second, owned_attn * clip_scale, matrix_rate, decay_rate
    )
    ffin_new = adamw_update(
        ffin_master, ffin_first, ffin_second, owned_in * clip_scale, matrix_rate, decay_rate
    )
    down_new = adamw_update(
        down_master, down_first, down_second, owned_down * clip_scale, matrix_rate, decay_rate
    )
    small_new = adamw_update(
        small_master, small_first, small_second, owned_small * clip_scale, small_rate, 0.0
    )
    return (
        block_out,
        grad_tokens,
        grad_norm,
        attn_new[0],
        attn_new[1],
        attn_new[2][1:],
        attn_new[2][0],
        ffin_new[0],
        ffin_new[1],
        ffin_new[2],
        down_new[0],
        down_new[1],
        down_new[2],
        small_new[0],
        small_new[1],
        small_new[2],
    )


MESH = pl.DeviceIdType.MESH
TILE = 256
HALF = 16
SLOTS = 4
VMEM_BYTES = 63 * 2**20
Z_SLOTS = 12
AHEAD = 3
LATE_GROUPS = 3
SUM_LAG = 5
Z_FIRST_SUMS = (1, 5, 9)
LAGS = (1, 2, 3, 5, 7)
LINE_LAG = 3
D_SLOTS = 4
VMEM_BYTES = 63 * 2**20
FIRST_AHEAD = 0
DIRECT = 3
SKIP = 1000
AG_LAGS = (1, 2, 3)
LATE_TICK = 10
LATE_STEP = 2
LINE = 4
QKV_GROUPS = 4
OUT_GROUPS = 2
OUT_START = 12
FF_START = 16


def bucket_limits(tok_count):
    buckets = relative_buckets(tok_count, BUCKETS)[:, 0]
    return [int(np.argmax(buckets >= k)) for k in range(1, BUCKETS // 2)]


def dot(a, b):
    return lax.dot_general(a, b, (((1,), (0,)), ((), ())), preferred_element_type=jnp.float32)


def dot_nt(a, b):
    return lax.dot_general(a, b, (((1,), (1,)), ((), ())), preferred_element_type=jnp.float32)


def split_dot(a, b):
    high = a.astype(jnp.bfloat16)
    rest = (a - high.astype(jnp.float32)).astype(jnp.bfloat16)
    return dot(high, b) + dot(rest, b)


def iota(shape, dim):
    return lax.broadcasted_iota(jnp.int32, shape, dim)


def layer_kernel(
    sizes,
    page_ref,
    pos_ref,
    small_ref,
    tok_hbm,
    cot_hbm,
    attn_hbm,
    ffin_hbm,
    down_hbm,
    out_hbm,
    gtok_hbm,
    own_hbm,
    osmall_ref,
    norm_ref,
    w,
    rh,
    rd,
    re,
    rf,
    rbz,
    rbd,
    rbe,
    own,
    mix,
    smb,
    sgr,
    sgz,
    nbr,
    nbz,
    tok,
    n1,
    n1t,
    qp,
    kp,
    vp,
    ctx,
    ctxt,
    res,
    n2,
    n2t,
    gout,
    goutt,
    gn,
    kxs,
    km,
    gv,
    lse,
    ggx,
    ggy,
    acc,
    hx,
    hxx,
    hq2,
    k2,
    hxt,
    hyt,
    dq,
    dk,
    dv,
    gains,
    gsum,
    load_sem,
    in_sem,
    ag_send,
    ag_recv,
    late_send,
    late_recv,
    bl_send,
    bl_recv,
    rs_send,
    rs_recv,
    sm_send,
    sm_recv,
):
    ny, nz, nx, per, ff_groups = sizes
    f32, bf16 = jnp.float32, jnp.bfloat16
    groups = QKV_GROUPS + OUT_GROUPS + ff_groups
    tok_count, width = tok.shape
    rows = w.shape[5]
    dp, fs = lax.axis_index("dp"), lax.axis_index("fsdp")
    y, c, z, x = dp // 2, dp % 2, fs // nx, fs % nx

    def device(yy, cc, zz, xx):
        return (yy * 2 + cc, zz * nx + xx)

    sib, xnb, ynb = device(y, 1 - c, z, x), device(y, c, z, 1 - x), device(1 - y, c, z, x)

    def zdev(k):
        return device(y, c, lax.rem(z + k, nz), x)

    inner = jnp.logical_and(z > 0, z < LINE - 1)
    across = lax.rem(z + 2, LINE)
    edge = jnp.where(z < 2, 0, LINE - 1)
    inward = jnp.where(z < 2, 1, LINE - 2)
    far_end = LINE - 1 - edge
    dev_up, dev_down = device(y, c, jnp.minimum(z + 1, LINE - 1), x), device(y, c, jnp.maximum(z - 1, 0), x)
    dev_across, dev_edge, dev_inward, dev_far = (
        device(y, c, at, x) for at in (across, edge, inward, far_end)
    )

    def to_sides(send_up, send_down):
        pl.when(z < LINE - 1)(send_up)
        pl.when(z > 0)(send_down)

    def remote(src, dst, send, recv, dev):
        return pltpu.make_async_remote_copy(
            src_ref=src, dst_ref=dst, send_sem=send, recv_sem=recv, device_id=dev, device_id_type=MESH
        )

    cube = [(a, b, d) for a in range(ny) for b in range(2) for d in range(nx)][1:]

    def cube_dev(step):
        return device(*(1 - at if turn else at for at, turn in zip((y, c), step)), z, 1 - x if step[2] else x)

    near = (y * 2 + c) * nx + x

    barrier = pltpu.get_barrier_semaphore()
    for dev in [cube_dev(step) for step in cube] + [zdev(k) for k in range(1, nz)]:
        pl.semaphore_signal(barrier, inc=1, device_id=dev, device_id_type=MESH)

    def on_group(g, fn):
        if isinstance(g, int):
            if 0 <= g < groups:
                if g < QKV_GROUPS:
                    fn(3 * g, 3, g)
                elif g < QKV_GROUPS + OUT_GROUPS:
                    fn(OUT_START + 2 * (g - QKV_GROUPS), 2, g)
                else:
                    fn(FF_START + 3 * (g - QKV_GROUPS - OUT_GROUPS), 3, g)
            return
        is_out = jnp.logical_and(g >= QKV_GROUPS, g < QKV_GROUPS + OUT_GROUPS)
        inside = jnp.logical_and(g >= 0, g < groups)

        @pl.when(is_out)
        def _():
            fn(OUT_START + 2 * (g - QKV_GROUPS), 2, g)

        @pl.when(jnp.logical_and(inside, jnp.logical_not(is_out)))
        def _():
            fn(jnp.where(g < QKV_GROUPS, 3 * g, FF_START + 3 * (g - QKV_GROUPS - OUT_GROUPS)), 3, g)

    def load(g):
        def go(t0, count, g):
            if count == 2:
                for i in range(2):
                    cols = pl.ds(pl.multiple_of((t0 - OUT_START + i) * TILE, TILE), TILE)
                    pltpu.make_async_copy(attn_hbm.at[3, :, cols], own.at[t0 + i], load_sem.at[g]).start()
            elif isinstance(g, int) and g < QKV_GROUPS:
                cols = pl.ds(g * TILE, TILE)
                pltpu.make_async_copy(
                    attn_hbm.at[pl.ds(0, 3), :, cols], own.at[pl.ds(t0, 3)], load_sem.at[g]
                ).start()
            else:
                cols = pl.ds((g - QKV_GROUPS - OUT_GROUPS) * TILE, TILE)
                pltpu.make_async_copy(
                    ffin_hbm.at[:, :, cols], own.at[pl.ds(t0, 2)], load_sem.at[g]
                ).start()
                pltpu.make_async_copy(down_hbm.at[:, cols], own.at[t0 + 2], load_sem.at[g]).start()

        on_group(g, go)

    def load_wait(g):
        def go(t0, count, g):
            tiles = own.at[pl.ds(t0, count)]
            pltpu.make_async_copy(tiles, tiles, load_sem.at[g]).wait()
            for i in range(count):
                w[t0 + i, y, c, z, x] = own[t0 + i].astype(bf16)

        on_group(g, go)

    for g in range(groups):
        load(g)
    tok_copy = pltpu.make_async_copy(tok_hbm, tok, in_sem.at[0])
    cot_copy = pltpu.make_async_copy(cot_hbm, gout, in_sem.at[1])
    tok_copy.start()
    cot_copy.start()

    def ag_parts(t0, count, g):
        t = pl.ds(t0, count)
        return t, (lambda i: ag_send.at[i, g]), (lambda i: ag_recv.at[i, g])

    late_start = groups - LATE_GROUPS

    def on_early(g, fn):
        if isinstance(g, int):
            if g < late_start:
                on_group(g, fn)
        else:
            on_group(jnp.where(g < late_start, g, -1), fn)

    def on_late(g, fn):
        if isinstance(g, int):
            if late_start <= g < groups:
                on_group(g, fn)
        else:

            @pl.when(jnp.logical_and(g >= late_start, g < groups))
            def _():
                fn(FF_START + 3 * (g - QKV_GROUPS - OUT_GROUPS), 3, g)

    def late1(g):
        def go(t0, count, g):
            t, s, r = ag_parts(t0, count, g)
            mine = w.at[t, y, c, z, x]
            remote(mine, mine, s(1), r(1), xnb).start()
            remote(mine, mine, s(2), r(2), ynb).start()

        on_late(g, go)

    def late2(g):
        def go(t0, count, g):
            t, s, r = ag_parts(t0, count, g)
            xpart = w.at[t, y, c, z, 1 - x]
            ypart = w.at[t, 1 - y, c, z, x]
            remote(xpart, xpart, s(1), r(1), xnb).wait_recv()
            remote(ypart, ypart, s(2), r(2), ynb).wait_recv()
            xhalf = w.at[t, y, c, z, 1 - x, pl.ds(0, HALF)]
            yhalf = w.at[t, 1 - y, c, z, x, pl.ds(HALF, HALF)]
            remote(xhalf, xhalf, s(4), r(4), ynb).start()
            remote(yhalf, yhalf, s(3), r(3), xnb).start()

        on_late(g, go)

    def late3(g):
        def go(t0, count, g):
            t, s, r = ag_parts(t0, count, g)
            low = w.at[t, 1 - y, c, z, 1 - x, pl.ds(0, HALF)]
            high = w.at[t, 1 - y, c, z, 1 - x, pl.ds(HALF, HALF)]
            remote(low, low, s(4), r(4), ynb).wait_recv()
            remote(high, high, s(3), r(3), xnb).wait_recv()

        on_late(g, go)

    def late_tile(b):
        return FF_START + 3 * (ff_groups - LATE_GROUPS) + b

    def late_line(b):
        square = w.at[late_tile(b), :, c, z]
        s, r = late_send, late_recv
        to_sides(
            lambda: remote(square, square, s.at[0, b], r.at[0, b], dev_up).start(),
            lambda: remote(square, square, s.at[0, b], r.at[0, b], dev_down).start(),
        )
        remote(square, square, s.at[1, b], r.at[1, b], dev_across).start()

    def late_relay(b):
        landed = w.at[late_tile(b), :, c, across]
        s, r = late_send, late_recv
        remote(landed, landed, s.at[1, b], r.at[1, b], dev_across).wait_recv()

        @pl.when(inner)
        def _():
            remote(landed, landed, s.at[0, b], r.at[0, b], dev_edge).start()

    def late_step(t, fn):
        if isinstance(t, int):
            if 1 <= t <= 3 * LATE_GROUPS:
                fn(t - 1)
        else:

            @pl.when(jnp.logical_and(t >= 1, t <= 3 * LATE_GROUPS))
            def _():
                fn(t - 1)

    def late4(g):
        def go(t0, count, g):
            t, s, r = ag_parts(t0, count, g)
            for i in range(3):
                b = t0 + i - late_tile(0)
                two = w.at[t0 + i, :, c, pl.ds(0, 2)]
                remote(two, two, late_send.at[0, b], late_recv.at[0, b], dev_across).wait_recv()
            plane = w.at[t, :, c]
            remote(plane, plane, s(5), r(5), sib).start()

        on_late(g, go)

    def ag1(g):
        def go(t0, count, g):
            t, s, r = ag_parts(t0, count, g)
            mine = w.at[t, y, c, z, x]
            to_sides(
                lambda: remote(mine, mine, s(0), r(0), dev_up).start(),
                lambda: remote(mine, mine, s(0), r(0), dev_down).start(),
            )
            remote(mine, mine, s(6), r(6), dev_across).start()

        on_early(g, go)

    def ag1_relay(g):
        def go(t0, count, g):
            t, s, r = ag_parts(t0, count, g)
            landed = w.at[t, y, c, across, x]
            remote(landed, landed, s(6), r(6), dev_across).wait_recv()

            @pl.when(inner)
            def _():
                remote(landed, landed, s(0), r(0), dev_edge).start()

        on_early(g, go)

    def ag2(g):
        def go(t0, count, g):
            t, s, r = ag_parts(t0, count, g)
            two = w.at[t, y, c, pl.ds(0, 2), x]
            remote(two, two, s(0), r(0), dev_across).wait_recv()
            column = w.at[t, y, c, :, x]
            remote(column, column, s(1), r(1), xnb).start()
            remote(column, column, s(2), r(2), ynb).start()
            remote(column, column, s(5), r(5), sib).start()

        on_early(g, go)

    def ag3(g):
        def go(t0, count, g):
            t, s, r = ag_parts(t0, count, g)
            xcol = w.at[t, y, c, :, 1 - x]
            ycol = w.at[t, 1 - y, c, :, x]
            remote(xcol, xcol, s(1), r(1), xnb).wait_recv()
            xhalf = w.at[t, y, c, :, 1 - x, pl.ds(0, HALF)]
            remote(xhalf, xhalf, s(4), r(4), ynb).start()
            remote(xcol, xcol, s(5), r(5), sib).start()
            remote(ycol, ycol, s(2), r(2), ynb).wait_recv()
            yhalf = w.at[t, 1 - y, c, :, x, pl.ds(HALF, HALF)]
            remote(yhalf, yhalf, s(3), r(3), xnb).start()
            remote(ycol, ycol, s(5), r(5), sib).start()

        on_early(g, go)

    def ag4(g):
        def go(t0, count, g):
            t, s, r = ag_parts(t0, count, g)
            low = w.at[t, 1 - y, c, :, 1 - x, pl.ds(0, HALF)]
            high = w.at[t, 1 - y, c, :, 1 - x, pl.ds(HALF, HALF)]
            remote(low, low, s(4), r(4), ynb).wait_recv()
            remote(high, high, s(3), r(3), xnb).wait_recv()
            diag = w.at[t, 1 - y, c, :, 1 - x]
            remote(diag, diag, s(5), r(5), sib).start()

        on_early(g, go)

    def ag5(g):
        def go(t0, count, g):
            t, s, r = ag_parts(t0, count, g)
            plane = w.at[t, :, 1 - c]
            remote(plane, plane, s(5), r(5), sib).wait_recv()

        on_group(g, go)

    def ag_sent(g):
        def go(t0, count, g):
            t, s, r = ag_parts(t0, count, g)
            one = w.at[t, y, c, z, x]
            column = w.at[t, y, c, :, x]
            half = w.at[t, y, c, :, x, pl.ds(0, HALF)]
            plane = w.at[t, :, c]
            for i, part in ((1, column), (2, column), (3, half), (4, half), (5, plane), (6, one)):
                remote(part, part, s(i), r(i), sib).wait_send()
            sent_sides(w.at[t, y, c, pl.ds(0, 3), x], one, s(0), r(0))

        on_early(g, go)

        def go_late(t0, count, g):
            t, s, r = ag_parts(t0, count, g)
            one = w.at[t, y, c, z, x]
            half = w.at[t, y, c, z, x, pl.ds(0, HALF)]
            plane = w.at[t, :, c]
            for i, part in ((1, one), (2, one), (3, half), (4, half), (5, plane)):
                remote(part, part, s(i), r(i), sib).wait_send()
            for i in range(3):
                b = t0 + i - late_tile(0)
                square = w.at[t0 + i, :, c, z]
                remote(square, square, late_send.at[1, b], late_recv.at[1, b], sib).wait_send()
                sent_sides(
                    w.at[t0 + i, :, c, pl.ds(0, 3)], square, late_send.at[0, b], late_recv.at[0, b]
                )

        on_late(g, go_late)

    def sent_sides(three, one, s, r):
        @pl.when(inner)
        def _():
            remote(three, three, s, r, sib).wait_send()

        @pl.when(jnp.logical_not(inner))
        def _():
            remote(one, one, s, r, sib).wait_send()

    def ag_front(t):
        ag1(t + AHEAD)
        ag1_relay(t + FIRST_AHEAD + 1)
        ag2(t + FIRST_AHEAD)
        late_step(t, late_line)
        ag3(t - AG_LAGS[0])

    def ag_back(t):
        late_step(t - 3, late_relay)
        ag4(t - AG_LAGS[1])
        late4(late_start + t - LATE_TICK)
        ag5(jnp.where(t - AG_LAGS[2] < late_start, t - AG_LAGS[2], -1) if not isinstance(t, int) else (t - AG_LAGS[2] if t - AG_LAGS[2] < late_start else -1))

    early_ff = ff_groups - LATE_GROUPS

    def ff_step(s):
        over = s - LATE_STEP
        if isinstance(s, int):
            if over < 0 or over >= 2 * LATE_GROUPS:
                before = s if over < 0 else s - LATE_GROUPS
                return before, False, before
            late = over % 2 == 0
            before = LATE_STEP + over // 2
            return (early_ff + over // 2 if late else before), late, before
        inside = jnp.logical_and(over >= 0, over < 2 * LATE_GROUPS)
        late = jnp.logical_and(inside, lax.rem(over + 2 * LATE_GROUPS, 2) == 0)
        before = jnp.where(over < 0, s, jnp.where(inside, LATE_STEP + over // 2, s - LATE_GROUPS))
        return jnp.where(late, early_ff + over // 2, before), late, before

    def rs_group(n):
        if isinstance(n, int):
            if n < 0 or n >= groups:
                return -1
            tail = n - ff_groups
            if tail < 0:
                return QKV_GROUPS + OUT_GROUPS + ff_step(n)[0]
            return QKV_GROUPS + tail if tail < OUT_GROUPS else tail - OUT_GROUPS
        tail = n - ff_groups
        g = jnp.where(
            tail < 0,
            QKV_GROUPS + OUT_GROUPS + ff_step(n)[0],
            jnp.where(tail < OUT_GROUPS, QKV_GROUPS + tail, tail - OUT_GROUPS),
        )
        return jnp.where(jnp.logical_or(n < 0, n >= groups), -1, g)

    def z_first(n):
        if isinstance(n, int):
            return n in Z_FIRST_SUMS
        return functools.reduce(jnp.logical_or, [n == m for m in Z_FIRST_SUMS])

    def on_sum(n, fn, kind=None):
        which = z_first(n)
        if isinstance(n, int):
            if kind is not None and which != kind:
                return
            slots = (n % SLOTS, n % Z_SLOTS, sum(n > m for m in Z_FIRST_SUMS), n % D_SLOTS)
            g = rs_group(n)
        else:
            bank = sum((n > m).astype(jnp.int32) for m in Z_FIRST_SUMS)
            slots = tuple(lax.rem(n + 10 * k, k) for k in (SLOTS, Z_SLOTS)) + (bank, lax.rem(n + 10 * D_SLOTS, D_SLOTS))
            g = rs_group(n)
            if kind is not None:
                g = jnp.where(which if kind else jnp.logical_not(which), g, -1)

        def go(t0, count, g):
            fn(t0, count, slots, (lambda i: rs_send.at[i, g]), (lambda i: rs_recv.at[i, g]))

        if kind:
            if isinstance(n, int):
                on_group(g, go)
            else:

                @pl.when(g >= 0)
                def _():
                    go(FF_START + 3 * (g - QKV_GROUPS - OUT_GROUPS), 3, g)

        else:
            on_group(g, go)

    def rs0(n):
        def go(t0, count, slots, s, r):
            slot = slots[0]
            remote(
                w.at[pl.ds(t0, count), :, 1 - c], rh.at[slot, pl.ds(0, count)], s(0), r(0), sib
            ).start()

        on_sum(n, go)

    def rs1(n):
        def go(t0, count, slots, s, r):
            slot = slots[0]
            t = pl.ds(t0, count)
            landed = rh.at[slot, pl.ds(0, count)]
            remote(w.at[t, :, 1 - c], landed, s(0), r(0), sib).wait_recv()

            def add(i, carry):
                for yy in range(ny):
                    w[t0 + i, yy, c] = w[t0 + i, yy, c] + rh[slot, i, yy]
                return carry

            lax.fori_loop(0, count, add, 0)

        on_sum(n, go)

        def go_early(t0, count, slots, s, r):
            for k, dev in ((0, xnb), (1, ynb)):
                remote(
                    w.at[pl.ds(t0, count), 1 - y, c, :, 1 - x, pl.ds(k * HALF, HALF)],
                    rd.at[slots[3], k, pl.ds(0, count)],
                    s(1 + k),
                    r(1 + k),
                    dev,
                ).start()

        on_sum(n, go_early, False)

    def rs1_line(n, i):
        def go_line(t0, count, slots, s, r):
            bank = slots[2]
            sems = line_sems(bank, i)
            line_sends(lambda at: w.at[t0 + i, :, c, at], lambda kind: rbz.at[bank, kind, i], *sems)

        on_sum(n, go_line, True)

    def line_sems(bank, i):
        return (lambda kind: bl_send.at[kind - 5, 3 * bank + i]), (lambda kind: bl_recv.at[kind - 5, 3 * bank + i])

    def line_sends(part, landed, s, r):
        to_sides(
            lambda: remote(part(dev_at(z + 1)), landed(0), s(5), r(5), dev_up).start(),
            lambda: remote(part(dev_at(z - 1)), landed(1), s(6), r(6), dev_down).start(),
        )

        @pl.when(jnp.logical_not(inner))
        def _():
            remote(part(across), landed(2), s(7), r(7), dev_across).start()
            remote(part(far_end), landed(3), s(8), r(8), dev_inward).start()

    def dev_at(at):
        return jnp.clip(at, 0, LINE - 1)

    def line_direct(part, landed, s, r):
        to_sides(
            lambda: remote(part(dev_at(z + 1)), landed(0), s(5), r(5), dev_up).start(),
            lambda: remote(part(dev_at(z - 1)), landed(1), s(6), r(6), dev_down).start(),
        )
        remote(part(across), landed(2), s(7), r(7), dev_across).start()

        @pl.when(jnp.logical_not(inner))
        def _():
            remote(part(far_end), landed(3), s(8), r(8), dev_far).start()

    def is_direct(n):
        return isinstance(n, int) and n >= groups - DIRECT

    def line_merge(part, landed, s, r, add):
        @pl.when(inner)
        def _():
            remote(part(across), landed(3), s(8), r(8), dev_edge).wait_recv()
            add()
            remote(part(across), landed(2), s(7), r(7), dev_across).start()

    def line_wait(part, landed, s, r, add):
        @pl.when(z > 0)
        def _():
            remote(part(z), landed(0), s(5), r(5), dev_down).wait_recv()
            add(0)

        @pl.when(z < LINE - 1)
        def _():
            remote(part(z), landed(1), s(6), r(6), dev_up).wait_recv()
            add(1)

        remote(part(z), landed(2), s(7), r(7), dev_across).wait_recv()
        add(2)

    def line_sent(part, s, r):
        pl.when(z < LINE - 1)(lambda: remote(part, part, s(5), r(5), sib).wait_send())
        pl.when(z > 0)(lambda: remote(part, part, s(6), r(6), sib).wait_send())
        remote(part, part, s(7), r(7), sib).wait_send()
        pl.when(jnp.logical_not(inner))(lambda: remote(part, part, s(8), r(8), sib).wait_send())

    def rs_merge(n):
        if is_direct(n):
            return

        def go(t0, count, slots, s, r):
            t = pl.ds(t0, count)

            def add():
                for i in range(count):
                    w[t0 + i, y, c, across, x] = w[t0 + i, y, c, across, x] + rf[slots[1], 3, i]

            line_merge(
                lambda at: w.at[t, y, c, at, x], lambda kind: rf.at[slots[1], kind, pl.ds(0, count)], s, r, add
            )

        on_sum(n, go, False)

    def rs_line_merge(n, i):
        def go(t0, count, slots, s, r):
            bank = slots[2]

            def add():
                for yy in range(ny):
                    w[t0 + i, yy, c, across] = w[t0 + i, yy, c, across] + rbz[bank, 3, i, yy]

            sems = line_sems(bank, i)
            line_merge(lambda at: w.at[t0 + i, :, c, at], lambda kind: rbz.at[bank, kind, i], *sems, add)

        on_sum(n, go, True)

    def rs2(n):
        def go(t0, count, slots, s, r):
            slot = slots[3]
            t = pl.ds(t0, count)
            for k, dev, yy, xx in ((0, xnb, 1 - y, x), (1, ynb, y, 1 - x)):
                landed = rd.at[slot, k, pl.ds(0, count)]
                rows_k = pl.ds(k * HALF, HALF)
                remote(w.at[t, 1 - y, c, :, 1 - x, rows_k], landed, s(1 + k), r(1 + k), dev).wait_recv()
                for i in range(count):
                    w[t0 + i, yy, c, :, xx, rows_k] = w[t0 + i, yy, c, :, xx, rows_k] + rd[slot, k, i]
            for k, dev, yy, xx in ((0, xnb, y, 1 - x), (1, ynb, 1 - y, x)):
                remote(
                    w.at[t, yy, c, :, xx], re.at[slot, k, pl.ds(0, count)], s(3 + k), r(3 + k), dev
                ).start()

        on_sum(n, go, False)

    def rs2_line(n):
        def go_line(t0, count, slots, s, r):
            t = pl.ds(t0, count)
            bank = slots[2]
            for i in range(count):

                def add(kind, i=i):
                    for yy in range(ny):
                        w[t0 + i, yy, c, z] = w[t0 + i, yy, c, z] + rbz[bank, kind, i, yy]

                line_wait(
                    lambda at, i=i: w.at[t0 + i, :, c, at],
                    lambda kind, i=i: rbz.at[bank, kind, i],
                    *line_sems(bank, i),
                    add,
                )
            for k, dev in ((0, xnb), (1, ynb)):
                remote(
                    w.at[t, 1 - y, c, z, 1 - x, pl.ds(k * HALF, HALF)],
                    rbd.at[slots[2], k],
                    s(1 + k),
                    r(1 + k),
                    dev,
                ).start()

        on_sum(n, go_line, True)

    def rs3(n):
        def go(t0, count, slots, s, r):
            slot = slots[3]
            t = pl.ds(t0, count)
            for k, dev in ((0, xnb), (1, ynb)):
                landed = re.at[slot, k, pl.ds(0, count)]
                remote(w.at[t, y, c, :, x], landed, s(3 + k), r(3 + k), dev).wait_recv()
            for i in range(count):
                total = (
                    w[t0 + i, y, c, z, x].astype(f32)
                    + re[slot, 0, i, z].astype(f32)
                    + re[slot, 1, i, z].astype(f32)
                )
                own[t0 + i] = total
                for zz in range(nz):
                    w[t0 + i, y, c, zz, x] = (
                        w[t0 + i, y, c, zz, x].astype(f32)
                        + re[slot, 0, i, zz].astype(f32)
                        + re[slot, 1, i, zz].astype(f32)
                    ).astype(bf16)
            (line_direct if is_direct(n) else line_sends)(
                lambda at: w.at[t, y, c, at, x], lambda kind: rf.at[slots[1], kind, pl.ds(0, count)], s, r
            )

        on_sum(n, go, False)

    def rs3_line(n):
        def go_line(t0, count, slots, s, r):
            t = pl.ds(t0, count)
            for k, dev, yy, xx in ((0, xnb, 1 - y, x), (1, ynb, y, 1 - x)):
                landed = rbd.at[slots[2], k]
                rows_k = pl.ds(k * HALF, HALF)
                remote(w.at[t, 1 - y, c, z, 1 - x, rows_k], landed, s(1 + k), r(1 + k), dev).wait_recv()
                for i in range(count):
                    w[t0 + i, yy, c, z, xx, rows_k] = w[t0 + i, yy, c, z, xx, rows_k] + rbd[slots[2], k, i]
            for k, dev, yy, xx in ((0, xnb, y, 1 - x), (1, ynb, 1 - y, x)):
                remote(w.at[t, yy, c, z, xx], rbe.at[slots[2], k], s(3 + k), r(3 + k), dev).start()

        on_sum(n, go_line, True)

    def rs4(n):
        def go(t0, count, slots, s, r):
            t = pl.ds(t0, count)

            def add(kind):
                for i in range(count):
                    own[t0 + i] += rf[slots[1], kind, i].astype(f32)

            line_wait(
                lambda at: w.at[t, y, c, at, x], lambda kind: rf.at[slots[1], kind, pl.ds(0, count)], s, r, add
            )
            if is_direct(n):

                @pl.when(jnp.logical_not(inner))
                def _():
                    landed = rf.at[slots[1], 3, pl.ds(0, count)]
                    remote(w.at[t, y, c, z, x], landed, s(8), r(8), dev_far).wait_recv()
                    add(3)

        on_sum(n, go, False)

    def rs4_line(n):
        def go_line(t0, count, slots, s, r):
            for k, dev in ((0, xnb), (1, ynb)):
                landed = rbe.at[slots[2], k]
                remote(landed, landed, s(3 + k), r(3 + k), dev).wait_recv()
            for i in range(count):
                own[t0 + i] = (
                    w[t0 + i, y, c, z, x].astype(f32)
                    + rbe[slots[2], 0, i].astype(f32)
                    + rbe[slots[2], 1, i].astype(f32)
                )

        on_sum(n, go_line, True)

    def rs_sent(n):
        def go(t0, count, slots, s, r):
            t = pl.ds(t0, count)
            plane = w.at[t, :, c]
            half = w.at[t, y, c, :, x, pl.ds(0, HALF)]
            column = w.at[t, y, c, :, x]
            for i, part in enumerate((plane, half, half, column, column)):
                remote(part, part, s(i), r(i), sib).wait_send()
            line_sent(w.at[t, y, c, z, x], s, r)

        on_sum(n, go, False)

        def go_line(t0, count, slots, s, r):
            t = pl.ds(t0, count)
            plane = w.at[t, :, c]
            half = w.at[t, y, c, z, x, pl.ds(0, HALF)]
            one = w.at[t, y, c, z, x]
            for i, part in enumerate((plane, half, half, one, one)):
                remote(part, part, s(i), r(i), sib).wait_send()
            for i in range(count):
                line_sent(w.at[t0 + i, :, c, z], *line_sems(slots[2], i))

        on_sum(n, go_line, True)

    def rs_front(n):
        rs0(n)
        rs1(n - LAGS[0])
        for i in range(3):
            rs1_line(n - LAGS[0] - i, i)
        rs2(n - LAGS[1])

    def rs_back(n):
        rs3(n - LAGS[2])
        for i in range(3):
            rs_line_merge(n - LAGS[0] - LINE_LAG - i, i)
        rs_merge(n - LAGS[3])
        rs4(n - LAGS[4])
        rs2_line(n - LAGS[0] - 2 * LINE_LAG - 2)
        rs3_line(n - LAGS[0] - 2 * LINE_LAG - 3)
        rs4_line(n - LAGS[0] - 2 * LINE_LAG - 4)

    def rs_tick(n):
        rs_front(n)
        rs_back(n)

    def cast_wait(copy):
        copy.wait_send()
        copy.wait_recv()

    def sm_start(i):
        if i == 0:
            part = smb.at[near, z]
            for k in range(1, nz):
                remote(part, part, sm_send.at[0], sm_recv.at[0], zdev(k)).start()
        else:
            part = smb.at[near]
            for step in cube:
                remote(part, part, sm_send.at[1], sm_recv.at[1], cube_dev(step)).start()

    def sm_wait(i):
        part = smb.at[near, pl.ds(0, nz - 1)] if i == 0 else smb.at[pl.ds(0, len(cube))]
        cast_wait(remote(part, part, sm_send.at[i], sm_recv.at[i], sib))

    smb[near, z] = jnp.zeros(smb.shape[2:], f32)
    smb[near, z, 0:1, 0:per] = small_ref[...].astype(bf16).astype(f32)
    load_wait(0)
    pl.semaphore_wait(barrier, len(cube) + nz - 1)
    ag1(0)
    sm_start(0)
    for g in range(1, AHEAD):
        load_wait(g)
        ag1(g)
    for g in range(late_start, groups):
        load_wait(g)
        late1(g)
    load_wait(AHEAD)

    lane = iota((tok_count, 128), 1)
    row = iota((tok_count, 128), 0)
    first_len = page_ref[:, 0:1]
    both_len = first_len + page_ref[:, 1:2]

    def pos_rows(k):
        line = pos_ref[k : k + 1, :].astype(f32)
        return jnp.broadcast_to(line, (128, tok_count)).T.astype(jnp.int32)

    pos_x, pos_y = pos_rows(0), pos_rows(1)
    hot_x = (pos_x == lane).astype(f32)
    hot_y = (pos_y == lane).astype(f32)
    page = jnp.where(row < first_len, 0, jnp.where(row < both_len, 1, 2))
    hx[...] = hot_x.astype(bf16)
    hxx[...] = (pos_x == lax.rem(lane, 64)).astype(f32).astype(bf16)
    hq2[...] = jnp.where(lane < 64, hot_y, (page == lane - 64).astype(f32)).astype(bf16)
    barred = jnp.where(jnp.logical_and(page == lane - 64, page < 2), 0.0, far_negative)
    k2[...] = jnp.where(lane < 64, hot_y, jnp.where(lane < 67, barred, 0.0)).astype(bf16)
    hxt[...] = hot_x.T[0:64].astype(bf16)
    hyt[...] = hot_y.T[0:64].astype(bf16)
    for g in range(FIRST_AHEAD + 1):
        ag1_relay(g)
        if g < FIRST_AHEAD:
            ag2(g)
    ag_front(0)
    ag_back(0)
    sm_wait(0)
    sm_start(1)
    for g in range(late_start, groups):
        late2(g)
    for g in range(AHEAD + 1, late_start):
        load_wait(g)
    cot_copy.wait()

    def mask_out(i, carry):
        at = pl.ds(pl.multiple_of(i * 128, 128), 128)
        valid = (iota((128, width), 0) + i * 128 < both_len).astype(f32)
        masked = valid * gout[at, :].astype(f32)
        gout[at, :] = masked.astype(bf16)
        goutt[:, at] = masked.T.astype(bf16)
        return carry

    lax.fori_loop(0, tok_count // 128, mask_out, 0)
    for g in range(late_start, groups):
        late3(g)
    ag_front(1)
    ag_back(1)
    sm_wait(1)

    devs = [(a, b, d, e) for a in range(ny) for b in range(2) for d in range(nz) for e in range(nx)]
    lane1 = iota((1, 128), 1)

    def flat_tile(n):
        tile = jnp.zeros((1, 128), f32)
        for d in range(128 * n // per, (128 * n + 127) // per + 1):
            shift = d * per - 128 * n
            a, b, at_z, at_x = devs[d]
            line = smb[(a * 2 + b) * nx + at_x, at_z, 0:1, :]
            line = pltpu.roll(line, shift % 128, 1)
            inside = jnp.logical_and(lane1 >= shift, lane1 < shift + per)
            tile = jnp.where(inside, line, tile)
        return tile

    for n in range(2 * width // 128):
        gains[n // (width // 128), :, pl.ds(128 * (n % (width // 128)), 128)] = flat_tile(n)
    first_table = 2 * width // 128

    def table(k):
        flat = jnp.concatenate([flat_tile(first_table + 4 * k + i) for i in range(4)], axis=1)
        keep = lax.rem(iota((HEADS, 512), 1), HEADS) == iota((HEADS, 512), 0)
        return jnp.where(keep, jnp.broadcast_to(flat, (HEADS, 512)), 0.0).astype(bf16)

    def hot(bucket_line, count):
        return (iota((512, count), 0) // HEADS == bucket_line).astype(f32).astype(bf16)

    limits = bucket_limits(tok_count)
    span = 2 * tok_count

    def rel_bucket(offset):
        distance = jnp.abs(offset)
        bucket = jnp.where(offset > 0, BUCKETS // 2, 0)
        for limit in limits:
            bucket = bucket + (distance >= limit).astype(jnp.int32)
        return bucket

    def layout_bucket(offset):
        return jnp.clip(offset, -(BUCKETS // 2), BUCKETS // 2 - 1) + BUCKETS // 2

    rel_values = dot(table(0), hot(rel_bucket(tok_count - iota((1, span), 1)), span))
    for h in range(HEADS):
        gv[h, 0:1, :] = rel_values[h : h + 1]
    turned = jnp.where(lane1 < 64, lane1, lane1 - 128)
    x_even = dot(table(1), hot(layout_bucket(lane1 - 64), 128))
    x_odd = dot(table(1), hot(layout_bucket(turned), 128))
    y_any = dot(table(2), hot(layout_bucket(turned), 128))
    sq_lane, sq_row = iota((128, 128), 1), iota((128, 128), 0)

    def slope(line):
        return pltpu.roll(jnp.broadcast_to(line, (128, line.shape[1])), 0, 1, stride=1, stride_axis=0)

    for p in range(HEADS // 2):
        a, b = 2 * p, 2 * p + 1
        both = jnp.where(sq_lane < 64, slope(x_odd[b : b + 1]), slope(x_even[a : a + 1]))
        kxs[p] = jnp.where(sq_row < 64, both, 0.0).astype(bf16)
        for h in (a, b):
            part = jnp.where(sq_lane < 64, slope(y_any[h : h + 1]), 0.0)
            km[h] = jnp.where(sq_row < 64, part, (sq_lane == sq_row).astype(f32)).astype(bf16)

    tok_copy.wait()

    def norm_one(i, carry):
        at = pl.ds(pl.multiple_of(i * 128, 128), 128)
        stream = tok[at, :].astype(f32)
        scale = lax.rsqrt(jnp.mean(stream * stream, axis=-1, keepdims=True) + norm_eps)
        low = (stream * scale * gains[0]).astype(bf16)
        n1[at, :] = low
        n1t[:, at] = low.astype(f32).T.astype(bf16)
        return carry

    lax.fori_loop(0, tok_count // 128, norm_one, 0)
    for t in range(2, AG_LAGS[2]):
        ag_front(t)
        ag_back(t)
    ag_front(AG_LAGS[2])

    def tile_of(t):
        return w[t].reshape(width, TILE)

    half_lane = iota((tok_count, 128), 1) < 64

    def pick(low, high):
        return jnp.where(half_lane, low.astype(f32), high.astype(f32)).astype(bf16)

    def augmented(p, e):
        shift = dot(hx[...], kxs[p])
        q_own, k_own = qp[p], kp[p]
        q_first = pick(q_own, shift) if e == 0 else pick(shift, q_own)
        k_first = pick(k_own, hxx[...]) if e == 0 else pick(hxx[...], k_own)
        q_second = dot(hq2[...], km[2 * p + e]).astype(bf16)
        return (
            jnp.concatenate([q_first, q_second], axis=1),
            jnp.concatenate([k_first, k2[...]], axis=1),
        )

    blocks = tok_count // 128
    half_rows = tok_count // 2

    def rel_bias(steep, part):
        return jnp.concatenate(
            [
                steep[:, tok_count - 128 * jb + half_rows * part : tok_count - 128 * jb + half_rows * (part + 1)]
                for jb in range(blocks)
            ],
            axis=0,
        )

    def forward_pair(p):
        v_turned = vp[p].astype(f32).T.astype(bf16)
        pieces = []
        for e in range(2):
            q_all, k_all = augmented(p, e)
            steep = slope(gv[2 * p + e, 0:1, :])
            parts = []
            for part in range(2):
                cols = slice(half_rows * part, half_rows * (part + 1))
                scores = dot_nt(k_all, q_all[cols]) + rel_bias(steep, part)
                top = jnp.max(scores, axis=0, keepdims=True)
                exponent = jnp.exp(scores - top)
                total = jnp.sum(exponent, axis=0, keepdims=True)
                weights = exponent.astype(bf16)
                lse[2 * p + e, 0:1, cols] = top + jnp.log(total)
                parts.append(dot(v_turned[64 * e : 64 * (e + 1)], weights) * (1.0 / total))
            pieces.append(jnp.concatenate(parts, axis=1))
        turned = jnp.concatenate(pieces, axis=0)
        at = pl.ds(pl.multiple_of(p * 128, 128), 128)
        ctxt[at, :] = turned.astype(bf16)
        ctx[:, at] = turned.T.astype(bf16)

    def project(j):
        for i, dest in enumerate((qp, kp, vp)):
            result = dot(n1[...], tile_of(3 * j + i)).astype(bf16)
            dest[2 * j] = result[:, 0:128]
            dest[2 * j + 1] = result[:, 128:256]

    def forward_heads(j, carry):
        ag_back(j + AG_LAGS[2])
        project(j)
        forward_pair(2 * j)
        ag_front(j + AG_LAGS[2] + 1)
        forward_pair(2 * j + 1)
        return carry

    lax.fori_loop(0, QKV_GROUPS, forward_heads, 0)
    tick = AG_LAGS[2] + QKV_GROUPS
    for i in range(OUT_GROUPS):
        ag_back(tick)
        tick += 1
        ag_front(tick)

    for e in range(4):
        cols = pl.ds(e * TILE, TILE)
        res[:, cols] = tok[:, cols].astype(f32) + dot(ctx[...], tile_of(OUT_START + e))

    def norm_two(i, carry):
        at = pl.ds(pl.multiple_of(i * 128, 128), 128)
        stream = res[at, :]
        scale = lax.rsqrt(jnp.mean(stream * stream, axis=-1, keepdims=True) + norm_eps)
        low = (stream * scale * gains[1]).astype(bf16)
        n2[at, :] = low
        n2t[:, at] = low.astype(f32).T.astype(bf16)
        mix[at, :] = stream
        gn[at, :] = jnp.zeros((128, width), f32)
        return carry

    lax.fori_loop(0, tok_count // 128, norm_two, 0)

    root = float(np.sqrt(2.0 / np.pi))

    def feed(step, carry):
        f, late, before = ff_step(step)

        @pl.when(late)
        def _():
            ag5(jnp.where(late, QKV_GROUPS + OUT_GROUPS + f, -1))

        @pl.when(jnp.logical_not(late))
        def _():
            ag_back(before + tick)

        t0 = FF_START + 3 * f
        gate_w, up_w, down_w = tile_of(t0), tile_of(t0 + 1), tile_of(t0 + 2)
        gate = dot(n2[...], gate_w)
        up = dot(n2[...], up_w)
        grad_hidden = dot(gout[...], down_w)
        square = gate * gate
        turn = jnp.tanh(root * gate * (1.0 + 0.044715 * square))
        half = 0.5 * (1.0 + turn)
        active = gate * half
        slope_of = half + 0.5 * gate * (1.0 - turn * turn) * (root * (1.0 + 3 * 0.044715 * square))
        hidden = (active * up).astype(bf16)

        @pl.when(jnp.logical_not(late))
        def _():
            ag_front(before + tick + 1)

        grad_gate = (grad_hidden * up * slope_of).astype(bf16)
        grad_up = (grad_hidden * active).astype(bf16)
        mix[...] += dot_nt(hidden, down_w)
        gn[...] += dot_nt(grad_gate, gate_w) + dot_nt(grad_up, up_w)
        ag_sent(f + QKV_GROUPS + OUT_GROUPS)
        shape = w.shape[1:]
        w[t0] = dot(n2t[...], grad_gate).astype(bf16).reshape(shape)
        w[t0 + 1] = dot(n2t[...], grad_up).astype(bf16).reshape(shape)
        w[t0 + 2] = dot(goutt[...], hidden).astype(bf16).reshape(shape)
        rs_tick(step - SUM_LAG)
        return carry

    lax.fori_loop(0, ff_groups, feed, 0)

    gsum[...] = jnp.zeros_like(gsum)
    grad_res, gctx = mix, gout

    def norm_two_back(i, carry):
        at = pl.ds(pl.multiple_of(i * 128, 128), 128)
        valid = (iota((128, width), 0) + i * 128 < both_len).astype(f32)
        ctx[at, :] = (valid * mix[at, :]).astype(bf16)
        stream = res[at, :]
        scale = lax.rsqrt(jnp.mean(stream * stream, axis=-1, keepdims=True) + norm_eps)
        got = gn[at, :]
        gsum[1] += jnp.sum((got * stream * scale).reshape(16, 8, width), axis=0)
        scaled = gains[1] * got
        inner = jnp.mean(scaled * stream, axis=-1, keepdims=True)
        total = gout[at, :].astype(f32) + scale * scaled - stream * (scale * scale * scale * inner)
        grad_res[at, :] = total
        n2[at, :] = total.astype(bf16)
        gn[at, :] = jnp.zeros((128, width), f32)
        return carry

    lax.fori_loop(0, tok_count // 128, norm_two_back, 0)
    out_copy = pltpu.make_async_copy(ctx, out_hbm, in_sem.at[0])
    out_copy.start()
    attended = n2
    shape = w.shape[1:]
    done = ff_groups - SUM_LAG
    rs_tick(done)
    done += 1
    for yy in range(ny):
        for cc in range(2):
            part = jnp.zeros((tok_count, TILE), f32)
            for e in range(4):
                block = w[OUT_START + e, yy, cc].reshape(TILE, TILE)
                part = part + dot_nt(attended[:, pl.ds(e * TILE, TILE)], block)
            gctx[:, pl.ds((yy * 2 + cc) * TILE, TILE)] = part.astype(bf16)
    for i in range(OUT_GROUPS):
        ag_sent(QKV_GROUPS + i)
        for e in (2 * i, 2 * i + 1):
            w[OUT_START + e] = (
                dot(ctxt[...], attended[:, pl.ds(e * TILE, TILE)]).astype(bf16).reshape(shape)
            )
        rs_front(done)
        if i < OUT_GROUPS - 1:
            rs_back(done)
        done += 1

    flip = (sq_row + sq_lane == 127).astype(f32).astype(bf16)
    flip_halves = jnp.where(
        (sq_row < 64) == (sq_lane < 64), (lax.rem(sq_row, 64) + lax.rem(sq_lane, 64) == 63).astype(f32), 0.0
    ).astype(bf16)

    def split_left(matrix, value):
        high = value.astype(bf16)
        rest = (value - high.astype(f32)).astype(bf16)
        return dot(matrix, high) + dot(matrix, rest)

    def backward_pair(p, local, between):
        at = pl.ds(pl.multiple_of(p * 128, 128), 128)
        k_turned = kp[p].astype(f32).T.astype(bf16)
        grad_rows = gctx[:, at]
        dv_parts, dk_parts, dq_parts, x_parts, y_parts = [], [], [], [], []
        for e in range(2):
            h = 2 * p + e
            q_all, k_all = augmented(p, e)
            steep = slope(gv[h, 0:1, :])
            zero = jnp.zeros((tok_count, 128), f32)
            one_head = pick(grad_rows, zero) if e == 0 else pick(zero, grad_rows)
            left = jnp.concatenate([k_turned[64 * e : 64 * (e + 1)], hxt[...], hyt[...]], axis=0)
            acc[...] = jnp.zeros_like(acc)
            dv_e = jnp.zeros((tok_count, 128), f32)
            dk_e = jnp.zeros((tok_count, 128), f32)
            turned = []
            for part in range(2):
                cols = slice(half_rows * part, half_rows * (part + 1))
                scores = dot_nt(k_all, q_all[cols]) + rel_bias(steep, part)
                probs = jnp.exp(scores - lse[h, 0:1, cols])
                grad_probs = dot_nt(vp[p], one_head[cols])
                inner = jnp.sum(grad_probs * probs, axis=0, keepdims=True)
                grad_scores = (probs * (grad_probs - inner)).astype(bf16)
                dv_e = dv_e + dot(probs.astype(bf16), grad_rows[cols])
                dk_e = dk_e + dot(grad_scores, qp[p, cols])
                turned.append(dot(left, grad_scores))
                for jb in range(blocks):
                    start = tok_count - 128 * jb + half_rows * part
                    acc[:, start : start + half_rows] += grad_scores[128 * jb : 128 * (jb + 1)].astype(f32)
            all_turned = jnp.concatenate(turned, axis=1)
            dq_parts.append(all_turned[0:64])
            x_parts.append(all_turned[64:128])
            y_parts.append(all_turned[128:192])
            dv_parts.append(dv_e)
            dk_parts.append(dk_e)
            rolled = pltpu.roll(split_left(flip, acc[...]), 0, 1, stride=1, stride_axis=0)
            gv[h, 0:1, :] = jnp.sum(rolled, axis=0, keepdims=True)
            if e == 0:
                between()
        low = half_lane
        cols = pl.ds(local * 128, 128)
        dq[:, cols] = jnp.concatenate(dq_parts, axis=0).T.astype(bf16)
        dk[:, cols] = jnp.where(low, dk_parts[0], dk_parts[1]).astype(bf16)
        dv[:, cols] = jnp.where(low, dv_parts[0], dv_parts[1]).astype(bf16)
        for parts, hots, dest in ((x_parts, hx, ggx), (y_parts, hq2, ggy)):
            table_grad = dot(jnp.concatenate(parts, axis=0).astype(bf16), hots[...])
            table_grad = jnp.where(sq_lane < 64, table_grad, 0.0)
            rolled = pltpu.roll(split_left(flip_halves, table_grad), 0, 1, stride=1, stride_axis=0)
            dest[2 * p, 0:1, :] = jnp.sum(rolled[0:64], axis=0, keepdims=True)
            dest[2 * p + 1, 0:1, :] = jnp.sum(rolled[64:128], axis=0, keepdims=True)

    first_head = ff_groups + OUT_GROUPS

    def end_tick(j):
        return jnp.minimum(done + 2 * j + 1, first_head + j)

    def backward_heads(j, carry):
        middle = jnp.where(j <= first_head - 1 - done, done + 2 * j, -SKIP)
        backward_pair(2 * j, 0, lambda: rs_back(end_tick(j - 1)))
        rs_front(middle)
        backward_pair(2 * j + 1, 1, lambda: rs_back(middle))
        gn[...] += (
            dot_nt(dq[...], tile_of(3 * j))
            + dot_nt(dk[...], tile_of(3 * j + 1))
            + dot_nt(dv[...], tile_of(3 * j + 2))
        )
        ag_sent(j)
        for i, part in enumerate((dq, dk, dv)):
            w[3 * j + i] = dot(n1t[...], part[...]).astype(bf16).reshape(shape)
        rs_front(end_tick(j))
        return carry

    lax.fori_loop(0, QKV_GROUPS, backward_heads, 0)
    done = min(done + 2 * QKV_GROUPS, groups)
    rs_back(done - 1)
    rs_tick(done)

    def norm_one_back(i, carry):
        at = pl.ds(pl.multiple_of(i * 128, 128), 128)
        stream = tok[at, :].astype(f32)
        scale = lax.rsqrt(jnp.mean(stream * stream, axis=-1, keepdims=True) + norm_eps)
        got = gn[at, :]
        gsum[0] += jnp.sum((got * stream * scale).reshape(16, 8, width), axis=0)
        scaled = gains[0] * got
        inner = jnp.mean(scaled * stream, axis=-1, keepdims=True)
        grad_res[at, :] = (
            grad_res[at, :] + scale * scaled - stream * (scale * scale * scale * inner)
        )
        return carry

    lax.fori_loop(0, tok_count // 128, norm_one_back, 0)
    gtok_copy = pltpu.make_async_copy(grad_res, gtok_hbm, in_sem.at[1])
    gtok_copy.start()
    rs_tick(done + 1)

    def unhot(bucket_col, count):
        return (bucket_col == iota((count, 128), 1)).astype(f32).astype(bf16)

    def head_rows(ref, start=0):
        return jnp.concatenate([ref[h, 0:1, :] for h in range(start, HEADS, 1)], axis=0)

    col_span = iota((span, 128), 0)
    rel_source = lax.rem(col_span - 127 + span, span)
    rel_sum = split_dot(head_rows(gv), unhot(rel_bucket(tok_count - rel_source), span))
    col_square = iota((128, 128), 0)
    low_source = lax.rem(col_square - 63 + 128, 128)
    high_source = lax.rem(col_square - 127 + 128, 128)

    def signed(source):
        return jnp.where(source < 64, source, source - 128)

    low_hot = unhot(layout_bucket(-signed(low_source)), 128)
    high_hot = unhot(layout_bucket(-signed(high_source)), 128)
    odd = lax.rem(iota((HEADS, 128), 0), 2) == 1

    def layout_sum(ref):
        lines = head_rows(ref)
        return jnp.where(odd, split_dot(lines, high_hot), split_dot(lines, low_hot))

    spread = (iota((128, 512), 0) == iota((128, 512), 1) // HEADS).astype(f32).astype(bf16)
    keep = lax.rem(iota((HEADS, 512), 1), HEADS) == iota((HEADS, 512), 0)

    def flat_table(value):
        high = value.astype(bf16)
        rest = (value - high.astype(f32)).astype(bf16)
        rest_two = (value - high.astype(f32) - rest.astype(f32)).astype(bf16)
        wide = dot(high, spread) + dot(rest, spread) + dot(rest_two, spread)
        return jnp.sum(jnp.where(keep, wide, 0.0), axis=0, keepdims=True)

    tiles = []
    for k in range(2):
        line = jnp.sum(gsum[k], axis=0, keepdims=True)
        tiles += [line[:, 128 * n : 128 * (n + 1)] for n in range(width // 128)]
    for value in (rel_sum, layout_sum(ggx), layout_sum(ggy)):
        line = flat_table(value)
        tiles += [line[:, 128 * n : 128 * (n + 1)] for n in range(4)]
    for d in range(len(devs)):
        line = jnp.zeros((1, 128), f32)
        for n in range(d * per // 128, (d * per + per - 1) // 128 + 1):
            shift = 128 * n - d * per
            moved = pltpu.roll(tiles[n], shift % 128, 1)
            inside = jnp.logical_and(lane1 >= shift, lane1 < min(shift + 128, per))
            line = jnp.where(inside, moved, line)
        sgr[near, d : d + 1, :] = line

    def near_start(k, landed):
        part = landed.at[near]
        for step in cube:
            remote(part, part, sm_send.at[k], sm_recv.at[k], cube_dev(step)).start()

    def near_sum(k, landed, lined):
        part = landed.at[pl.ds(0, len(cube))]
        cast_wait(remote(part, part, sm_send.at[k], sm_recv.at[k], sib))
        total = landed[0]
        for i in range(1, len(cube) + 1):
            total = total + landed[i]
        lined[z] = total
        for i in range(1, nz):
            remote(lined.at[z], lined.at[z], sm_send.at[k + 1], sm_recv.at[k + 1], zdev(i)).start()

    def line_sum(k, lined):
        part = lined.at[pl.ds(0, nz - 1)]
        cast_wait(remote(part, part, sm_send.at[k + 1], sm_recv.at[k + 1], sib))
        total = lined[0]
        for i in range(1, nz):
            total = total + lined[i]
        return total

    near_start(2, sgr)
    rs_tick(done + 2)
    near_sum(2, sgr, sgz)
    for n in range(done + 3, groups + LAGS[4] - 1):
        rs_tick(n)
    small_total = line_sum(2, sgz)
    me = ((y * 2 + c) * nz + z) * nx + x
    mine = iota(small_total.shape, 0) == me
    osmall_ref[...] = jnp.sum(jnp.where(mine, small_total, 0.0), axis=0, keepdims=True)

    last = range(3 * (QKV_GROUPS - 1), 3 * QKV_GROUPS)

    def add_squares(squares, tiles):
        for t in tiles:
            value = own[t]
            squares = squares + jnp.sum((value * value).reshape(rows // 8, 8, TILE), axis=0)
        return squares

    squares = add_squares(jnp.zeros((8, TILE), f32), [t for t in range(own.shape[0]) if t not in last])
    rs_tick(groups + LAGS[4] - 1)
    own_copy = pltpu.make_async_copy(own, own_hbm, in_sem.at[2])
    own_copy.start()
    squares = add_squares(squares, last)
    nbr[near] = squares[:, 0:128] + squares[:, 128:256]
    near_start(4, nbr)
    out_copy.wait()
    gtok_copy.wait()
    for n in range(groups):
        rs_sent(n)
    near_sum(4, nbr, nbz)
    total = jnp.sum(line_sum(4, nbz)) + jnp.sum(small_total * small_total)
    norm_ref[...] = jnp.full((8, 128), 1.0, f32) * total
    own_copy.wait()


def update_kernel(
    sizes,
    total_ref,
    small_grad,
    small_master,
    small_first,
    small_second,
    own_hbm,
    block_hbm,
    gtok_hbm,
    attn_hbm,
    attn_first_hbm,
    attn_second_hbm,
    ffin_hbm,
    ffin_first_hbm,
    ffin_second_hbm,
    down_hbm,
    down_first_hbm,
    down_second_hbm,
    norm_out,
    small_master_out,
    small_first_out,
    small_second_out,
    block_out,
    gtok_out,
    attn_out,
    attn_first_out,
    attn_second_out,
    query_second_out,
    ffin_out,
    ffin_first_out,
    ffin_second_out,
    down_out,
    down_first_out,
    down_second_out,
    own,
    attn,
    ffin,
    down,
    block,
    gtok,
    in_sem,
    out_sem,
    pass_sem,
):
    (ff_groups,) = sizes
    passing = [
        pltpu.make_async_copy(block_hbm, block, pass_sem.at[0]),
        pltpu.make_async_copy(gtok_hbm, gtok, pass_sem.at[1]),
    ]
    passed = [
        pltpu.make_async_copy(block, block_out, pass_sem.at[2]),
        pltpu.make_async_copy(gtok, gtok_out, pass_sem.at[3]),
    ]
    first_tiles, other_tiles = pl.ds(0, FF_START), pl.ds(FF_START, 3 * ff_groups)
    loads = [
        [pltpu.make_async_copy(own_hbm.at[first_tiles], own.at[first_tiles], in_sem.at[0])],
        [pltpu.make_async_copy(own_hbm.at[other_tiles], own.at[other_tiles], in_sem.at[1])],
        [],
    ]
    sources = (
        (attn_hbm, attn_first_hbm, attn_second_hbm),
        (ffin_hbm, ffin_first_hbm, ffin_second_hbm),
        (down_hbm, down_first_hbm, down_second_hbm),
    )
    state = (attn, ffin, down)
    for i in range(3):
        loads[i] += [
            pltpu.make_async_copy(src, state[i].at[k], in_sem.at[2 + 3 * i + k])
            for k, src in enumerate(sources[i])
        ]
    for part in (*loads, passing):
        for copy in part:
            copy.start()
    norm = jnp.sqrt(total_ref[0:1, 0:1])
    norm_out[...] = norm
    clip = clip_max / jnp.maximum(norm, clip_max)
    per = small_master.shape[1]
    results = adamw_update(
        small_master[...], small_first[...], small_second[...], small_grad[:, 0:per] * clip, small_rate, 0.0
    )
    for ref, value in zip((small_master_out, small_first_out, small_second_out), results):
        ref[...] = value

    def update(ref, at, tile):
        results = adamw_update(
            ref[(0,) + at], ref[(1,) + at], ref[(2,) + at], own[tile] * clip, matrix_rate, decay_rate
        )
        for k in range(3):
            ref[(k,) + at] = results[k]

    every = slice(None)
    stores = []

    def store(i, pairs):
        for src, dst in pairs:
            copy = pltpu.make_async_copy(src, dst, out_sem.at[len(stores)])
            copy.start()
            stores.append(copy)

    for copy in loads[0]:
        copy.wait()
    for j in range(QKV_GROUPS):
        cols = pl.ds(j * TILE, TILE)
        for i in range(3):
            update(attn, (i, every, cols), 3 * j + i)
        update(attn, (3, every, cols), OUT_START + j)
    store(
        0,
        [
            (attn.at[0], attn_out),
            (attn.at[1], attn_first_out),
            (attn.at[2, pl.ds(1, 3)], attn_second_out),
            (attn.at[2, 0], query_second_out),
        ],
    )
    for copy in loads[1]:
        copy.wait()

    def update_in(f, carry):
        cols = pl.ds(pl.multiple_of(f * TILE, TILE), TILE)
        for i in range(2):
            update(ffin, (i, every, cols), FF_START + 3 * f + i)
        return carry

    lax.fori_loop(0, ff_groups, update_in, 0)
    store(1, [(ffin.at[k], ref) for k, ref in enumerate((ffin_out, ffin_first_out, ffin_second_out))])
    for copy in loads[2]:
        copy.wait()

    def update_down(f, carry):
        cols = pl.ds(pl.multiple_of(f * TILE, TILE), TILE)
        update(down, (every, cols), FF_START + 3 * f + 2)
        return carry

    lax.fori_loop(0, ff_groups, update_down, 0)
    store(2, [(down.at[k], ref) for k, ref in enumerate((down_out, down_first_out, down_second_out))])
    for arrived, copy in zip(passing, passed):
        arrived.wait()
        copy.start()
    for copy in stores + passed:
        copy.wait()


def fused_on_device(
    tokens,
    cotangent,
    page_lengths,
    layout_pos,
    attn_master,
    attn_first,
    attn_second,
    ffin_master,
    ffin_first,
    ffin_second,
    down_master,
    down_first,
    down_second,
    small_master,
    small_first,
    small_second,
    *,
    ny,
    nz,
    nx,
):
    f32, bf16 = jnp.float32, jnp.bfloat16
    tok_count, width = tokens.shape
    rows, ff = down_master.shape
    per = small_master.shape[0]
    ff_groups = ff // TILE
    tiles = FF_START + 3 * ff_groups
    groups = QKV_GROUPS + OUT_GROUPS + ff_groups
    pairs = HEADS // 2
    vmem, dma = pltpu.VMEM, pltpu.SemaphoreType.DMA
    square = (tok_count, width)
    banks = len(Z_FIRST_SUMS)
    scratch = [
        vmem((tiles, ny, 2, nz, nx, rows, TILE), bf16),
        vmem((SLOTS, 3, ny, nz, nx, rows, TILE), bf16),
        vmem((D_SLOTS, 2, 3, nz, HALF, TILE), bf16),
        vmem((D_SLOTS, 2, 3, nz, rows, TILE), bf16),
        vmem((Z_SLOTS, 4, 3, rows, TILE), bf16),
        vmem((banks, 4, 3, ny, nx, rows, TILE), bf16),
        vmem((banks, 2, 3, HALF, TILE), bf16),
        vmem((banks, 2, 3, rows, TILE), bf16),
        vmem((tiles, rows, TILE), f32),
        vmem(square, f32),
        vmem((ny * 2 * nx, nz, 8, 128), f32),
        vmem((ny * 2 * nx, ny * 2 * nz * nx, 128), f32),
        vmem((nz, ny * 2 * nz * nx, 128), f32),
        vmem((ny * 2 * nx, 8, 128), f32),
        vmem((nz, 8, 128), f32),
        vmem(square, bf16),
        vmem(square, bf16),
        vmem((width, tok_count), bf16),
        vmem((pairs, tok_count, 128), bf16),
        vmem((pairs, tok_count, 128), bf16),
        vmem((pairs, tok_count, 128), bf16),
        vmem(square, bf16),
        vmem((width, tok_count), bf16),
        vmem(square, f32),
        vmem(square, bf16),
        vmem((width, tok_count), bf16),
        vmem(square, bf16),
        vmem((width, tok_count), bf16),
        vmem(square, f32),
        vmem((pairs, 128, 128), bf16),
        vmem((HEADS, 128, 128), bf16),
        vmem((HEADS, 8, 2 * tok_count), f32),
        vmem((HEADS, 8, tok_count), f32),
        vmem((HEADS, 8, 128), f32),
        vmem((HEADS, 8, 128), f32),
        vmem((128, 2 * tok_count), f32),
        vmem((tok_count, 128), bf16),
        vmem((tok_count, 128), bf16),
        vmem((tok_count, 128), bf16),
        vmem((tok_count, 128), bf16),
        vmem((64, tok_count), bf16),
        vmem((64, tok_count), bf16),
        vmem((tok_count, TILE), bf16),
        vmem((tok_count, TILE), bf16),
        vmem((tok_count, TILE), bf16),
        vmem((2, 1, width), f32),
        vmem((2, 8, width), f32),
        dma((groups,)),
        dma((3,)),
        dma((7, groups)),
        dma((7, groups)),
        dma((2, 3 * LATE_GROUPS)),
        dma((2, 3 * LATE_GROUPS)),
        dma((4, 3 * banks)),
        dma((4, 3 * banks)),
        dma((9, groups)),
        dma((9, groups)),
        dma((6,)),
        dma((6,)),
    ]
    in_vmem = pl.BlockSpec(memory_space=pltpu.VMEM)
    in_hbm = pl.BlockSpec(memory_space=pl.ANY)
    weights = attn_master.size + ffin_master.size + down_master.size
    block_out, grad_tokens, owned, owned_small, squares = pl.pallas_call(
        functools.partial(layer_kernel, (ny, nz, nx, per, ff_groups)),
        out_shape=[
            jax.ShapeDtypeStruct(square, bf16),
            jax.ShapeDtypeStruct(square, f32),
            jax.ShapeDtypeStruct((tiles, rows, TILE), f32),
            jax.ShapeDtypeStruct((1, 128), f32),
            jax.ShapeDtypeStruct((8, 128), f32),
        ],
        in_specs=[in_vmem] * 3 + [in_hbm] * 5,
        out_specs=[in_hbm] * 3 + [in_vmem] * 2,
        scratch_shapes=scratch,
        compiler_params=pltpu.CompilerParams(
            collective_id=0, has_side_effects=True, vmem_limit_bytes=VMEM_BYTES
        ),
        cost_estimate=pl.CostEstimate(
            flops=6 * tok_count * weights * ny * 2 * nz * nx,
            bytes_accessed=24 * weights,
            transcendentals=3 * tok_count * tok_count * HEADS,
        ),
    )(
        page_lengths.T,
        layout_pos,
        small_master.reshape(1, per),
        tokens,
        cotangent,
        attn_master,
        ffin_master,
        down_master,
    )
    like = [
        jax.ShapeDtypeStruct((1, 1), f32),
        *[jax.ShapeDtypeStruct((1, per), f32)] * 3,
        jax.ShapeDtypeStruct(square, bf16),
        jax.ShapeDtypeStruct(square, f32),
        jax.ShapeDtypeStruct(attn_master.shape, f32),
        jax.ShapeDtypeStruct(attn_master.shape, f32),
        jax.ShapeDtypeStruct((3,) + attn_master.shape[1:], f32),
        jax.ShapeDtypeStruct(attn_master.shape[1:], f32),
        *[jax.ShapeDtypeStruct(ffin_master.shape, f32)] * 3,
        *[jax.ShapeDtypeStruct(down_master.shape, f32)] * 3,
    ]
    results = pl.pallas_call(
        functools.partial(update_kernel, (ff_groups,)),
        out_shape=like,
        in_specs=[in_vmem] * 5 + [in_hbm] * 12,
        out_specs=[in_vmem] * 4 + [in_hbm] * 12,
        scratch_shapes=[
            vmem((tiles, rows, TILE), f32),
            vmem((3,) + attn_master.shape, f32),
            vmem((3,) + ffin_master.shape, f32),
            vmem((3,) + down_master.shape, f32),
            vmem(square, bf16),
            vmem(square, f32),
            dma((11,)),
            dma((10,)),
            dma((4,)),
        ],
        compiler_params=pltpu.CompilerParams(vmem_limit_bytes=VMEM_BYTES),
        cost_estimate=pl.CostEstimate(
            flops=20 * weights, bytes_accessed=28 * weights, transcendentals=2 * weights
        ),
    )(
        squares,
        owned_small,
        small_master.reshape(1, per),
        small_first.reshape(1, per),
        small_second.reshape(1, per),
        owned,
        block_out,
        grad_tokens,
        attn_master,
        attn_first,
        attn_second,
        ffin_master,
        ffin_first,
        ffin_second,
        down_master,
        down_first,
        down_second,
    )
    norm, small_new, small_one, small_two = results[:4]
    return (
        results[4],
        results[5],
        norm.reshape(()),
        *results[6:],
        small_new.reshape(per),
        small_one.reshape(per),
        small_two.reshape(per),
    )


def choose(mesh, width):
    n_dp, n_fsdp = mesh.shape["dp"], mesh.shape["fsdp"]
    rows = width // (n_dp * n_fsdp)
    if n_dp == 4 and n_fsdp == 2 * LINE and rows % (2 * HALF) == 0:
        return functools.partial(fused_on_device, ny=n_dp // 2, nz=n_fsdp // 2, nx=2)
    return on_device


def sharded(mesh, program):
    return jax.shard_map(
        program,
        mesh=mesh,
        in_specs=(
            P(("dp", "fsdp"), None),
            P(("dp", "fsdp"), None),
            P(None, ("dp", "fsdp")),
            P(None, ("dp", "fsdp")),
            P(None, ("dp", "fsdp"), None),
            P(None, ("dp", "fsdp"), None),
            P(None, ("dp", "fsdp"), None),
            P(None, ("dp", "fsdp"), None),
            P(None, ("dp", "fsdp"), None),
            P(None, ("dp", "fsdp"), None),
            P(("dp", "fsdp"), None),
            P(("dp", "fsdp"), None),
            P(("dp", "fsdp"), None),
            P(("dp", "fsdp")),
            P(("dp", "fsdp")),
            P(("dp", "fsdp")),
        ),
        out_specs=(
            P(("dp", "fsdp"), None),
            P(("dp", "fsdp"), None),
            P(),
            P(None, ("dp", "fsdp"), None),
            P(None, ("dp", "fsdp"), None),
            P(None, ("dp", "fsdp"), None),
            P(("dp", "fsdp"), None),
            P(None, ("dp", "fsdp"), None),
            P(None, ("dp", "fsdp"), None),
            P(None, ("dp", "fsdp"), None),
            P(("dp", "fsdp"), None),
            P(("dp", "fsdp"), None),
            P(("dp", "fsdp"), None),
            P(("dp", "fsdp")),
            P(("dp", "fsdp")),
            P(("dp", "fsdp")),
        ),
        check_vma=False,
    )


def solution(mesh):
    def step(*args):
        return sharded(mesh, choose(mesh, args[0].shape[1]))(*args)

    return step
```
